256 devices in a mesh: tile: 64 (over x, z, core), lev: 4 (over y).
Axes of the slice: x: 4, y: 4, z: 8, core: 2. Of those that a mesh axis runs over, the one named last changes fastest.
Arguments:
- features: bfloat16 [8, 64, 12, 90, 192], P('lev', 'tile'), may hold values from -6 to 6
- attn_gain: float32 [192], replicated, may hold values from 0.5 to 1.5
- w_qkv: bfloat16 [192, 576], replicated, may hold values from -0.4375 to 0.4375
- w_proj: bfloat16 [192, 192], replicated, may hold values from -0.4375 to 0.4375
- window_bias: float32 [6, 144, 144], replicated, may hold values from -6 to 350, as said below
- patterns: int32 [8, 144], replicated, may hold values from 0 to 3
- window_pattern: int32 [4, 960], P(None, 'tile'), may hold values from 0 to 7
- mlp_gain: float32 [192], replicated, may hold values from 0.5 to 1.5
- w_expand: bfloat16 [192, 768], replicated, may hold values from -0.4375 to 0.4375
- w_reduce: bfloat16 [768, 192], replicated, may hold values from -0.21875 to 0.21875
- temp_head: bfloat16 [192], replicated, may hold values from -0.4375 to 0.4375
- temp_base: float32 [8], P('lev'), may hold values from 0.5 to 1.5
- thickness: float32 [8], P('lev'), may hold values from 0.2 to 1
- level_weight: float32 [8], P('lev'), may hold values from 0.5 to 2
- surface: float32 [64, 12, 90], P('tile'), may hold values from -6 to 6
- target: float32 [8, 64, 12, 90], P('lev', 'tile'), may hold values from -12 to 12
Outputs:
- height: float32 [8, 64, 12, 90], P('lev', 'tile')
- grad_features: bfloat16 [8, 64, 12, 90, 192], P('lev', 'tile')
The draws below stay inside these ranges and needn't reach their ends.
Inputs may be any that keep to these rules, and one draw needn't show every extreme that they name: `window_bias`: the bias that a head adds to the score of a query and key position of a window.
All inputs are finite; a program needn't handle non-finite values.
Results may differ from the reference program's by a relative error of at most 0.023.
Values may be sent and summed in bfloat16 or wider, within the bound.
No kernel may reach another device: no remote copies, remote signals or barrier semaphores. Data moves between devices by JAX's collectives and lax.ppermute only.
A program may use at most 64 MiB of HBM per device.

```python
import math
import jax
import jax.numpy as jnp
from jax import lax

C = 192
HEADS = 6
FF = 768
LAT_DEV = 12
LON_BLOCKS = 4
LON_DEV = 90
WIN = 144
GROUP = 3
NPAT = 8
TILES = 64
BANDS = 16
LEVELS = 8


def draw_window_bias(key, part):
    key = jax.random.fold_in(key, 7)
    table = jnp.clip(jax.random.normal(key, (HEADS, WIN, WIN), jnp.float32), -6.0, 6.0)
    return table


def place_ends(values, own_key, low, high):
    shape = values.shape
    spot = [jax.random.randint(jax.random.fold_in(own_key, axis), (), 0, shape[axis]) for axis in range(len(shape))]
    values = values.at[tuple(spot)].set(low)
    longest = shape.index(max(shape))
    spot[longest] = (spot[longest] + 1) % shape[longest]
    return values.at[tuple(spot)].set(high)


def block_scale(key, shape, pieces, low, top_value):
    loudness = 1.0
    for axis_at, blocks in pieces:
        heights = jax.random.uniform(jax.random.fold_in(jax.random.fold_in(key, 6), axis_at), (blocks,), jnp.float32, low / len(pieces), top_value / len(pieces))
        loudness = loudness * jnp.repeat(jnp.exp(heights), shape[axis_at] // blocks).reshape((-1,) + (1,) * (len(shape) - 1 - axis_at))
    return loudness


def normal_values(stream_key, shape, deviation, most, cuts=(), kind=jnp.bfloat16):
    array = jax.random.normal(stream_key, shape, jnp.float32) * deviation
    if len(cuts) > 0:
        array = block_scale(stream_key, shape, cuts, -0.22, 0.18) * array
    return jnp.clip(array, min=-most, max=most).astype(kind)


def setup_inputs(seed: int = 0) -> dict:
    key_list = jax.random.split(jax.random.key(seed), 17)
    features = normal_values(key_list[0], (LEVELS, TILES, LAT_DEV, LON_DEV, C), 1.0, 6.0, ((0, 4), (1, 64)))
    attn_gain = jnp.clip(1.0 + 0.1 * jax.random.normal(key_list[1], (C,), jnp.float32), 0.5, 1.5)
    w_qkv = normal_values(key_list[2], (C, 3 * C), C ** -0.5, 0.4375)
    w_proj = normal_values(key_list[3], (C, C), C ** -0.5, 0.4375)
    window_bias = draw_window_bias(jax.random.fold_in(key_list[16], 71), 0)
    patterns = place_ends(jax.random.randint(key_list[5], (NPAT, WIN), 0, 4), jax.random.fold_in(key_list[5], 1), 0, 3).astype(jnp.int32)
    window_pattern = place_ends(jax.random.randint(key_list[6], (LEVELS // 2, TILES * (LON_DEV // 6)), 0, NPAT), jax.random.fold_in(key_list[6], 1), 0, NPAT - 1).astype(jnp.int32)
    mlp_gain = jnp.clip(1.0 + 0.1 * jax.random.normal(key_list[7], (C,), jnp.float32), 0.5, 1.5)
    w_expand = normal_values(key_list[8], (C, FF), C ** -0.5, 0.4375)
    w_reduce = normal_values(key_list[9], (FF, C), FF ** -0.5, 0.21875)
    temp_head = normal_values(key_list[10], (C,), C ** -0.5, 0.4375)
    temp_base = jnp.clip(0.5 + 1.0 * jax.random.uniform(key_list[11], (LEVELS,), jnp.float32) ** block_scale(key_list[11], (LEVELS,), ((0, 4),), -0.2, 0.2), 0.5, 1.5)
    thickness = jnp.clip(jnp.exp(math.log(1.0) - 1.609438 * jax.random.uniform(key_list[12], (LEVELS,), jnp.float32) ** block_scale(key_list[12], (LEVELS,), ((0, 4),), -0.2, 0.2)), 0.2, 1.0)
    level_weight = jnp.clip(jnp.exp(math.log(2.0) - 1.3862944 * jax.random.uniform(key_list[13], (LEVELS,), jnp.float32) ** block_scale(key_list[13], (LEVELS,), ((0, 4),), -0.2, 0.2)), 0.5, 2.0)
    surface = normal_values(key_list[14], (TILES, LAT_DEV, LON_DEV), 1.0, 6.0, ((0, 64),), jnp.float32)
    target = normal_values(key_list[15], (LEVELS, TILES, LAT_DEV, LON_DEV), 2.0, 12.0, ((0, 4), (1, 64)), jnp.float32)
    return {"features": features, "attn_gain": attn_gain, "w_qkv": w_qkv, "w_proj": w_proj, "window_bias": window_bias, "patterns": patterns, "window_pattern": window_pattern, "mlp_gain": mlp_gain, "w_expand": w_expand, "w_reduce": w_reduce, "temp_head": temp_head, "temp_base": temp_base, "thickness": thickness, "level_weight": level_weight, "surface": surface, "target": target}


epsilon = 1e-05

def product(form, left, right):
    return jnp.einsum(form, left.astype(jnp.float32), right.astype(jnp.float32))

def layer_norm(tokens, scale_gain):
    values = tokens.astype(jnp.float32)
    center = lax.optimization_barrier(jnp.mean(values, axis=-1, keepdims=True))
    spread = lax.optimization_barrier(jnp.mean(jnp.square(values - center), axis=-1, keepdims=True))
    return ((values - center) * lax.rsqrt(spread + epsilon) * scale_gain).astype(jnp.bfloat16)

def window_block(tokens, labels, weights):
    attn_gain, w_qkv, w_proj, window_bias, mlp_gain, w_expand, w_reduce = weights
    groups, length, channels = tokens.shape
    head_count = window_bias.shape[0]
    head_size = channels // head_count
    token_rows = tokens.reshape(groups * length, channels)
    normed = layer_norm(token_rows, attn_gain)
    projected = jnp.dot(normed, w_qkv, preferred_element_type=jnp.float32)
    queries = (projected[:, :channels] * (1.0 / head_size ** 0.5)).astype(jnp.bfloat16).reshape(groups, length, head_count, head_size)
    key_rows = projected[:, channels:2 * channels].astype(jnp.bfloat16).reshape(groups, length, head_count, head_size)
    value_rows = projected[:, 2 * channels:].astype(jnp.bfloat16).reshape(groups, length, head_count, head_size)
    scores = product('gqhd,gkhd->ghqk', queries, key_rows) + window_bias[None]
    allowed = labels[:, None, :, None] == labels[:, None, None, :]
    scores = jnp.where(allowed, scores, -1e+30)
    scores = scores - lax.optimization_barrier(jnp.max(scores, axis=-1, keepdims=True))
    raised = jnp.exp(scores)
    attn_weights = (raised / lax.optimization_barrier(jnp.sum(raised, axis=-1, keepdims=True))).astype(jnp.bfloat16)
    context = product('ghqk,gkhd->gqhd', attn_weights, value_rows).astype(jnp.bfloat16).reshape(groups * length, channels)
    middle = (token_rows.astype(jnp.float32) + jnp.dot(context, w_proj, preferred_element_type=jnp.float32)).astype(jnp.bfloat16)
    normed_two = layer_norm(middle, mlp_gain)
    expanded = jax.nn.gelu(jnp.dot(normed_two, w_expand, preferred_element_type=jnp.float32)).astype(jnp.bfloat16)
    result = (middle.astype(jnp.float32) + jnp.dot(expanded, w_reduce, preferred_element_type=jnp.float32)).astype(jnp.bfloat16)
    return result.reshape(groups, length, channels)

def windowed(shifted, window_ids, patterns, weights):
    levels_here, lat_rows, lon_cols, channels = shifted.shape
    level_pairs = levels_here // 2
    band_count = lat_rows // LAT_DEV
    lon_windows = lon_cols // 6
    windows = shifted.reshape(level_pairs, 2, band_count, LAT_DEV, lon_windows, 6, channels).transpose(0, 2, 4, 1, 3, 5, 6)
    total_windows = level_pairs * band_count * lon_windows
    windows = windows.reshape(total_windows // GROUP, GROUP, 2 * LAT_DEV * 6, channels)
    choose = (window_ids.reshape(-1)[:, None] == jnp.arange(patterns.shape[0], dtype=jnp.int32)[None, :]).astype(jnp.int32)
    labels = lax.optimization_barrier(jnp.sum(choose[:, :, None] * patterns[None], axis=1)).reshape(total_windows // GROUP, GROUP, -1)
    runner = jax.checkpoint(lambda packed: window_block(packed[0], packed[1], weights))
    outcome = lax.map(runner, (windows, labels))
    outcome = outcome.reshape(level_pairs, band_count, lon_windows, 2, LAT_DEV, 6, channels).transpose(0, 3, 1, 4, 2, 5, 6)
    return outcome.reshape(levels_here, lat_rows, lon_cols, channels)

def assemble(field):
    rest = field.shape[4:]
    order = (0, 1, 3, 2, 4) + tuple(range(5, 5 + len(rest)))
    spread = field.reshape((field.shape[0], BANDS, LON_BLOCKS, LAT_DEV, LON_DEV) + rest).transpose(order)
    return spread.reshape((field.shape[0], BANDS * LAT_DEV, LON_BLOCKS * LON_DEV) + rest)

def split_tiles(field):
    rest = field.shape[3:]
    order = (0, 1, 3, 2, 4) + tuple(range(5, 5 + len(rest)))
    spread = field.reshape((field.shape[0], BANDS, LAT_DEV, LON_BLOCKS, LON_DEV) + rest).transpose(order)
    return spread.reshape((field.shape[0], TILES, LAT_DEV, LON_DEV) + rest)

def reference(features, attn_gain, w_qkv, w_proj, window_bias, patterns, window_pattern, mlp_gain, w_expand, w_reduce, temp_head, temp_base, thickness, level_weight, surface, target):
    weights = (attn_gain, w_qkv, w_proj, window_bias, mlp_gain, w_expand, w_reduce)
    half = LAT_DEV // 2

    def whole_layer(inputs):
        rolled = jnp.roll(inputs, (-1, -half, -3), axis=(0, 1, 2))
        return jnp.roll(windowed(rolled, window_pattern, patterns, weights), (1, half, 3), axis=(0, 1, 2))
    output, pullback = jax.vjp(whole_layer, assemble(features))
    temp_delta = jnp.dot(output, temp_head, preferred_element_type=jnp.float32)
    temps = temp_base[:, None, None] + temp_delta
    layer_thick = thickness[:, None, None] * temps
    height = assemble(surface[None])[0][None] + jnp.cumsum(layer_thick, axis=0)
    misfit = level_weight[:, None, None] * (height - assemble(target))
    carried = jnp.flip(jnp.cumsum(jnp.flip(misfit, 0), axis=0), 0)
    grad_temp = thickness[:, None, None] * carried
    grad_output = (grad_temp[..., None] * temp_head.astype(jnp.float32)).astype(jnp.bfloat16)
    grad_grid, = pullback(grad_output)
    return (split_tiles(height), split_tiles(grad_grid))
```

```python
import jax
import jax.numpy as jnp
import numpy as np
from jax import lax
from jax.experimental import pallas as pl
from jax.experimental.pallas import tpu as pltpu
from jax.sharding import PartitionSpec as P

F32 = jnp.float32
BF16 = jnp.bfloat16
C = 192
HEADS = 6
HEAD = 32
FF = 768
WIN = 144
HALF = 72
QUARTER = 36
LONS = 90
SHIFT = 3
BLOCKS = 4
BANDS = 16
LEVS = 4
GROUP = 8
ROWS = 240
WIDE = 896
EPS = 1e-05
VMEM_LIMIT = 56 * 1024 * 1024


def source_rows():
    table = np.zeros((GROUP * HALF, 6 * 112), np.float32)
    for m in range(GROUP * HALF):
        w, r, o = m // QUARTER, (m % QUARTER) // 6, m % 6
        e = 6 * w + o
        if w < 15:
            lon = e + SHIFT
            table[m, 112 * r + (lon if lon < LONS else 96 + lon - LONS)] = 1.0
    return table


def target_rows():
    table = np.zeros((6 * 96, (GROUP + 1) * HALF), np.float32)
    for m in range(GROUP * HALF):
        w, r, o = m // QUARTER, (m % QUARTER) // 6, m % 6
        lon = 6 * w + o + SHIFT
        if w < 15 and lon < LONS:
            table[96 * r + lon, m] = 1.0
    for r in range(6):
        for o in range(3):
            table[96 * r + o, GROUP * HALF + 6 * r + o + 3] = 1.0
    return table


def window_rows():
    table = np.zeros((2 * WIN, 2 * WIN), np.float32)
    for part in range(4):
        for col in range(2):
            for i in range(QUARTER):
                table[col * WIN + part * QUARTER + i, (part * 2 + col) * QUARTER + i] = 1.0
    return table


def dot(a, b):
    return jnp.dot(a, b, preferred_element_type=F32)


def dot_nt(a, b):
    return lax.dot_general(a, b, (((1,), (1,)), ((), ())), preferred_element_type=F32)


def lanes(shape):
    return lax.broadcasted_iota(jnp.int32, shape, len(shape) - 1)


def split3(value):
    top = value.astype(BF16).astype(F32)
    rest = value - top
    middle = rest.astype(BF16).astype(F32)
    return top, middle, rest - middle


def roll(value, steps):
    return pltpu.roll(value, steps % 128, 1)


def pack_block(out_ref, at, first, second, spare):
    lane = lanes((HALF, 128))
    out_ref[at, 0:WIN, :] = jnp.concatenate(first, axis=0).astype(BF16)
    tail = jnp.where(lane < 64, second[0], roll(second[1], 64))
    tail = jnp.concatenate([tail, jnp.zeros((8, 128), F32)], axis=0)
    both = jnp.concatenate(second, axis=0)
    lane16 = lanes((16, 128))
    extra = spare
    for g in range(9):
        moved = roll(both[16 * g : 16 * g + 16], 8 * g - 64)
        extra = jnp.where((lane16 >= 8 * g) & (lane16 < 8 * g + 8), moved, extra)
    out_ref[at, WIN : WIN + 16, :] = extra.astype(BF16)
    out_ref[at, WIN + 16 : ROWS, :] = tail.astype(BF16)


def unpack_block(block):
    first = block[0:WIN].astype(F32)
    extra = block[WIN : WIN + 16].astype(F32)
    tail = block[WIN + 16 : ROWS].astype(F32)[0:HALF]
    lane16 = lanes((16, 128))
    keep = (lane16 >= 64) & (lane16 < 72)
    spread = [jnp.where(keep, roll(extra, 64 - 8 * g), 0.0) for g in range(9)]
    spread = jnp.concatenate(spread, axis=0)
    lane = lanes((HALF, 128))
    second = [
        jnp.where(lane < 64, tail, spread[0:HALF]),
        jnp.where(lane < 64, roll(tail, 64), spread[HALF:WIN]),
    ]
    return first, second, extra


def prep_kernel(
    start_ref, ids_ref, thick_ref, weight_ref, base_ref,
    f_ref, edge_ref, target_ref, surface_ref, perm_ref,
    out_ref, rows_ref, made_ref,
):
    start = start_ref[0]
    rows_ref[...] = jnp.zeros(rows_ref.shape, BF16)
    surf = jnp.where(start == 0, surface_ref[0:6, :], surface_ref[6:12, :])
    lane = lanes((LONS, 128))
    for lev in range(2):
        goal = jnp.where(start == 0, target_ref[lev, 0:6, :], target_ref[lev, 6:12, :])
        values = split3(goal) + split3(surf)
        stacked = []
        for r in range(6):
            stacked += [v[r : r + 1] for v in values]
            stacked.append(jnp.zeros((2, LONS), F32))
        stacked.append(jnp.zeros((128 - 48, LONS), F32))
        columns = jnp.concatenate(stacked, axis=0)
        columns = jnp.concatenate([columns, jnp.zeros((128, 128 - LONS), F32)], axis=1).T
        for r in range(6):
            row = f_ref[lev, start + r]
            second = jnp.concatenate(
                [row[:, 128:].astype(F32), jnp.zeros((LONS, 64), F32)], axis=1
            )
            extra = roll(columns, 64 - 8 * r)[0:LONS]
            second = jnp.where(lane < 64, second, jnp.where(lane < 72, extra, 0.0))
            rows_ref[112 * r : 112 * r + LONS, 0:128] = row[:, 0:128]
            rows_ref[112 * r : 112 * r + LONS, 128:256] = second.astype(BF16)
            rows_ref[112 * r + 96 : 112 * r + 104, :] = edge_ref[lev, start + r]
        made_ref[lev] = dot(perm_ref[...], rows_ref[...])
    lane16 = lanes((16, 128))
    row16 = lax.broadcasted_iota(jnp.int32, (16, 128), 0)
    scalars = jnp.zeros((16, 128), F32)
    for lev in range(2):
        for k, ref in enumerate((thick_ref, weight_ref, base_ref)):
            scalars = jnp.where((row16 == lev) & (lane16 == 72 + k), ref[lev], scalars)
    top, middle, low = split3(scalars)
    scalars = top + roll(middle, 3) + roll(low, 6)
    for d in range(GROUP):
        spare = scalars
        for p in range(4):
            for col in range(2):
                if 2 * d + col < 15:
                    ident = ids_ref[p, 2 * d + col].astype(F32)
                    spare = jnp.where((row16 == 2 + p) & (lane16 == 81 + col), ident, spare)
        at = slice(HALF * d, HALF * d + HALF)
        pack_block(
            out_ref, d,
            [made_ref[lev, at, 0:128] for lev in range(2)],
            [made_ref[lev, at, 128:256] for lev in range(2)],
            spare,
        )


def vmem():
    return pl.BlockSpec(memory_space=pltpu.VMEM)


def smem():
    return pl.BlockSpec(memory_space=pltpu.SMEM)


def prep(start, ids, thick, weight, base, feats, edge, target, surface, perm):
    return pl.pallas_call(
        prep_kernel,
        out_shape=jax.ShapeDtypeStruct((GROUP, ROWS, 128), BF16),
        in_specs=[smem()] * 5 + [vmem()] * 5,
        out_specs=vmem(),
        scratch_shapes=[
            pltpu.VMEM((6 * 112, 256), BF16),
            pltpu.VMEM((2, GROUP * HALF, 256), F32),
        ],
        compiler_params=pltpu.CompilerParams(vmem_limit_bytes=VMEM_LIMIT),
        cost_estimate=pl.CostEstimate(
            flops=3_000_000_000, bytes_accessed=2_500_000, transcendentals=0
        ),
        name="prep",
    )(start, ids, thick, weight, base, feats, edge, target, surface, perm)


def post_kernel(
    lower_ref, a_ref, b_ref, ea_ref, eb_ref, perm_ref, height_ref, grad_ref, rows_ref
):
    lower = lower_ref[0] == 1
    lane = lanes((96, 128))
    for half in range(2):
        for d in range(GROUP + 1):
            one = a_ref[d] if d < GROUP else ea_ref[...]
            two = b_ref[d] if d < GROUP else eb_ref[...]
            take = lower if half == 1 else jnp.logical_not(lower)
            block = jnp.where(take, one, two)
            first, second, _ = unpack_block(block)
            for lev in range(2):
                at = slice(HALF * d, HALF * d + HALF)
                rows_ref[lev, at, 0:128] = first[HALF * lev : HALF * lev + HALF]
                rows_ref[lev, at, 128:256] = second[lev]
        for lev in range(2):
            made = dot(perm_ref[...], rows_ref[lev].astype(BF16))
            columns = jnp.zeros((96, 128), F32)
            for r in range(6):
                grad_ref[lev, 6 * half + r] = made[96 * r : 96 * r + LONS, 0:C].astype(BF16)
                tile = made[96 * r : 96 * r + 96, 128:256]
                total = (tile + roll(tile, -1)) + roll(tile, -2)
                columns = jnp.where(lane == r, roll(total, r - 64), columns)
            columns = columns.T
            height_ref[lev, 6 * half : 6 * half + 6, :] = columns[0:6, 0:LONS]


def post(lower, a, b, ea, eb, perm):
    return pl.pallas_call(
        post_kernel,
        out_shape=(
            jax.ShapeDtypeStruct((2, 12, LONS), F32),
            jax.ShapeDtypeStruct((2, 12, LONS, C), BF16),
        ),
        in_specs=[smem()] + [vmem()] * 5,
        out_specs=(vmem(), vmem()),
        scratch_shapes=[pltpu.VMEM((2, (GROUP + 1) * HALF, 256), F32)],
        compiler_params=pltpu.CompilerParams(vmem_limit_bytes=VMEM_LIMIT),
        cost_estimate=pl.CostEstimate(
            flops=3_000_000_000, bytes_accessed=2_500_000, transcendentals=0
        ),
        name="post",
    )(lower, a, b, ea, eb, perm)


def norm_parts(x):
    center = jnp.sum(x, axis=-1, keepdims=True) * (1.0 / C)
    moved = x - center
    spread = jnp.sum(moved * moved, axis=-1, keepdims=True) * (1.0 / C)
    scale = lax.rsqrt(spread + EPS)
    return moved * scale, scale


def norm_back(cotangent, hat, scale):
    mean = jnp.sum(cotangent, axis=-1, keepdims=True) * (1.0 / C)
    along = jnp.sum(cotangent * hat, axis=-1, keepdims=True) * (1.0 / C)
    return scale * (cotangent - mean - hat * along)


def fill_diagonal(ref, turned):
    lane = lanes((HEAD, 128))
    for h in range(HEADS):
        rows = slice(HEAD * h, HEAD * h + HEAD)
        ref[rows, 128 * h : 128 * h + 128] = turned[rows, 0:128].astype(BF16)
        tail = jnp.concatenate([turned[rows, 128:WIN], jnp.zeros((HEAD, 112), F32)], axis=1)
        tail = roll(tail, 16 * h)
        tail = jnp.where((lane >= 16 * h) & (lane < 16 * h + 16), tail, 0.0)
        ref[rows, 768:WIDE] = tail.astype(BF16)


def gather_heads(turned, weights):
    main = [
        dot(turned[HEAD * h : HEAD * h + HEAD], weights[:, 128 * h : 128 * h + 128])
        for h in range(HEADS)
    ]
    main = jnp.concatenate(main, axis=0).T
    tail = dot(turned, weights[:, 768:WIDE]).T
    lane = lanes((16, C))
    last = jnp.zeros((16, C), F32)
    for h in range(HEADS):
        mine = (lane >= HEAD * h) & (lane < HEAD * h + HEAD)
        last = jnp.where(mine, tail[16 * h : 16 * h + 16], last)
    return jnp.concatenate([main, last], axis=0)


def head_rows(value):
    lane = lanes((WIN, C))
    parts, tails = [], []
    for h in range(HEADS):
        mine = jnp.where((lane >= HEAD * h) & (lane < HEAD * h + HEAD), value, 0.0).astype(BF16)
        parts.append(mine[0:128])
        tails.append(mine[128:WIN])
    return jnp.concatenate(parts + tails + [jnp.zeros((32, C), BF16)], axis=0)


def main_kernel(
    x_ref, order_ref, back_ref, w_ref, wt_ref, proj_ref, projt_ref, expand_ref, expandt_ref,
    reduce_ref, bias_ref, pat_q_ref, pat_k_ref, gains_ref,
    out_ref,
    tok_in, tok, diag_q, diag_n, probs, dscores, q_rows, n_rows, dq_rows, resid, hats, scales,
    deltas, source, heights, levels_ref, made,
):
    scale_q = 1.0 / HEAD**0.5
    lane72 = lanes((HALF, 128))
    for s in range(GROUP):
        first, second, extra = unpack_block(x_ref[s])
        tok_in[s, :, 0:128] = first
        tok_in[s, 0:HALF, 128:256] = second[0]
        tok_in[s, HALF:WIN, 128:256] = second[1]
        if s < 4:
            whole = (extra + roll(extra, -3)) + roll(extra, -6)
            lane16 = lanes((16, 128))
            levels_ref[s] = jnp.where(lane16 < 75, whole, extra)
    diag_q[...] = jnp.zeros(diag_q.shape, BF16)
    diag_n[...] = jnp.zeros(diag_n.shape, BF16)

    def place(p, part):
        a, beta = part // 2, part % 2
        return beta * 4 + (p + a) % 4, (HALF if a == 0 else 0)

    for p in range(4):
        pieces = []
        for part in range(4):
            s, at = place(p, part)
            pieces.append(tok_in[s, at : at + HALF, :])
        moved = dot(order_ref[...], jnp.concatenate(pieces, axis=0).astype(BF16))
        tok[2 * p] = moved[0:WIN]
        tok[2 * p + 1] = moved[WIN : 2 * WIN]

    gain_one = gains_ref[0:1, 0:C]
    gain_two = gains_ref[1:2, 0:C]
    head_row = gains_ref[2:3, 0:C]
    head_eight = jnp.broadcast_to(head_row, (8, C)).astype(BF16)
    u_row = dot_nt(head_eight, reduce_ref[...])[0:1]

    def forward(i, carry):
        p = i // 2
        col = i - 2 * p
        x = tok[i, :, 0:C]
        hat, scale = norm_parts(x)
        normed = (hat * gain_one).astype(BF16)
        hats[i] = hat
        scales[i] = jnp.broadcast_to(scale, (WIN, 128))
        turned = dot_nt(wt_ref[...], normed)
        queries = (dot(normed, w_ref[0]) * scale_q).astype(BF16)
        keys = dot(normed, w_ref[1]).astype(BF16)
        values = dot(normed, w_ref[2]).astype(BF16)
        q_rows[i] = queries
        fill_diagonal(diag_q, turned[0:C] * scale_q)
        keys_t = turned[C : 2 * C].astype(BF16)
        values_t = turned[2 * C : 3 * C].astype(BF16)
        scores = dot(keys, diag_q[...]) + bias_ref[...]
        idents = levels_ref[0]
        lane16 = lanes((16, 128))
        row16 = lax.broadcasted_iota(jnp.int32, (16, 128), 0)
        spot = (row16 == 2 + p) & (lane16 == 81 + col)
        ident = jnp.sum(jnp.where(spot, idents, 0.0), axis=0, keepdims=True)
        ident = jnp.sum(ident, axis=1, keepdims=True)
        row8 = lax.broadcasted_iota(jnp.int32, (8, 1), 0).astype(F32)
        label_q = jnp.sum(jnp.where(row8 == ident, pat_q_ref[...], 0.0), axis=0, keepdims=True)
        lane8 = lanes((1, 8)).astype(F32)
        label_k = jnp.sum(jnp.where(lane8 == ident, pat_k_ref[...], 0.0), axis=1, keepdims=True)
        scores = jnp.where(label_k == label_q, scores, -1e30)
        raised = jnp.exp(scores - jnp.max(scores, axis=0, keepdims=True))
        weights = (raised * (1.0 / jnp.sum(raised, axis=0, keepdims=True))).astype(BF16)
        probs[i] = weights
        context = gather_heads(values_t, weights).astype(BF16)
        middle = (x + dot(context, proj_ref[...])).astype(BF16).astype(F32)
        hat_two, scale_two = norm_parts(middle)
        normed_two = (hat_two * gain_two).astype(BF16)
        acc = jnp.zeros((WIN, 256), F32)
        back = jnp.zeros((WIN, C), F32)
        for f in range(3):
            at = slice(256 * f, 256 * f + 256)
            pre = dot(normed_two, expand_ref[:, at])
            u = u_row[:, at]
            square = pre * pre
            c0 = 0.7978845608028654
            wave = jnp.tanh(pre * (c0 + (c0 * 0.044715) * square))
            half = 0.5 * pre
            acc = acc + (half + half * wave) * u
            slope = (0.5 + 0.5 * wave) + half * (1.0 - wave * wave) * (
                c0 + (3.0 * c0 * 0.044715) * square
            )
            back = back + dot((slope * u).astype(BF16), expandt_ref[at, :])
        delta = jnp.sum(acc, axis=1, keepdims=True) + jnp.sum(
            middle * head_row, axis=1, keepdims=True
        )
        deltas[i] = jnp.broadcast_to(delta, (WIN, 128))
        kept = head_row + norm_back(back * gain_two, hat_two, scale_two)
        resid[i] = kept
        kept = kept.astype(BF16)
        fill_diagonal(diag_n, dot_nt(proj_ref[...], kept))
        n_rows[i] = dot(kept, projt_ref[...]).astype(BF16)
        dweights = dot(values, diag_n[...])
        weights = weights.astype(F32)
        inner = jnp.sum(weights * dweights, axis=0, keepdims=True)
        dscore = (weights * (dweights - inner)).astype(BF16)
        dscores[i] = dscore
        dq_rows[i] = gather_heads(keys_t, dscore)
        return carry

    lax.fori_loop(0, 8, forward, 0)

    def scalar(l, k):
        return levels_ref[l // 2, l % 2 : l % 2 + 1, 72 + k : 73 + k]

    for col in range(2):
        total = jnp.zeros((HALF, 128), F32)
        misfits, spots = [], []
        for l in range(8):
            a = 1 - l % 2
            i = 2 * ((l // 2 - a) % 4) + col
            rows = slice(HALF * a, HALF * a + HALF)
            spots.append((i, rows))
            extra = tok[i, rows, 128:256]
            goal = (extra[:, 64:65] + extra[:, 65:66]) + extra[:, 66:67]
            ground = (extra[:, 67:68] + extra[:, 68:69]) + extra[:, 69:70]
            temps = scalar(l, 2) + deltas[i, rows, :]
            total = total + scalar(l, 0) * temps
            height = ground + total
            misfits.append(scalar(l, 1) * (height - goal))
            top, middle, low = split3(height)
            heights[i, rows, :] = jnp.where(
                lane72 == 64, top, jnp.where(lane72 == 65, middle, low)
            )
        carried = jnp.zeros((HALF, 128), F32)
        for l in reversed(range(8)):
            i, rows = spots[l]
            carried = carried + misfits[l]
            source[i, rows, :] = scalar(l, 0) * carried

    def backward(i, carry):
        s = source[i, :, 0:1]
        dk = dot(dscores[i], head_rows(s * q_rows[i].astype(F32))).astype(BF16)
        dv = dot(probs[i], head_rows(s * n_rows[i].astype(F32))).astype(BF16)
        dq = ((s * scale_q) * dq_rows[i]).astype(BF16)
        dnormed = (
            dot(dq, wt_ref[0:C, :]) + dot(dk, wt_ref[C : 2 * C, :]) + dot(dv, wt_ref[2 * C :, :])
        )
        dx = norm_back(dnormed * gain_one, hats[i], scales[i, :, 0:1])
        grad = s * resid[i] + dx
        lane = lanes((WIN, 128))
        last = jnp.concatenate([grad[:, 128:C], jnp.zeros((WIN, 64), F32)], axis=1)
        last = jnp.where(lane < 64, last, jnp.where(lane < 67, heights[i], 0.0))
        made[i, :, 0:128] = grad[:, 0:128].astype(BF16)
        made[i, :, 128:256] = last.astype(BF16)
        return carry

    lax.fori_loop(0, 8, backward, 0)

    for p in range(4):
        moved = dot(back_ref[...], jnp.concatenate([made[2 * p], made[2 * p + 1]], axis=0))
        for part in range(4):
            s, at = place(p, part)
            tok_in[s, at : at + HALF, :] = moved[HALF * part : HALF * part + HALF]
    zero = jnp.zeros((16, 128), F32)
    for s in range(GROUP):
        pack_block(
            out_ref, s,
            [tok_in[s, HALF * k : HALF * k + HALF, 0:128] for k in range(2)],
            [tok_in[s, HALF * k : HALF * k + HALF, 128:256] for k in range(2)],
            zero,
        )


def layer(x, consts):
    return pl.pallas_call(
        main_kernel,
        out_shape=jax.ShapeDtypeStruct((GROUP, ROWS, 128), BF16),
        in_specs=[vmem()] * (1 + len(consts)),
        out_specs=vmem(),
        scratch_shapes=[
            pltpu.VMEM((GROUP, WIN, 256), F32),
            pltpu.VMEM((8, WIN, 256), F32),
            pltpu.VMEM((C, WIDE), BF16),
            pltpu.VMEM((C, WIDE), BF16),
            pltpu.VMEM((8, WIN, WIDE), BF16),
            pltpu.VMEM((8, WIN, WIDE), BF16),
            pltpu.VMEM((8, WIN, C), BF16),
            pltpu.VMEM((8, WIN, C), BF16),
            pltpu.VMEM((8, WIN, C), F32),
            pltpu.VMEM((8, WIN, C), F32),
            pltpu.VMEM((8, WIN, C), F32),
            pltpu.VMEM((8, WIN, 128), F32),
            pltpu.VMEM((8, WIN, 128), F32),
            pltpu.VMEM((8, WIN, 128), F32),
            pltpu.VMEM((8, WIN, 128), F32),
            pltpu.VMEM((4, 16, 128), F32),
            pltpu.VMEM((8, WIN, 256), BF16),
        ],
        compiler_params=pltpu.CompilerParams(vmem_limit_bytes=VMEM_LIMIT),
        cost_estimate=pl.CostEstimate(
            flops=20_000_000_000, bytes_accessed=4_000_000, transcendentals=3_000_000
        ),
        name="layer",
    )(x, *consts)


def pair_groups(odd):
    out = []
    for block in range(BLOCKS):
        for band in range(odd, BANDS, 2):
            members = (band, (band + 1) % BANDS)
            out.append(
                [(b * BLOCKS + block) * LEVS + lev for b in members for lev in range(LEVS)]
            )
    return out


def exchange(blocks, odd):
    return lax.all_to_all(
        blocks, ("tile", "lev"), 0, 0, axis_index_groups=pair_groups(odd)
    )


def block_step(value, steps):
    pairs = [
        (t, t - t % BLOCKS + (t + steps) % BLOCKS) for t in range(BANDS * BLOCKS)
    ]
    return lax.ppermute(value, "tile", pairs)


def exact_parts(value):
    top = lax.reduce_precision(value, 8, 7)
    middle = lax.reduce_precision(value - top, 8, 7)
    return [top, middle, value - top - middle]


def by_head_columns(value):
    main = value[:, :, 0:128].reshape(WIN, 768)
    tail = value[:, :, 128:WIN].reshape(WIN, 96)
    return jnp.pad(jnp.concatenate([main, tail], axis=1), ((0, 0), (0, 32)))


def on_device(
    features, attn_gain, w_qkv, w_proj, window_bias, patterns, window_pattern, mlp_gain,
    w_expand, w_reduce, temp_head, temp_base, thickness, level_weight, surface, target,
):
    feats = features[:, 0]
    goal = target[:, 0]
    ground = surface[0]
    rim = exact_parts(goal[:, :, 0:8]) + exact_parts(
        jnp.broadcast_to(ground[None, :, 0:8], (2, 12, 8))
    )
    rim = jnp.stack(rim + [jnp.zeros((2, 12, 8), F32)] * 2, axis=-1).astype(BF16)
    edge = jnp.concatenate(
        [feats[:, :, 0:8, :], rim, jnp.zeros((2, 12, 8, 56), BF16)], axis=-1
    )
    edge = block_step(edge, -1)

    band = lax.axis_index("tile") // BLOCKS
    even = (band % 2 == 0).astype(jnp.int32)
    perm = jnp.asarray(source_rows(), BF16)
    perm_back = jnp.asarray(target_rows(), BF16)
    order = jnp.asarray(window_rows(), BF16)
    order_back = jnp.asarray(window_rows().T, BF16)

    pat = patterns.astype(F32)
    pat_q = jnp.concatenate(
        [jnp.tile(pat[:, 0:128], (1, HEADS)), jnp.tile(pat[:, 128:WIN], (1, HEADS + 2))], axis=1
    )
    gains = jnp.pad(
        jnp.stack([attn_gain, mlp_gain, temp_head.astype(F32)]), ((0, 5), (0, 64))
    )
    consts = (
        order, order_back,
        jnp.stack([w_qkv[:, 0:C], w_qkv[:, C : 2 * C], w_qkv[:, 2 * C :]]),
        w_qkv.T, w_proj, w_proj.T, w_expand, w_expand.T, w_reduce,
        by_head_columns(window_bias.transpose(2, 0, 1)),
        pat_q, pat.T, gains,
    )

    made, back = [], []
    for odd in range(2):
        start = (6 * (even if odd == 0 else 1 - even)).reshape(1)
        made.append(
            prep(
                start, window_pattern, thickness, level_weight, temp_base,
                feats, edge, goal, ground, perm,
            )
        )
    for odd in range(2):
        got = exchange(made[odd], odd)
        back.append(exchange(layer(got, consts), odd))
    rims = [block_step(b[GROUP - 1], 1) for b in back]
    height, grad = post(even.reshape(1), back[0], back[1], rims[0], rims[1], perm_back)
    return height[:, None], grad[:, None]


def solution(mesh):
    placed = (
        P("lev", "tile", None, None, None),
        P(), P(), P(), P(), P(),
        P(None, "tile"),
        P(), P(), P(), P(),
        P("lev"), P("lev"), P("lev"),
        P("tile", None, None),
        P("lev", "tile", None, None),
    )
    return jax.shard_map(
        on_device,
        mesh=mesh,
        in_specs=placed,
        out_specs=(P("lev", "tile", None, None), P("lev", "tile", None, None, None)),
        check_vma=False,
    )
```

```python
import jax
import jax.numpy as jnp
import numpy as np
from jax import lax
from jax.experimental import pallas as pl
from jax.experimental.pallas import tpu as pltpu
from jax.sharding import PartitionSpec as P

F32 = jnp.float32
BF16 = jnp.bfloat16
C = 192
HEADS = 6
HEAD = 32
FF = 768
WIN = 144
HALF = 72
QUARTER = 36
LONS = 90
SHIFT = 3
BLOCKS = 4
BANDS = 16
LEVS = 4
GROUP = 8
ROWS = 240
WIDE = 896
EPS = 1e-05
VMEM_LIMIT = 28 * 1024 * 1024
SMALL_VMEM = 12 * 1024 * 1024
VMEM_ALL = 60 * 1024 * 1024


def source_rows():
    table = np.zeros((2 * WIN, 6 * 64), np.float32)
    for q in range(2):
        for lev in range(2):
            for col in range(2):
                for i in range(QUARTER):
                    r, o = i // 6, i % 6
                    place = 2 * (12 * q + 6 * col + o + SHIFT) + lev
                    table[((q * 2 + lev) * 2 + col) * QUARTER + i, 64 * r + place] = 1.0
    return table


def target_rows():
    table = np.zeros((6 * 48, 3 * WIN), np.float32)
    for r in range(6):
        for x in range(48):
            e, lev = x // 2 + 9, x % 2
            d, col, o = e // 12, e % 12 // 6, e % 6
            table[48 * r + x, d * WIN + lev * HALF + col * QUARTER + 6 * r + o] = 1.0
    return table


def window_rows():
    table = np.zeros((WIN, WIN), np.float32)
    for col in range(2):
        for beta in range(2):
            for i in range(QUARTER):
                table[(col * 2 + beta) * QUARTER + i, (beta * 2 + col) * QUARTER + i] = 1.0
    return table


def dot(a, b):
    return jnp.dot(a, b, preferred_element_type=F32)


def dot_nt(a, b):
    return lax.dot_general(a, b, (((1,), (1,)), ((), ())), preferred_element_type=F32)


def lanes(shape):
    return lax.broadcasted_iota(jnp.int32, shape, len(shape) - 1)


def split3(value):
    top = value.astype(BF16).astype(F32)
    rest = value - top
    middle = rest.astype(BF16).astype(F32)
    return top, middle, rest - middle


def roll(value, steps):
    return pltpu.roll(value, steps % 128, 1)


def pack_block(out_ref, at, made, spare):
    lane = lanes((HALF, 128))
    out_ref[at, 0:WIN, :] = made[:, 0:128].astype(BF16)
    both = made[:, 128:256]
    tail = jnp.where(lane < 64, both[0:HALF], roll(both[HALF:WIN], 64))
    tail = jnp.concatenate([tail, jnp.zeros((8, 128), F32)], axis=0)
    lane16 = lanes((16, 128))
    extra = spare
    for g in range(9):
        moved = roll(both[16 * g : 16 * g + 16], 8 * g - 64)
        extra = jnp.where((lane16 >= 8 * g) & (lane16 < 8 * g + 8), moved, extra)
    out_ref[at, WIN : WIN + 16, :] = extra.astype(BF16)
    out_ref[at, WIN + 16 : ROWS, :] = tail.astype(BF16)


def unpack_block(block):
    first = block[0:WIN].astype(F32)
    extra = block[WIN : WIN + 16].astype(F32)
    tail = block[WIN + 16 : ROWS].astype(F32)[0:HALF]
    lane16 = lanes((16, 128))
    keep = (lane16 >= 64) & (lane16 < 72)
    spread = [jnp.where(keep, roll(extra, 64 - 8 * g), 0.0) for g in range(9)]
    spread = jnp.concatenate(spread, axis=0)
    lane = lanes((HALF, 128))
    second = [
        jnp.where(lane < 64, tail, spread[0:HALF]),
        jnp.where(lane < 64, roll(tail, 64), spread[HALF:WIN]),
    ]
    return first, second, extra


def vmem():
    return pl.BlockSpec(memory_space=pltpu.VMEM)


def smem():
    return pl.BlockSpec(memory_space=pltpu.SMEM)


def field_rows(targets, ground, count, padded):
    blank = jnp.zeros((count, 128 - LONS), F32)
    goal = [jnp.concatenate([t, blank], axis=1) for t in targets]
    ground = jnp.concatenate([ground, blank], axis=1)
    parts = split3(jnp.concatenate(goal, axis=1)) + split3(
        jnp.concatenate([ground, ground], axis=1)
    )
    if padded > count:
        more = jnp.zeros((padded - count, 256), F32)
        parts = [jnp.concatenate([v, more], axis=0) for v in parts]
    stacked = jnp.concatenate(parts, axis=0).astype(BF16)
    i = lax.broadcasted_iota(jnp.int32, (128, 6 * padded), 0)
    j = lanes((128, 6 * padded))
    hit = (j == padded * (i & 7) + (i >> 3)) & ((i & 7) < 6) & ((i >> 3) < count)
    return dot(jnp.where(hit, 1.0, 0.0).astype(BF16), stacked).astype(BF16)


def lon_pick(rows, first):
    x = lax.broadcasted_iota(jnp.int32, (rows, 256), 0)
    y = lanes((rows, 256))
    return jnp.where(y == 128 * (x & 1) + (x >> 1) + first, 1.0, 0.0).astype(BF16)


def rim_kernel(ids_ref, fa_ref, fb_ref, target_ref, surface_ref, next_ref, prev_ref):
    targets = [
        jnp.concatenate([target_ref[lev, r] for r in range(12)], axis=0) for lev in range(2)
    ]
    ground = jnp.concatenate([surface_ref[r] for r in range(12)], axis=0)
    fields = field_rows(targets, ground, 12, 16)
    spots = jnp.concatenate([lon_pick(8, 0), lon_pick(8, 86)], axis=0)
    values = dot_nt(spots, fields)
    lane = lanes((8, 128))
    idents = jnp.zeros((8, 128), F32)
    for p in range(4):
        idents = jnp.where(lane == 72 + p, ids_ref[p, 14].astype(F32), idents)
    for out_ref, f_ref, at, row, more in (
        (next_ref, fa_ref, 0, 0, 0.0), (prev_ref, fb_ref, 12, 8, idents)
    ):
        made = []
        for r in range(12):
            tokens = f_ref[r].reshape(20, C).astype(F32)[at : at + 8]
            second = jnp.concatenate([tokens[:, 128:C], jnp.zeros((8, 64), F32)], axis=1)
            extra = roll(values, 64 - 8 * r)[row : row + 8]
            second = jnp.where(lane < 64, second, jnp.where(lane < 72, extra, more))
            made.append(jnp.concatenate([tokens[:, 0:128], second], axis=1))
        out_ref[...] = jnp.concatenate(made, axis=0).astype(BF16)


def rim(ids, feats, target, surface):
    edge = jax.ShapeDtypeStruct((96, 256), BF16)
    return pl.pallas_call(
        rim_kernel,
        out_shape=(edge, edge),
        grid=(1,),
        in_specs=[
            smem(),
            pl.BlockSpec((12, 10, 2, C), lambda i: (0, 0, 0, 0)),
            pl.BlockSpec((12, 10, 2, C), lambda i: (0, 8, 0, 0)),
            pl.BlockSpec((2, 12, 1, LONS), lambda i: (0, 0, 0, 0)),
            pl.BlockSpec((12, 1, LONS), lambda i: (0, 0, 0)),
        ],
        out_specs=(
            pl.BlockSpec((96, 256), lambda i: (0, 0)),
            pl.BlockSpec((96, 256), lambda i: (0, 0)),
        ),
        compiler_params=pltpu.CompilerParams(vmem_limit_bytes=VMEM_ALL),
        name="rim",
    )(ids, feats, feats, target, surface)


def prep_kernel(
    half_ref, ids_ref, thick_ref, weight_ref, base_ref,
    f_ref, next_ref, prev_ref, target_ref, surface_ref, perm_ref,
    out_ref, rows_ref,
):
    targets = [
        jnp.concatenate([target_ref[lev, r] for r in range(6)], axis=0) for lev in range(2)
    ]
    ground = jnp.concatenate([surface_ref[r] for r in range(6)], axis=0)
    values = dot_nt(lon_pick(2 * LONS, 0), field_rows(targets, ground, 6, 8))
    after = next_ref[...].astype(F32)
    before = prev_ref[...].astype(F32)
    lane = lanes((2 * LONS, 128))
    for r in range(6):
        tokens = f_ref[r].reshape(2 * LONS, C).astype(F32)
        second = jnp.concatenate([tokens[:, 128:C], jnp.zeros((2 * LONS, 64), F32)], axis=1)
        extra = jnp.where(lane < 72, roll(values, 64 - 8 * r), 0.0)
        second = jnp.where(lane < 64, second, extra)
        for at, part in ((0, tokens[:, 0:128]), (128, second)):
            cut = slice(at, at + 128)
            rows_ref[208 * r : 208 * r + 176, cut] = part[0:176].astype(BF16)
            tail = [
                part[176:180],
                after[8 * r : 8 * r + 6, cut],
                before[8 * r + 2 : 8 * r + 8, cut],
                part[0:6],
                jnp.zeros((10, 128), F32),
            ]
            tail = jnp.concatenate(tail, axis=0).astype(BF16)
            rows_ref[208 * r + 176 : 208 * r + 208, cut] = tail
    lane16 = lanes((16, 128))
    row16 = lax.broadcasted_iota(jnp.int32, (16, 128), 0)
    scalars = jnp.zeros((16, 128), F32)
    for lev in range(2):
        for k, ref in enumerate((thick_ref, weight_ref, base_ref)):
            scalars = jnp.where((row16 == lev) & (lane16 == 72 + k), ref[lev], scalars)
    top, middle, low = split3(scalars)
    scalars = top + roll(middle, 3) + roll(low, 6)
    for m in range(4):
        source = [rows_ref[208 * r + 48 * m : 208 * r + 48 * m + 64, :] for r in range(6)]
        made = dot(perm_ref[...], jnp.concatenate(source, axis=0))
        for q in range(2):
            d = 2 * m + q
            spare = scalars
            for p in range(4):
                for col in range(2):
                    if 2 * d + col < 15:
                        ident = ids_ref[p, 2 * d + col].astype(F32)
                    else:
                        ident = before[0:1, 200 + p : 201 + p]
                    spare = jnp.where((row16 == 2 + p) & (lane16 == 81 + col), ident, spare)
            pack_block(out_ref, d, made[WIN * q : WIN * q + WIN], spare)


def prep(half, ids, thick, weight, base, feats, after, before, target, surface, perm):
    return pl.pallas_call(
        prep_kernel,
        out_shape=jax.ShapeDtypeStruct((GROUP, ROWS, 128), BF16),
        grid_spec=pltpu.PrefetchScalarGridSpec(
            num_scalar_prefetch=1,
            grid=(1,),
            in_specs=[smem()] * 4
            + [
                pl.BlockSpec((6, LONS, 2, C), lambda i, h: (h[0], 0, 0, 0)),
                pl.BlockSpec((48, 256), lambda i, h: (h[0], 0)),
                pl.BlockSpec((48, 256), lambda i, h: (h[0], 0)),
                pl.BlockSpec((2, 6, 1, LONS), lambda i, h: (0, h[0], 0, 0)),
                pl.BlockSpec((6, 1, LONS), lambda i, h: (h[0], 0, 0)),
                pl.BlockSpec((2 * WIN, 384), lambda i, h: (0, 0)),
            ],
            out_specs=pl.BlockSpec((GROUP, ROWS, 128), lambda i, h: (0, 0, 0)),
            scratch_shapes=[pltpu.VMEM((6 * 208, 256), BF16)],
        ),
        compiler_params=pltpu.CompilerParams(vmem_limit_bytes=SMALL_VMEM),
        cost_estimate=pl.CostEstimate(
            flops=1_000_000_000, bytes_accessed=2_500_000, transcendentals=0
        ),
        name="prep",
    )(half, ids, thick, weight, base, feats, after, before, target, surface, perm)


def post_kernel(half_ref, x_ref, perm_ref, *refs):
    height_ref, grad_ref, rows_ref = refs[-3:]
    for d in range(GROUP):
        first, second, _ = unpack_block(x_ref[d])
        rows_ref[d, :, 0:128] = first.astype(BF16)
        rows_ref[d, :, 128:256] = jnp.concatenate(second, axis=0).astype(BF16)
    lane = lanes((48, 128))
    columns = []
    for m in range(4):
        source = [rows_ref[(2 * m + k) % GROUP] for k in (-1, 0, 1)]
        made = dot(perm_ref[...], jnp.concatenate(source, axis=0))
        count = 24 if m < 3 else 18
        column = jnp.zeros((48, 128), F32)
        for r in range(6):
            tokens = made[48 * r : 48 * r + 2 * count, 0:C].astype(BF16)
            grad_ref[r, 24 * m : 24 * m + count] = tokens.reshape(count, 2, C)
            moved = roll(made[48 * r : 48 * r + 48, 128:256], 8 * r - 64)
            column = jnp.where((lane >= 8 * r) & (lane < 8 * r + 3), moved, column)
        columns.append(column)
    columns = jnp.concatenate(columns, axis=0).astype(BF16)
    rows = lax.dot_general(
        columns, lon_pick(192, 0), (((0,), (0,)), ((), ())), preferred_element_type=F32
    )
    for r in range(6):
        row = rows[8 * r : 8 * r + 1] + rows[8 * r + 1 : 8 * r + 2] + rows[8 * r + 2 : 8 * r + 3]
        for lev in range(2):
            height_ref[lev, r] = row[:, 128 * lev : 128 * lev + LONS]


def post(half, blocks, perm, earlier):
    kept = [] if earlier is None else list(earlier)
    return pl.pallas_call(
        post_kernel,
        out_shape=(
            jax.ShapeDtypeStruct((2, 12, 1, LONS), F32),
            jax.ShapeDtypeStruct((12, LONS, 2, C), BF16),
        ),
        grid_spec=pltpu.PrefetchScalarGridSpec(
            num_scalar_prefetch=1,
            grid=(1,),
            in_specs=[
                pl.BlockSpec((GROUP, ROWS, 128), lambda i, h: (0, 0, 0)),
                pl.BlockSpec((6 * 48, 3 * WIN), lambda i, h: (0, 0)),
            ]
            + [pl.BlockSpec(memory_space=pl.ANY) for _ in kept],
            out_specs=(
                pl.BlockSpec((2, 6, 1, LONS), lambda i, h: (0, h[0], 0, 0)),
                pl.BlockSpec((6, LONS, 2, C), lambda i, h: (h[0], 0, 0, 0)),
            ),
            scratch_shapes=[pltpu.VMEM((GROUP, WIN, 256), BF16)],
        ),
        input_output_aliases={3: 0, 4: 1} if kept else {},
        compiler_params=pltpu.CompilerParams(vmem_limit_bytes=SMALL_VMEM),
        cost_estimate=pl.CostEstimate(
            flops=1_000_000_000, bytes_accessed=2_500_000, transcendentals=0
        ),
        name="post",
    )(half, blocks, perm, *kept)


def norm_parts(x):
    center = jnp.sum(x, axis=-1, keepdims=True) * (1.0 / C)
    moved = x - center
    spread = jnp.sum(moved * moved, axis=-1, keepdims=True) * (1.0 / C)
    scale = lax.rsqrt(spread + EPS)
    return moved * scale, scale


def norm_back(cotangent, hat, scale):
    mean = jnp.sum(cotangent, axis=-1, keepdims=True) * (1.0 / C)
    along = jnp.sum(cotangent * hat, axis=-1, keepdims=True) * (1.0 / C)
    return scale * (cotangent - mean - hat * along)


def wide(value):
    return jnp.concatenate([value, value[:, 0:64]], axis=1)


def diagonal_tails(turned):
    lane = lanes((HEAD, 128))
    out = []
    for h in range(HEADS):
        rows = slice(HEAD * h, HEAD * h + HEAD)
        tail = jnp.concatenate([turned[rows, 128:WIN], jnp.zeros((HEAD, 112), F32)], axis=1)
        tail = roll(tail, 16 * h)
        out.append(jnp.where((lane >= 16 * h) & (lane < 16 * h + 16), tail, 0.0))
    return jnp.concatenate(out, axis=0)


def fill_diagonal(ref, turned, tails):
    for h in range(HEADS):
        rows = slice(HEAD * h, HEAD * h + HEAD)
        ref[rows, 128 * h : 128 * h + 128] = turned[rows, 0:128].astype(BF16)
    ref[0:C, 768:WIDE] = tails.astype(BF16)


def per_head(turned, weights):
    main = [
        dot(turned[HEAD * h : HEAD * h + HEAD], weights[:, 128 * h : 128 * h + 128])
        for h in range(HEADS)
    ]
    return jnp.concatenate(main, axis=0), dot(turned, weights[:, 768:WIDE])


def token_rows(main, tails):
    tails = tails.T
    lane = lanes((16, C))
    last = jnp.zeros((16, C), F32)
    for h in range(HEADS):
        mine = (lane >= HEAD * h) & (lane < HEAD * h + HEAD)
        last = jnp.where(mine, tails[16 * h : 16 * h + 16], last)
    return jnp.concatenate([main.T, last], axis=0)


def head_rows(value):
    lane = lanes((WIN, C))
    parts, tails = [], []
    for h in range(HEADS):
        mine = jnp.where((lane >= HEAD * h) & (lane < HEAD * h + HEAD), value, 0.0).astype(BF16)
        parts.append(mine[0:128])
        tails.append(mine[128:WIN])
    return jnp.concatenate(parts + tails + [jnp.zeros((32, C), BF16)], axis=0)


def setup_kernel(
    w_ref, bias_ref, pat_ref, attn_gain_ref, mlp_gain_ref, temp_head_ref,
    wt_ref, w3_ref, bias_out_ref, pat_q_ref, pat_k_ref, gains_ref,
):
    whole = w_ref[...].astype(F32)
    wt_ref[...] = whole.T.astype(BF16)
    for k in range(3):
        piece = whole[:, C * k : C * k + C]
        piece = jnp.concatenate([piece, jnp.zeros((C, 64), F32)], axis=1)
        w3_ref[k] = piece.astype(BF16)
    lane = lanes((WIN, 128))
    tails = jnp.zeros((WIN, 128), F32)
    for h in range(HEADS):
        turned = bias_ref[h].T
        bias_out_ref[:, 128 * h : 128 * h + 128] = turned[:, 0:128]
        tail = jnp.concatenate([turned[:, 128:WIN], jnp.zeros((WIN, 112), F32)], axis=1)
        tail = roll(tail, 16 * h)
        tails = jnp.where((lane >= 16 * h) & (lane < 16 * h + 16), tail, tails)
    bias_out_ref[:, 768:WIDE] = tails
    pat = pat_ref[...].astype(F32)
    for h in range(HEADS):
        pat_q_ref[:, 128 * h : 128 * h + 128] = pat[:, 0:128]
    tail = jnp.concatenate([pat[:, 128:WIN], jnp.zeros((8, 112), F32)], axis=1)
    tails = tail
    for h in range(1, 8):
        tails = tails + roll(tail, 16 * h)
    pat_q_ref[:, 768:WIDE] = tails
    pat_k_ref[...] = jnp.concatenate([pat, jnp.zeros((120, WIN), F32)], axis=0).T
    gains_ref[...] = jnp.zeros((8, 256), F32)
    gains_ref[0:1, 0:C] = attn_gain_ref[...]
    gains_ref[1:2, 0:C] = mlp_gain_ref[...]
    gains_ref[2:3, 0:C] = temp_head_ref[...].astype(F32)


def setup(w_qkv, window_bias, patterns, attn_gain, mlp_gain, temp_head):
    return pl.pallas_call(
        setup_kernel,
        out_shape=(
            jax.ShapeDtypeStruct((3 * C, C), BF16),
            jax.ShapeDtypeStruct((3, C, 256), BF16),
            jax.ShapeDtypeStruct((WIN, WIDE), F32),
            jax.ShapeDtypeStruct((8, WIDE), F32),
            jax.ShapeDtypeStruct((WIN, 128), F32),
            jax.ShapeDtypeStruct((8, 256), F32),
        ),
        in_specs=[vmem()] * 6,
        out_specs=(vmem(),) * 6,
        compiler_params=pltpu.CompilerParams(vmem_limit_bytes=VMEM_ALL),
        cost_estimate=pl.CostEstimate(
            flops=1_000_000_000, bytes_accessed=3_000_000, transcendentals=0
        ),
        name="setup",
    )(w_qkv, window_bias, patterns, attn_gain[None], mlp_gain[None], temp_head[None])


LOG2E = 1.4426950408889634


def interleave(runs, lag):
    live = list(runs)
    ahead = 0
    while live:
        for k, run in enumerate(list(live)):
            if run is runs[-1] and len(runs) > 1 and ahead < lag and runs[0] in live:
                continue
            try:
                next(run)
            except StopIteration:
                live.remove(run)
        ahead += 1


PER_COLUMN = (
    ((4, WIN, 256), F32),
    ((208, WIDE), BF16),
    ((208, WIDE), BF16),
    ((4, WIN, WIDE), BF16),
    ((4, WIN, WIDE), BF16),
    ((4, WIN, C), BF16),
    ((4, WIN, C), BF16),
    ((4, WIN, C), F32),
    ((4, WIN, C), F32),
    ((4, WIN, C), F32),
    ((4, WIN, 128), F32),
    ((4, WIN, 128), F32),
    ((4, WIN, 128), F32),
    ((4, WIN, 256), F32),
    ((4, WIN, 128), F32),
    ((4, WIN, 256), BF16),
)


def main_kernel(
    x_ref, order_ref, back_ref, wt_ref, w_ref, bias_ref, pat_q_ref, pat_k_ref, gains_ref,
    proj_ref, expand_ref, reduce_ref,
    out_ref, tok_in, levels_ref, *scratch,
):
    columns = (scratch[: len(PER_COLUMN)], scratch[len(PER_COLUMN) :])
    scale_q = 1.0 / HEAD**0.5
    lane72 = lanes((HALF, 128))
    lane16 = lanes((16, 128))
    row16 = lax.broadcasted_iota(jnp.int32, (16, 128), 0)
    for s in range(GROUP):
        first, second, extra = unpack_block(x_ref[s])
        tok_in[s, :, 0:128] = first
        tok_in[s, 0:HALF, 128:256] = second[0]
        tok_in[s, HALF:WIN, 128:256] = second[1]
        if s < 4:
            whole = (extra + roll(extra, -3)) + roll(extra, -6)
            levels_ref[s] = jnp.where(lane16 < 75, whole, extra)
    for col in range(2):
        for ref in columns[col][1:3]:
            ref[...] = jnp.zeros(ref.shape, BF16)

    def place(p, part):
        a, beta = part // 2, part % 2
        return beta * 4 + (p + a) % 4, (HALF if a == 0 else 0)

    pick_row = lax.broadcasted_iota(jnp.int32, (128, 256), 0)
    pick_lane = lanes((128, 256))
    pick = jnp.where(
        pick_lane < 128,
        jnp.where((pick_row >= 64) & (pick_row < 67), 1.0, 0.0),
        jnp.where((pick_row >= 67) & (pick_row < 70), 1.0, 0.0),
    ).astype(BF16)
    for p in range(4):
        for a in range(2):
            pieces = []
            for beta in range(2):
                s, at = place(p, 2 * a + beta)
                pieces.append(tok_in[s, at : at + HALF, :])
            moved = dot(order_ref[...], jnp.concatenate(pieces, axis=0).astype(BF16))
            fields = dot(moved[:, 128:256].astype(BF16), pick)
            for col in range(2):
                rows = slice(HALF * a, HALF * a + HALF)
                columns[col][0][p, rows, :] = moved[HALF * col : HALF * col + HALF]
                columns[col][13][p, rows, :] = fields[HALF * col : HALF * col + HALF]

    gain_one = gains_ref[0:1, 0:C]
    gain_two = gains_ref[1:2, 0:C]
    head_row = gains_ref[2:3, 0:C]
    head_eight = jnp.broadcast_to(head_row, (8, C)).astype(BF16)
    u_row = dot(head_eight, reduce_ref[...])[0:1]

    def forward(p, col):
        (tok, diag_q, diag_n, probs, dscores, q_rows, n_rows, dq_rows, resid, hats, scales,
         deltas, _, _, _, _) = columns[col]
        x = tok[p, :, 0:C]
        hat, scale = norm_parts(x)
        normed = (hat * gain_one).astype(BF16)
        hats[p] = hat
        scales[p] = jnp.broadcast_to(scale, (WIN, 128))
        spot = (row16 == 2 + p) & (lane16 == 81 + col)
        ident = jnp.sum(jnp.where(spot, levels_ref[0], 0.0), axis=0, keepdims=True)
        ident = jnp.sum(ident, axis=1, keepdims=True)
        row8 = lax.broadcasted_iota(jnp.int32, (8, 1), 0).astype(F32)
        label_q = jnp.sum(jnp.where(row8 == ident, pat_q_ref[...], 0.0), axis=0, keepdims=True)
        lane_row = lanes((1, 128)).astype(F32)
        label_k = jnp.sum(
            jnp.where(lane_row == ident, pat_k_ref[...], 0.0), axis=1, keepdims=True
        )
        yield
        turned = dot_nt(wt_ref[...], normed)
        q_turned = turned[0:C] * (scale_q * LOG2E)
        fill_diagonal(diag_q, q_turned, diagonal_tails(q_turned))
        apart = jnp.where(row8 == label_q, 0.0, -1e30)
        diag_q[C : C + 16, :] = jnp.concatenate(
            [apart, jnp.zeros((8, WIDE), F32)], axis=0
        ).astype(BF16)
        keys_t = turned[C : 2 * C].astype(BF16)
        values_t = turned[2 * C : 3 * C].astype(BF16)
        yield
        q_rows[p] = (dot(normed, w_ref[0])[:, 0:C] * scale_q).astype(BF16)
        keys = dot(normed, w_ref[1])
        marks = jnp.where(lanes((WIN, 128)).astype(F32) == label_k + 64.0, 1.0, keys[:, 128:256])
        keys = jnp.concatenate([keys[:, 0:128], marks], axis=1)[:, 0:208].astype(BF16)
        values = dot(normed, w_ref[2])
        lane_wide = lanes((1, 256))
        ones = jnp.where((lane_wide == C) | (lane_wide == C + 1), 1.0, 0.0)
        values = (values + ones)[:, 0:208].astype(BF16)
        yield
        scores = dot(keys, diag_q[...]) + bias_ref[...] * LOG2E
        yield
        raised = jnp.exp2(scores - jnp.max(scores, axis=0, keepdims=True))
        weights = (raised * (1.0 / jnp.sum(raised, axis=0, keepdims=True))).astype(BF16)
        probs[p] = weights
        yield
        main, tails = per_head(values_t, weights)
        context = token_rows(main, tails).astype(BF16)
        yield
        middle = (x + dot(context, proj_ref[...])).astype(BF16).astype(F32)
        hat_two, scale_two = norm_parts(middle)
        normed_two = (hat_two * gain_two).astype(BF16)
        yield
        acc = jnp.zeros((WIN, 256), F32)
        back = jnp.zeros((WIN, C), F32)
        c0 = 0.7978845608028654
        c1 = c0 * 0.044715
        for f in range(3):
            at = slice(256 * f, 256 * f + 256)
            pre = dot(normed_two, expand_ref[:, at])
            u = u_row[:, at]
            square = pre * pre
            gate = 0.5 + 0.5 * jnp.tanh(pre * (c0 + c1 * square))
            unit = pre * gate
            acc = acc + unit * u
            slope = gate * (1.0 + (pre - unit) * (2.0 * c0 + (6.0 * c1) * square))
            back = back + dot_nt((slope * u).astype(BF16), expand_ref[:, at])
            yield
        delta = jnp.sum(acc, axis=1, keepdims=True) + jnp.sum(
            middle * head_row, axis=1, keepdims=True
        )
        deltas[p] = jnp.broadcast_to(delta, (WIN, 128))
        kept = head_row + norm_back(back * gain_two, hat_two, scale_two)
        resid[p] = kept
        kept = kept.astype(BF16)
        yield
        n_turned = dot_nt(proj_ref[...], kept)
        n_tails = diagonal_tails(n_turned)
        fill_diagonal(diag_n, n_turned, n_tails)
        product = n_turned[:, 0:128] * main
        inner = [
            jnp.sum(product[HEAD * h : HEAD * h + HEAD], axis=0, keepdims=True)
            for h in range(HEADS)
        ]
        inner.append(jnp.sum(n_tails * tails, axis=0, keepdims=True))
        inner = jnp.concatenate(inner, axis=1)
        top = inner.astype(BF16).astype(F32)
        diag_n[C : C + 16, :] = jnp.concatenate(
            [-top, top - inner, jnp.zeros((14, WIDE), F32)], axis=0
        ).astype(BF16)
        n_rows[p] = dot_nt(kept, proj_ref[...]).astype(BF16)
        yield
        dweights = dot(values, diag_n[...])
        dscore = (probs[p].astype(F32) * dweights).astype(BF16)
        dscores[p] = dscore
        yield
        main, tails = per_head(keys_t, dscore)
        dq_rows[p] = token_rows(main, tails)

    def forward_step(p, carry):
        interleave([forward(p, 0), forward(p, 1)], LAG)
        return carry

    lax.fori_loop(0, 4, forward_step, 0)

    def scalar(l, k):
        return levels_ref[l // 2, l % 2 : l % 2 + 1, 72 + k : 73 + k]

    for col in range(2):
        deltas, source, fields, heights = (columns[col][k] for k in (11, 12, 13, 14))
        total = jnp.zeros((HALF, 128), F32)
        misfits, spots = [], []
        for l in range(8):
            a = 1 - l % 2
            p = (l // 2 - a) % 4
            rows = slice(HALF * a, HALF * a + HALF)
            spots.append((p, rows))
            temps = scalar(l, 2) + deltas[p, rows, :]
            total = total + scalar(l, 0) * temps
            height = fields[p, rows, 128:256] + total
            misfits.append(scalar(l, 1) * (height - fields[p, rows, 0:128]))
            top, middle, low = split3(height)
            heights[p, rows, :] = jnp.where(
                lane72 == 64, top, jnp.where(lane72 == 65, middle, low)
            )
        carried = jnp.zeros((HALF, 128), F32)
        for l in reversed(range(8)):
            p, rows = spots[l]
            carried = carried + misfits[l]
            source[p, rows, :] = scalar(l, 0) * carried

    def backward(p, col):
        (_, _, _, probs, dscores, q_rows, n_rows, dq_rows, resid, hats, scales,
         _, source, _, heights, made) = columns[col]
        s = wide(source[p])
        dk = dot(dscores[p], head_rows(s * q_rows[p].astype(F32))).astype(BF16)
        yield
        dv = dot(probs[p], head_rows(s * n_rows[p].astype(F32))).astype(BF16)
        yield
        dq = ((s * scale_q) * dq_rows[p]).astype(BF16)
        dnormed = (
            dot(dq, wt_ref[0:C, :]) + dot(dk, wt_ref[C : 2 * C, :]) + dot(dv, wt_ref[2 * C :, :])
        )
        yield
        dx = norm_back(dnormed * gain_one, hats[p], wide(scales[p]))
        grad = s * resid[p] + dx
        lane = lanes((WIN, 128))
        last = jnp.concatenate([grad[:, 128:C], jnp.zeros((WIN, 64), F32)], axis=1)
        last = jnp.where(lane < 64, last, jnp.where(lane < 67, heights[p], 0.0))
        made[p, :, 0:128] = grad[:, 0:128].astype(BF16)
        made[p, :, 128:256] = last.astype(BF16)

    def backward_step(p, carry):
        interleave([backward(p, 0), backward(p, 1)], 0)
        return carry

    lax.fori_loop(0, 4, backward_step, 0)

    for p in range(4):
        for a in range(2):
            rows = slice(HALF * a, HALF * a + HALF)
            pair = [columns[col][15][p].astype(F32)[rows] for col in range(2)]
            moved = dot(back_ref[...], jnp.concatenate(pair, axis=0).astype(BF16))
            for beta in range(2):
                s, at = place(p, 2 * a + beta)
                tok_in[s, at : at + HALF, :] = moved[HALF * beta : HALF * beta + HALF]
    zero = jnp.zeros((16, 128), F32)
    for s in range(GROUP):
        pack_block(out_ref, s, tok_in[s], zero)


LAG = 0


def layer(x, consts):
    return pl.pallas_call(
        main_kernel,
        out_shape=jax.ShapeDtypeStruct((GROUP, ROWS, 128), BF16),
        in_specs=[vmem()] * (1 + len(consts)),
        out_specs=vmem(),
        scratch_shapes=[
            pltpu.VMEM((GROUP, WIN, 256), F32),
            pltpu.VMEM((4, 16, 128), F32),
        ]
        + [pltpu.VMEM(shape, kind) for shape, kind in PER_COLUMN] * 2,
        compiler_params=pltpu.CompilerParams(vmem_limit_bytes=VMEM_LIMIT),
        cost_estimate=pl.CostEstimate(
            flops=20_000_000_000, bytes_accessed=4_000_000, transcendentals=3_000_000
        ),
        name="layer",
    )(x, *consts)


def pair_groups(odd):
    out = []
    for block in range(BLOCKS):
        for band in range(odd, BANDS, 2):
            members = (band, (band + 1) % BANDS)
            out.append(
                [(b * BLOCKS + block) * LEVS + lev for b in members for lev in range(LEVS)]
            )
    return out


def exchange(blocks, odd):
    return lax.all_to_all(
        blocks, ("tile", "lev"), 0, 0, axis_index_groups=pair_groups(odd)
    )


def block_step(value, steps):
    pairs = [
        (t, t - t % BLOCKS + (t + steps) % BLOCKS) for t in range(BANDS * BLOCKS)
    ]
    return lax.ppermute(value, "tile", pairs)


def on_device(
    features, attn_gain, w_qkv, w_proj, window_bias, patterns, window_pattern, mlp_gain,
    w_expand, w_reduce, temp_head, temp_base, thickness, level_weight, surface, target,
):
    feats = features[:, 0].transpose(1, 2, 0, 3)
    goal = target.transpose(0, 2, 1, 3)
    ground = surface.transpose(1, 0, 2)
    after, before = rim(window_pattern, feats, goal, ground)
    after = block_step(after, -1)
    before = block_step(before, 1)

    band = lax.axis_index("tile") // BLOCKS
    even = (band % 2 == 0).astype(jnp.int32)
    halves = [even.reshape(1), (1 - even).reshape(1)]
    perm = jnp.asarray(source_rows(), BF16)
    perm_back = jnp.asarray(target_rows(), BF16)
    order = jnp.asarray(window_rows(), BF16)
    order_back = jnp.asarray(window_rows().T, BF16)

    made = [
        prep(
            half, window_pattern, thickness, level_weight, temp_base,
            feats, after, before, goal, ground, perm,
        )
        for half in halves
    ]
    weights = (w_qkv, window_bias, patterns, attn_gain, mlp_gain, temp_head)
    weights, made[0] = lax.optimization_barrier((weights, made[0]))
    consts = (order, order_back) + tuple(setup(*weights)) + (w_proj, w_expand, w_reduce.T)
    done = None
    for odd in range(2):
        got = exchange(made[odd], odd)
        done = post(halves[odd], exchange(layer(got, consts), odd), perm_back, done)
    height, grad = done
    return height.transpose(0, 2, 1, 3), grad.transpose(2, 0, 1, 3)[:, None]


def solution(mesh):
    placed = (
        P("lev", "tile", None, None, None),
        P(), P(), P(), P(), P(),
        P(None, "tile"),
        P(), P(), P(), P(),
        P("lev"), P("lev"), P("lev"),
        P("tile", None, None),
        P("lev", "tile", None, None),
    )
    return jax.shard_map(
        on_device,
        mesh=mesh,
        in_specs=placed,
        out_specs=(P("lev", "tile", None, None), P("lev", "tile", None, None, None)),
        check_vma=False,
    )
```

```python
import jax
import jax.numpy as jnp
import numpy as np
from jax import lax
from jax.experimental import pallas as pl
from jax.experimental.pallas import tpu as pltpu
from jax.sharding import PartitionSpec as P

F32 = jnp.float32
BF16 = jnp.bfloat16
C = 192
HEADS = 6
HEAD = 32
FF = 768
WIN = 144
HALF = 72
QUARTER = 36
LONS = 90
SHIFT = 3
BLOCKS = 4
BANDS = 16
LEVS = 4
GROUP = 8
ROWS = 240
WIDE = 896
EPS = 1e-05
VMEM_LIMIT = 28 * 1024 * 1024
SMALL_VMEM = 12 * 1024 * 1024
VMEM_ALL = 60 * 1024 * 1024


def source_rows():
    table = np.zeros((2 * WIN, 6 * 64), np.float32)
    for q in range(2):
        for lev in range(2):
            for col in range(2):
                for i in range(QUARTER):
                    r, o = i // 6, i % 6
                    place = 2 * (12 * q + 6 * col + o + SHIFT) + lev
                    table[((q * 2 + lev) * 2 + col) * QUARTER + i, 64 * r + place] = 1.0
    return table


def target_rows():
    table = np.zeros((6 * 48, 3 * WIN), np.float32)
    for r in range(6):
        for x in range(48):
            e, lev = x // 2 + 9, x % 2
            d, col, o = e // 12, e % 12 // 6, e % 6
            table[48 * r + x, d * WIN + lev * HALF + col * QUARTER + 6 * r + o] = 1.0
    return table


def window_rows():
    table = np.zeros((WIN, WIN), np.float32)
    for col in range(2):
        for beta in range(2):
            for i in range(QUARTER):
                table[(col * 2 + beta) * QUARTER + i, (beta * 2 + col) * QUARTER + i] = 1.0
    return table


def dot(a, b):
    return jnp.dot(a, b, preferred_element_type=F32)


def dot_nt(a, b):
    return lax.dot_general(a, b, (((1,), (1,)), ((), ())), preferred_element_type=F32)


def lanes(shape):
    return lax.broadcasted_iota(jnp.int32, shape, len(shape) - 1)


def split3(value):
    top = value.astype(BF16).astype(F32)
    rest = value - top
    middle = rest.astype(BF16).astype(F32)
    return top, middle, rest - middle


def roll(value, steps):
    return pltpu.roll(value, steps % 128, 1)


def pack_block(out_ref, at, made, spare):
    lane = lanes((HALF, 128))
    out_ref[at, 0:WIN, :] = made[:, 0:128].astype(BF16)
    both = made[:, 128:256]
    tail = jnp.where(lane < 64, both[0:HALF], roll(both[HALF:WIN], 64))
    tail = jnp.concatenate([tail, jnp.zeros((8, 128), F32)], axis=0)
    lane16 = lanes((16, 128))
    extra = spare
    for g in range(9):
        moved = roll(both[16 * g : 16 * g + 16], 8 * g - 64)
        extra = jnp.where((lane16 >= 8 * g) & (lane16 < 8 * g + 8), moved, extra)
    out_ref[at, WIN : WIN + 16, :] = extra.astype(BF16)
    out_ref[at, WIN + 16 : ROWS, :] = tail.astype(BF16)


def unpack_block(block):
    first = block[0:WIN].astype(F32)
    extra = block[WIN : WIN + 16].astype(F32)
    tail = block[WIN + 16 : ROWS].astype(F32)[0:HALF]
    lane16 = lanes((16, 128))
    keep = (lane16 >= 64) & (lane16 < 72)
    spread = [jnp.where(keep, roll(extra, 64 - 8 * g), 0.0) for g in range(9)]
    spread = jnp.concatenate(spread, axis=0)
    lane = lanes((HALF, 128))
    second = [
        jnp.where(lane < 64, tail, spread[0:HALF]),
        jnp.where(lane < 64, roll(tail, 64), spread[HALF:WIN]),
    ]
    return first, second, extra


def vmem():
    return pl.BlockSpec(memory_space=pltpu.VMEM)


def smem():
    return pl.BlockSpec(memory_space=pltpu.SMEM)


def field_rows(targets, ground, count, padded):
    blank = jnp.zeros((count, 128 - LONS), F32)
    goal = [jnp.concatenate([t, blank], axis=1) for t in targets]
    ground = jnp.concatenate([ground, blank], axis=1)
    parts = split3(jnp.concatenate(goal, axis=1)) + split3(
        jnp.concatenate([ground, ground], axis=1)
    )
    if padded > count:
        more = jnp.zeros((padded - count, 256), F32)
        parts = [jnp.concatenate([v, more], axis=0) for v in parts]
    stacked = jnp.concatenate(parts, axis=0).astype(BF16)
    i = lax.broadcasted_iota(jnp.int32, (128, 6 * padded), 0)
    j = lanes((128, 6 * padded))
    hit = (j == padded * (i & 7) + (i >> 3)) & ((i & 7) < 6) & ((i >> 3) < count)
    return dot(jnp.where(hit, 1.0, 0.0).astype(BF16), stacked).astype(BF16)


def lon_pick(rows, first):
    x = lax.broadcasted_iota(jnp.int32, (rows, 256), 0)
    y = lanes((rows, 256))
    return jnp.where(y == 128 * (x & 1) + (x >> 1) + first, 1.0, 0.0).astype(BF16)


def rim_kernel(ids_ref, fa_ref, fb_ref, target_ref, surface_ref, next_ref, prev_ref):
    targets = [
        jnp.concatenate([target_ref[lev, r] for r in range(12)], axis=0) for lev in range(2)
    ]
    ground = jnp.concatenate([surface_ref[r] for r in range(12)], axis=0)
    fields = field_rows(targets, ground, 12, 16)
    spots = jnp.concatenate([lon_pick(8, 0), lon_pick(8, 86)], axis=0)
    values = dot_nt(spots, fields)
    lane = lanes((8, 128))
    idents = jnp.zeros((8, 128), F32)
    for p in range(4):
        idents = jnp.where(lane == 72 + p, ids_ref[p, 14].astype(F32), idents)
    for out_ref, f_ref, at, row, more in (
        (next_ref, fa_ref, 0, 0, 0.0), (prev_ref, fb_ref, 12, 8, idents)
    ):
        made = []
        for r in range(12):
            tokens = f_ref[r].reshape(20, C).astype(F32)[at : at + 8]
            second = jnp.concatenate([tokens[:, 128:C], jnp.zeros((8, 64), F32)], axis=1)
            extra = roll(values, 64 - 8 * r)[row : row + 8]
            second = jnp.where(lane < 64, second, jnp.where(lane < 72, extra, more))
            made.append(jnp.concatenate([tokens[:, 0:128], second], axis=1))
        out_ref[...] = jnp.concatenate(made, axis=0).astype(BF16)


def rim(ids, feats, target, surface):
    edge = jax.ShapeDtypeStruct((96, 256), BF16)
    return pl.pallas_call(
        rim_kernel,
        out_shape=(edge, edge),
        grid=(1,),
        in_specs=[
            smem(),
            pl.BlockSpec((12, 10, 2, C), lambda i: (0, 0, 0, 0)),
            pl.BlockSpec((12, 10, 2, C), lambda i: (0, 8, 0, 0)),
            pl.BlockSpec((2, 12, 1, LONS), lambda i: (0, 0, 0, 0)),
            pl.BlockSpec((12, 1, LONS), lambda i: (0, 0, 0)),
        ],
        out_specs=(
            pl.BlockSpec((96, 256), lambda i: (0, 0)),
            pl.BlockSpec((96, 256), lambda i: (0, 0)),
        ),
        compiler_params=pltpu.CompilerParams(vmem_limit_bytes=VMEM_ALL),
        name="rim",
    )(ids, feats, feats, target, surface)


def prep_kernel(
    half_ref, ids_ref, thick_ref, weight_ref, base_ref,
    f_ref, next_ref, prev_ref, target_ref, surface_ref, perm_ref,
    out_ref, rows_ref,
):
    targets = [
        jnp.concatenate([target_ref[lev, r] for r in range(6)], axis=0) for lev in range(2)
    ]
    ground = jnp.concatenate([surface_ref[r] for r in range(6)], axis=0)
    values = dot_nt(lon_pick(2 * LONS, 0), field_rows(targets, ground, 6, 8))
    after = next_ref[...].astype(F32)
    before = prev_ref[...].astype(F32)
    lane = lanes((2 * LONS, 128))
    for r in range(6):
        tokens = f_ref[r].reshape(2 * LONS, C).astype(F32)
        second = jnp.concatenate([tokens[:, 128:C], jnp.zeros((2 * LONS, 64), F32)], axis=1)
        extra = jnp.where(lane < 72, roll(values, 64 - 8 * r), 0.0)
        second = jnp.where(lane < 64, second, extra)
        for at, part in ((0, tokens[:, 0:128]), (128, second)):
            cut = slice(at, at + 128)
            rows_ref[208 * r : 208 * r + 176, cut] = part[0:176].astype(BF16)
            tail = [
                part[176:180],
                after[8 * r : 8 * r + 6, cut],
                before[8 * r + 2 : 8 * r + 8, cut],
                part[0:6],
                jnp.zeros((10, 128), F32),
            ]
            tail = jnp.concatenate(tail, axis=0).astype(BF16)
            rows_ref[208 * r + 176 : 208 * r + 208, cut] = tail
    lane16 = lanes((16, 128))
    row16 = lax.broadcasted_iota(jnp.int32, (16, 128), 0)
    scalars = jnp.zeros((16, 128), F32)
    for lev in range(2):
        for k, ref in enumerate((thick_ref, weight_ref, base_ref)):
            scalars = jnp.where((row16 == lev) & (lane16 == 72 + k), ref[lev], scalars)
    top, middle, low = split3(scalars)
    scalars = top + roll(middle, 3) + roll(low, 6)
    for m in range(4):
        source = [rows_ref[208 * r + 48 * m : 208 * r + 48 * m + 64, :] for r in range(6)]
        made = dot(perm_ref[...], jnp.concatenate(source, axis=0))
        for q in range(2):
            d = 2 * m + q
            spare = scalars
            for p in range(4):
                for col in range(2):
                    if 2 * d + col < 15:
                        ident = ids_ref[p, 2 * d + col].astype(F32)
                    else:
                        ident = before[0:1, 200 + p : 201 + p]
                    spare = jnp.where((row16 == 2 + p) & (lane16 == 81 + col), ident, spare)
            pack_block(out_ref, d, made[WIN * q : WIN * q + WIN], spare)


def prep(half, ids, thick, weight, base, feats, after, before, target, surface, perm):
    return pl.pallas_call(
        prep_kernel,
        out_shape=jax.ShapeDtypeStruct((GROUP, ROWS, 128), BF16),
        grid_spec=pltpu.PrefetchScalarGridSpec(
            num_scalar_prefetch=1,
            grid=(1,),
            in_specs=[smem()] * 4
            + [
                pl.BlockSpec((6, LONS, 2, C), lambda i, h: (h[0], 0, 0, 0)),
                pl.BlockSpec((48, 256), lambda i, h: (h[0], 0)),
                pl.BlockSpec((48, 256), lambda i, h: (h[0], 0)),
                pl.BlockSpec((2, 6, 1, LONS), lambda i, h: (0, h[0], 0, 0)),
                pl.BlockSpec((6, 1, LONS), lambda i, h: (h[0], 0, 0)),
                pl.BlockSpec((2 * WIN, 384), lambda i, h: (0, 0)),
            ],
            out_specs=pl.BlockSpec((GROUP, ROWS, 128), lambda i, h: (0, 0, 0)),
            scratch_shapes=[pltpu.VMEM((6 * 208, 256), BF16)],
        ),
        compiler_params=pltpu.CompilerParams(vmem_limit_bytes=SMALL_VMEM),
        cost_estimate=pl.CostEstimate(
            flops=1_000_000_000, bytes_accessed=2_500_000, transcendentals=0
        ),
        name="prep",
    )(half, ids, thick, weight, base, feats, after, before, target, surface, perm)


def post_kernel(half_ref, x_ref, perm_ref, *refs):
    height_ref, grad_ref, rows_ref = refs[-3:]
    for d in range(GROUP):
        first, second, _ = unpack_block(x_ref[d])
        rows_ref[d, :, 0:128] = first.astype(BF16)
        rows_ref[d, :, 128:256] = jnp.concatenate(second, axis=0).astype(BF16)
    lane = lanes((48, 128))
    columns = []
    for m in range(4):
        source = [rows_ref[(2 * m + k) % GROUP] for k in (-1, 0, 1)]
        made = dot(perm_ref[...], jnp.concatenate(source, axis=0))
        count = 24 if m < 3 else 18
        column = jnp.zeros((48, 128), F32)
        for r in range(6):
            tokens = made[48 * r : 48 * r + 2 * count, 0:C].astype(BF16)
            grad_ref[r, 24 * m : 24 * m + count] = tokens.reshape(count, 2, C)
            moved = roll(made[48 * r : 48 * r + 48, 128:256], 8 * r - 64)
            column = jnp.where((lane >= 8 * r) & (lane < 8 * r + 3), moved, column)
        columns.append(column)
    columns = jnp.concatenate(columns, axis=0).astype(BF16)
    rows = lax.dot_general(
        columns, lon_pick(192, 0), (((0,), (0,)), ((), ())), preferred_element_type=F32
    )
    for r in range(6):
        row = rows[8 * r : 8 * r + 1] + rows[8 * r + 1 : 8 * r + 2] + rows[8 * r + 2 : 8 * r + 3]
        for lev in range(2):
            height_ref[lev, r] = row[:, 128 * lev : 128 * lev + LONS]


def post(half, blocks, perm, earlier):
    kept = [] if earlier is None else list(earlier)
    return pl.pallas_call(
        post_kernel,
        out_shape=(
            jax.ShapeDtypeStruct((2, 12, 1, LONS), F32),
            jax.ShapeDtypeStruct((12, LONS, 2, C), BF16),
        ),
        grid_spec=pltpu.PrefetchScalarGridSpec(
            num_scalar_prefetch=1,
            grid=(1,),
            in_specs=[
                pl.BlockSpec((GROUP, ROWS, 128), lambda i, h: (0, 0, 0)),
                pl.BlockSpec((6 * 48, 3 * WIN), lambda i, h: (0, 0)),
            ]
            + [pl.BlockSpec(memory_space=pl.ANY) for _ in kept],
            out_specs=(
                pl.BlockSpec((2, 6, 1, LONS), lambda i, h: (0, h[0], 0, 0)),
                pl.BlockSpec((6, LONS, 2, C), lambda i, h: (h[0], 0, 0, 0)),
            ),
            scratch_shapes=[pltpu.VMEM((GROUP, WIN, 256), BF16)],
        ),
        input_output_aliases={3: 0, 4: 1} if kept else {},
        compiler_params=pltpu.CompilerParams(vmem_limit_bytes=SMALL_VMEM),
        cost_estimate=pl.CostEstimate(
            flops=1_000_000_000, bytes_accessed=2_500_000, transcendentals=0
        ),
        name="post",
    )(half, blocks, perm, *kept)


def norm_parts(x):
    center = jnp.sum(x, axis=-1, keepdims=True) * (1.0 / C)
    moved = x - center
    spread = jnp.sum(moved * moved, axis=-1, keepdims=True) * (1.0 / C)
    scale = lax.rsqrt(spread + EPS)
    return moved * scale, scale


def norm_back(cotangent, hat, scale):
    mean = jnp.sum(cotangent, axis=-1, keepdims=True) * (1.0 / C)
    along = jnp.sum(cotangent * hat, axis=-1, keepdims=True) * (1.0 / C)
    return scale * (cotangent - mean - hat * along)


def wide(value):
    return jnp.concatenate([value, value[:, 0:64]], axis=1)


def diagonal_tails(turned):
    lane = lanes((HEAD, 128))
    out = []
    for h in range(HEADS):
        rows = slice(HEAD * h, HEAD * h + HEAD)
        tail = jnp.concatenate([turned[rows, 128:WIN], jnp.zeros((HEAD, 112), F32)], axis=1)
        tail = roll(tail, 16 * h)
        out.append(jnp.where((lane >= 16 * h) & (lane < 16 * h + 16), tail, 0.0))
    return jnp.concatenate(out, axis=0)


def fill_diagonal(ref, turned, tails):
    for h in range(HEADS):
        rows = slice(HEAD * h, HEAD * h + HEAD)
        ref[rows, 128 * h : 128 * h + 128] = turned[rows, 0:128].astype(BF16)
    ref[0:C, 768:WIDE] = tails.astype(BF16)


def per_head(turned, weights):
    main = [
        dot(turned[HEAD * h : HEAD * h + HEAD], weights[:, 128 * h : 128 * h + 128])
        for h in range(HEADS)
    ]
    return jnp.concatenate(main, axis=0), dot(turned, weights[:, 768:WIDE])


def token_rows(main, tails):
    tails = tails.astype(BF16).T
    lane = lanes((16, C))
    last = jnp.zeros((16, C), BF16)
    for h in range(HEADS):
        mine = (lane >= HEAD * h) & (lane < HEAD * h + HEAD)
        last = jnp.where(mine, tails[16 * h : 16 * h + 16], last)
    return jnp.concatenate([main.astype(BF16).T, last], axis=0)


def head_rows(value):
    lane = lanes((WIN, C))
    parts, tails = [], []
    for h in range(HEADS):
        mine = jnp.where((lane >= HEAD * h) & (lane < HEAD * h + HEAD), value, 0.0).astype(BF16)
        parts.append(mine[0:128])
        tails.append(mine[128:WIN])
    return jnp.concatenate(parts + tails + [jnp.zeros((32, C), BF16)], axis=0)


def setup_kernel(
    w_ref, bias_ref, pat_ref, attn_gain_ref, mlp_gain_ref, temp_head_ref,
    wt_ref, w3_ref, bias_out_ref, pat_q_ref, pat_k_ref, gains_ref,
):
    whole = w_ref[...].astype(F32)
    wt_ref[...] = whole.T.astype(BF16)
    for k in range(3):
        piece = whole[:, C * k : C * k + C]
        piece = jnp.concatenate([piece, jnp.zeros((C, 64), F32)], axis=1)
        w3_ref[k] = piece.astype(BF16)
    lane = lanes((WIN, 128))
    tails = jnp.zeros((WIN, 128), F32)
    for h in range(HEADS):
        turned = bias_ref[h].T
        bias_out_ref[:, 128 * h : 128 * h + 128] = turned[:, 0:128] * LOG2E
        tail = jnp.concatenate([turned[:, 128:WIN], jnp.zeros((WIN, 112), F32)], axis=1)
        tail = roll(tail, 16 * h)
        tails = jnp.where((lane >= 16 * h) & (lane < 16 * h + 16), tail, tails)
    bias_out_ref[:, 768:WIDE] = tails * LOG2E
    pat = pat_ref[...].astype(F32)
    for h in range(HEADS):
        pat_q_ref[:, 128 * h : 128 * h + 128] = pat[:, 0:128]
    tail = jnp.concatenate([pat[:, 128:WIN], jnp.zeros((8, 112), F32)], axis=1)
    tails = tail
    for h in range(1, 8):
        tails = tails + roll(tail, 16 * h)
    pat_q_ref[:, 768:WIDE] = tails
    pat_k_ref[...] = jnp.concatenate([pat, jnp.zeros((120, WIN), F32)], axis=0).T
    gains_ref[...] = jnp.zeros((8, 256), F32)
    gains_ref[0:1, 0:C] = attn_gain_ref[...]
    gains_ref[1:2, 0:C] = mlp_gain_ref[...]
    gains_ref[2:3, 0:C] = temp_head_ref[...].astype(F32)


def setup(w_qkv, window_bias, patterns, attn_gain, mlp_gain, temp_head):
    return pl.pallas_call(
        setup_kernel,
        out_shape=(
            jax.ShapeDtypeStruct((3 * C, C), BF16),
            jax.ShapeDtypeStruct((3, C, 256), BF16),
            jax.ShapeDtypeStruct((WIN, WIDE), F32),
            jax.ShapeDtypeStruct((8, WIDE), F32),
            jax.ShapeDtypeStruct((WIN, 128), F32),
            jax.ShapeDtypeStruct((8, 256), F32),
        ),
        in_specs=[vmem()] * 6,
        out_specs=(vmem(),) * 6,
        compiler_params=pltpu.CompilerParams(vmem_limit_bytes=VMEM_ALL),
        cost_estimate=pl.CostEstimate(
            flops=1_000_000_000, bytes_accessed=3_000_000, transcendentals=0
        ),
        name="setup",
    )(w_qkv, window_bias, patterns, attn_gain[None], mlp_gain[None], temp_head[None])


LOG2E = 1.4426950408889634


def interleave(*runs):
    live = list(runs)
    while live:
        for run in list(live):
            try:
                next(run)
            except StopIteration:
                live.remove(run)


PER_COLUMN = (
    ((4, WIN, 256), F32),
    ((208, WIDE), BF16),
    ((208, WIDE), BF16),
    ((4, WIN, WIDE), BF16),
    ((4, WIN, WIDE), BF16),
    ((4, WIN, C), BF16),
    ((4, WIN, C), BF16),
    ((4, C, 256), F32),
    ((4, WIN, C), F32),
    ((4, WIN, C), F32),
    ((4, WIN, 128), F32),
    ((4, WIN, 128), F32),
    ((4, WIN, 128), F32),
    ((4, WIN, 256), F32),
    ((4, WIN, 128), F32),
    ((4, WIN, 256), BF16),
)


def main_kernel(
    x_ref, *refs
):
    given, out_ref, held = refs[:N_CONST], refs[N_CONST], refs[N_CONST + 1 : 2 * N_CONST + 1]
    tok_in, levels_ref, sems, *scratch = refs[2 * N_CONST + 1 :]
    copies = [
        pltpu.make_async_copy(a, b, sems.at[k]) for k, (a, b) in enumerate(zip(given, held))
    ]
    for copy in copies:
        copy.start()
    (order_ref, back_ref, wt_ref, w_ref, bias_ref, pat_q_ref, pat_k_ref, gains_ref, proj_ref,
     expand_ref, reduce_ref) = held
    columns = (scratch[: len(PER_COLUMN)], scratch[len(PER_COLUMN) :])
    scale_q = 1.0 / HEAD**0.5
    lane72 = lanes((HALF, 128))
    lane16 = lanes((16, 128))
    row16 = lax.broadcasted_iota(jnp.int32, (16, 128), 0)
    for s in range(GROUP):
        first, second, extra = unpack_block(x_ref[s])
        tok_in[s, :, 0:128] = first
        tok_in[s, 0:HALF, 128:256] = second[0]
        tok_in[s, HALF:WIN, 128:256] = second[1]
        if s < 4:
            whole = (extra + roll(extra, -3)) + roll(extra, -6)
            levels_ref[s] = jnp.where(lane16 < 75, whole, extra)
    for col in range(2):
        for ref in columns[col][1:3]:
            ref[...] = jnp.zeros(ref.shape, BF16)

    def place(p, part):
        a, beta = part // 2, part % 2
        return beta * 4 + (p + a) % 4, (HALF if a == 0 else 0)

    pick_row = lax.broadcasted_iota(jnp.int32, (128, 256), 0)
    pick_lane = lanes((128, 256))
    pick = jnp.where(
        pick_lane < 128,
        jnp.where((pick_row >= 64) & (pick_row < 67), 1.0, 0.0),
        jnp.where((pick_row >= 67) & (pick_row < 70), 1.0, 0.0),
    ).astype(BF16)
    copies[0].wait()
    for p in range(4):
        for a in range(2):
            pieces = []
            for beta in range(2):
                s, at = place(p, 2 * a + beta)
                pieces.append(tok_in[s, at : at + HALF, :])
            moved = dot(order_ref[...], jnp.concatenate(pieces, axis=0).astype(BF16))
            fields = dot(moved[:, 128:256].astype(BF16), pick)
            for col in range(2):
                rows = slice(HALF * a, HALF * a + HALF)
                columns[col][0][p, rows, :] = moved[HALF * col : HALF * col + HALF]
                columns[col][13][p, rows, :] = fields[HALF * col : HALF * col + HALF]

    for copy in copies[1:]:
        copy.wait()
    gain_one = gains_ref[0:1, 0:C]
    gain_two = gains_ref[1:2, 0:C]
    head_row = gains_ref[2:3, 0:C]
    head_eight = jnp.broadcast_to(head_row, (8, C)).astype(BF16)
    u_row = dot(head_eight, reduce_ref[...])[0:1]

    def forward(p, col):
        (tok, diag_q, diag_n, probs, dscores, q_rows, n_rows, dq_rows, resid, hats, scales,
         deltas, _, _, _, _) = columns[col]
        x = tok[p, :, 0:C]
        hat, scale = norm_parts(x)
        normed = (hat * gain_one).astype(BF16)
        hats[p] = hat
        scales[p] = jnp.broadcast_to(scale, (WIN, 128))
        spot = (row16 == 2 + p) & (lane16 == 81 + col)
        ident = jnp.sum(jnp.where(spot, levels_ref[0], 0.0), axis=0, keepdims=True)
        ident = jnp.sum(ident, axis=1, keepdims=True)
        row8 = lax.broadcasted_iota(jnp.int32, (8, 1), 0).astype(F32)
        label_q = jnp.sum(jnp.where(row8 == ident, pat_q_ref[...], 0.0), axis=0, keepdims=True)
        lane_row = lanes((1, 128)).astype(F32)
        label_k = jnp.sum(
            jnp.where(lane_row == ident, pat_k_ref[...], 0.0), axis=1, keepdims=True
        )
        yield
        turned = dot_nt(wt_ref[...], normed)
        q_turned = turned[0:C] * (scale_q * LOG2E)
        fill_diagonal(diag_q, q_turned, diagonal_tails(q_turned))
        apart = jnp.where(row8 == label_q, 0.0, -1e30)
        diag_q[C : C + 16, :] = jnp.concatenate(
            [apart, jnp.zeros((8, WIDE), F32)], axis=0
        ).astype(BF16)
        keys_t = turned[C : 2 * C].astype(BF16)
        values_t = turned[2 * C : 3 * C].astype(BF16)
        yield
        q_rows[p] = (dot(normed, w_ref[0])[:, 0:C] * scale_q).astype(BF16)
        keys = dot(normed, w_ref[1])
        marks = jnp.where(lanes((WIN, 128)).astype(F32) == label_k + 64.0, 1.0, keys[:, 128:256])
        keys = jnp.concatenate([keys[:, 0:128], marks], axis=1)[:, 0:208].astype(BF16)
        values = dot(normed, w_ref[2])
        lane_wide = lanes((1, 256))
        ones = jnp.where((lane_wide == C) | (lane_wide == C + 1), 1.0, 0.0)
        values = (values + ones)[:, 0:208].astype(BF16)
        yield
        scores = dot(keys, diag_q[...]) + bias_ref[...]
        yield
        raised = jnp.exp2(scores - jnp.max(scores, axis=0, keepdims=True))
        weights = (raised * (1.0 / jnp.sum(raised, axis=0, keepdims=True))).astype(BF16)
        probs[p] = weights
        yield
        main, tails = per_head(values_t, weights)
        context = token_rows(main, tails)
        yield
        middle = (x + dot(context, proj_ref[...])).astype(BF16).astype(F32)
        hat_two, scale_two = norm_parts(middle)
        normed_two = (hat_two * gain_two).astype(BF16)
        yield
        acc = jnp.zeros((WIN, 256), F32)
        back = jnp.zeros((WIN, C), F32)
        c0 = 0.7978845608028654
        c1 = c0 * 0.044715
        for f in range(3):
            at = slice(256 * f, 256 * f + 256)
            pre = dot(normed_two, expand_ref[:, at])
            u = u_row[:, at]
            gate = 0.5 + 0.5 * jnp.tanh(pre * (c0 + c1 * (pre * pre)))
            unit = pre * gate
            acc = acc + unit * u
            pre, gate, unit = pre.astype(BF16), gate.astype(BF16), unit.astype(BF16)
            slope = gate * (1.0 + (pre - unit) * (2.0 * c0 + (6.0 * c1) * (pre * pre)))
            back = back + dot_nt(slope * u.astype(BF16), expand_ref[:, at])
            yield
        delta = jnp.sum(acc, axis=1, keepdims=True) + jnp.sum(
            middle * head_row, axis=1, keepdims=True
        )
        deltas[p] = jnp.broadcast_to(delta, (WIN, 128))
        kept = head_row + norm_back(back * gain_two, hat_two, scale_two)
        resid[p] = kept
        kept = kept.astype(BF16)
        yield
        n_turned = dot_nt(proj_ref[...], kept)
        n_tails = diagonal_tails(n_turned)
        fill_diagonal(diag_n, n_turned, n_tails)
        product = n_turned[:, 0:128] * main
        inner = [
            jnp.sum(product[HEAD * h : HEAD * h + HEAD], axis=0, keepdims=True)
            for h in range(HEADS)
        ]
        inner.append(jnp.sum(n_tails * tails, axis=0, keepdims=True))
        inner = jnp.concatenate(inner, axis=1)
        top = inner.astype(BF16).astype(F32)
        diag_n[C : C + 16, :] = jnp.concatenate(
            [-top, top - inner, jnp.zeros((14, WIDE), F32)], axis=0
        ).astype(BF16)
        n_rows[p] = dot_nt(kept, proj_ref[...]).astype(BF16)
        yield
        dweights = dot(values, diag_n[...])
        dscore = probs[p] * dweights.astype(BF16)
        dscores[p] = dscore
        yield
        main, tails = per_head(keys_t, dscore)
        dq_rows[p, :, 0:128] = main
        dq_rows[p, :, 128:256] = tails

    def forward_step(p, carry):
        interleave(forward(p, 0), forward(p, 1))
        return carry

    lax.fori_loop(0, 4, forward_step, 0)

    def scalar(l, k):
        return levels_ref[l // 2, l % 2 : l % 2 + 1, 72 + k : 73 + k]

    for col in range(2):
        deltas, source, fields, heights = (columns[col][k] for k in (11, 12, 13, 14))
        total = jnp.zeros((HALF, 128), F32)
        misfits, spots = [], []
        for l in range(8):
            a = 1 - l % 2
            p = (l // 2 - a) % 4
            rows = slice(HALF * a, HALF * a + HALF)
            spots.append((p, rows))
            temps = scalar(l, 2) + deltas[p, rows, :]
            total = total + scalar(l, 0) * temps
            height = fields[p, rows, 128:256] + total
            misfits.append(scalar(l, 1) * (height - fields[p, rows, 0:128]))
            top, middle, low = split3(height)
            heights[p, rows, :] = jnp.where(
                lane72 == 64, top, jnp.where(lane72 == 65, middle, low)
            )
        carried = jnp.zeros((HALF, 128), F32)
        for l in reversed(range(8)):
            p, rows = spots[l]
            carried = carried + misfits[l]
            source[p, rows, :] = scalar(l, 0) * carried

    def backward(p, col):
        (_, _, _, probs, dscores, q_rows, n_rows, dq_rows, resid, hats, scales,
         _, source, _, heights, made) = columns[col]
        s = wide(source[p])
        dk = dot(dscores[p], head_rows(s * q_rows[p].astype(F32))).astype(BF16)
        yield
        dv = dot(probs[p], head_rows(s * n_rows[p].astype(F32))).astype(BF16)
        yield
        dq = token_rows(dq_rows[p, :, 0:128], dq_rows[p, :, 128:256])
        dq = ((s * scale_q) * dq.astype(F32)).astype(BF16)
        dnormed = (
            dot(dq, wt_ref[0:C, :]) + dot(dk, wt_ref[C : 2 * C, :]) + dot(dv, wt_ref[2 * C :, :])
        )
        yield
        dx = norm_back(dnormed * gain_one, hats[p], wide(scales[p]))
        grad = s * resid[p] + dx
        lane = lanes((WIN, 128))
        last = jnp.concatenate([grad[:, 128:C], jnp.zeros((WIN, 64), F32)], axis=1)
        last = jnp.where(lane < 64, last, jnp.where(lane < 67, heights[p], 0.0))
        made[p, :, 0:128] = grad[:, 0:128].astype(BF16)
        made[p, :, 128:256] = last.astype(BF16)

    def backward_step(p, carry):
        interleave(backward(p, 0), backward(p, 1))
        return carry

    lax.fori_loop(0, 4, backward_step, 0)

    for p in range(4):
        for a in range(2):
            rows = slice(HALF * a, HALF * a + HALF)
            pair = [columns[col][15][p].astype(F32)[rows] for col in range(2)]
            moved = dot(back_ref[...], jnp.concatenate(pair, axis=0).astype(BF16))
            for beta in range(2):
                s, at = place(p, 2 * a + beta)
                tok_in[s, at : at + HALF, :] = moved[HALF * beta : HALF * beta + HALF]
    zero = jnp.zeros((16, 128), F32)
    for s in range(GROUP):
        pack_block(out_ref, s, tok_in[s], zero)


N_CONST = 11


def layer(x, consts):
    return pl.pallas_call(
        main_kernel,
        out_shape=jax.ShapeDtypeStruct((GROUP, ROWS, 128), BF16),
        in_specs=[vmem()] + [pl.BlockSpec(memory_space=pltpu.HBM)] * N_CONST,
        out_specs=vmem(),
        scratch_shapes=[pltpu.VMEM(c.shape, c.dtype) for c in consts]
        + [
            pltpu.VMEM((GROUP, WIN, 256), F32),
            pltpu.VMEM((4, 16, 128), F32),
            pltpu.SemaphoreType.DMA((N_CONST,)),
        ]
        + [pltpu.VMEM(shape, kind) for shape, kind in PER_COLUMN] * 2,
        compiler_params=pltpu.CompilerParams(vmem_limit_bytes=VMEM_ALL),
        cost_estimate=pl.CostEstimate(
            flops=20_000_000_000, bytes_accessed=4_000_000, transcendentals=3_000_000
        ),
        name="layer",
    )(x, *consts)


def pair_groups(odd):
    out = []
    for block in range(BLOCKS):
        for band in range((odd + block) % 2, BANDS, 2):
            members = (band, (band + 1) % BANDS)
            out.append(
                [(b * BLOCKS + block) * LEVS + lev for b in members for lev in range(LEVS)]
            )
    return out


def exchange(blocks, odd):
    return lax.all_to_all(
        blocks, ("tile", "lev"), 0, 0, axis_index_groups=pair_groups(odd)
    )


def block_step(value, steps):
    pairs = [
        (t, t - t % BLOCKS + (t + steps) % BLOCKS) for t in range(BANDS * BLOCKS)
    ]
    return lax.ppermute(value, "tile", pairs)


def on_device(
    features, attn_gain, w_qkv, w_proj, window_bias, patterns, window_pattern, mlp_gain,
    w_expand, w_reduce, temp_head, temp_base, thickness, level_weight, surface, target,
):
    feats = features[:, 0].transpose(1, 2, 0, 3)
    goal = target.transpose(0, 2, 1, 3)
    ground = surface.transpose(1, 0, 2)
    after, before = rim(window_pattern, feats, goal, ground)
    after = block_step(after, -1)
    before = block_step(before, 1)

    band = lax.axis_index("tile") // BLOCKS
    block = lax.axis_index("tile") % BLOCKS
    even = ((band + block) % 2 == 0).astype(jnp.int32)
    halves = [even.reshape(1), (1 - even).reshape(1)]
    perm = jnp.asarray(source_rows(), BF16)
    perm_back = jnp.asarray(target_rows(), BF16)
    order = jnp.asarray(window_rows(), BF16)
    order_back = jnp.asarray(window_rows().T, BF16)

    made = [
        prep(
            half, window_pattern, thickness, level_weight, temp_base,
            feats, after, before, goal, ground, perm,
        )
        for half in halves
    ]
    weights = (w_qkv, window_bias, patterns, attn_gain, mlp_gain, temp_head)
    weights, made[0] = lax.optimization_barrier((weights, made[0]))
    consts = (order, order_back) + tuple(setup(*weights)) + (w_proj, w_expand, w_reduce.T)
    done = None
    for odd in range(2):
        got = exchange(made[odd], odd)
        done = post(halves[odd], exchange(layer(got, consts), odd), perm_back, done)
    height, grad = done
    return height.transpose(0, 2, 1, 3), grad.transpose(2, 0, 1, 3)[:, None]


def solution(mesh):
    placed = (
        P("lev", "tile", None, None, None),
        P(), P(), P(), P(), P(),
        P(None, "tile"),
        P(), P(), P(), P(),
        P("lev"), P("lev"), P("lev"),
        P("tile", None, None),
        P("lev", "tile", None, None),
    )
    return jax.shard_map(
        on_device,
        mesh=mesh,
        in_specs=placed,
        out_specs=(P("lev", "tile", None, None), P("lev", "tile", None, None, None)),
        check_vma=False,
    )
```

```python
import jax
import jax.numpy as jnp
import numpy as np
from jax import lax
from jax.experimental import pallas as pl
from jax.experimental.pallas import tpu as pltpu
from jax.sharding import PartitionSpec as P

F32 = jnp.float32
BF16 = jnp.bfloat16
C = 192
HEADS = 6
HEAD = 32
FF = 768
WIN = 144
HALF = 72
QUARTER = 36
LONS = 90
SHIFT = 3
BLOCKS = 4
BANDS = 16
LEVS = 4
GROUP = 8
ROWS = 240
WIDE = 896
EPS = 1e-05
VMEM_LIMIT = 28 * 1024 * 1024
SMALL_VMEM = 12 * 1024 * 1024
VMEM_ALL = 60 * 1024 * 1024


def source_rows():
    table = np.zeros((2 * WIN, 6 * 64), np.float32)
    for q in range(2):
        for lev in range(2):
            for col in range(2):
                for i in range(QUARTER):
                    r, o = i // 6, i % 6
                    place = 2 * (12 * q + 6 * col + o + SHIFT) + lev
                    table[((q * 2 + lev) * 2 + col) * QUARTER + i, 64 * r + place] = 1.0
    return table


def target_rows():
    table = np.zeros((6 * 48, 3 * WIN), np.float32)
    for r in range(6):
        for x in range(48):
            e, lev = x // 2 + 9, x % 2
            d, col, o = e // 12, e % 12 // 6, e % 6
            table[48 * r + x, d * WIN + lev * HALF + col * QUARTER + 6 * r + o] = 1.0
    return table


def window_rows():
    table = np.zeros((WIN, WIN), np.float32)
    for col in range(2):
        for beta in range(2):
            for i in range(QUARTER):
                table[(col * 2 + beta) * QUARTER + i, (beta * 2 + col) * QUARTER + i] = 1.0
    return table


def dot(a, b):
    return jnp.dot(a, b, preferred_element_type=F32)


def dot_nt(a, b):
    return lax.dot_general(a, b, (((1,), (1,)), ((), ())), preferred_element_type=F32)


def lanes(shape):
    return lax.broadcasted_iota(jnp.int32, shape, len(shape) - 1)


def split3(value):
    top = value.astype(BF16).astype(F32)
    rest = value - top
    middle = rest.astype(BF16).astype(F32)
    return top, middle, rest - middle


def roll(value, steps):
    return pltpu.roll(value, steps % 128, 1)


def pack_block(out_ref, at, made, spare):
    lane = lanes((HALF, 128))
    out_ref[at, 0:WIN, :] = made[:, 0:128].astype(BF16)
    both = made[:, 128:256]
    tail = jnp.where(lane < 64, both[0:HALF], roll(both[HALF:WIN], 64))
    tail = jnp.concatenate([tail, jnp.zeros((8, 128), F32)], axis=0)
    lane16 = lanes((16, 128))
    extra = spare
    for g in range(9):
        moved = roll(both[16 * g : 16 * g + 16], 8 * g - 64)
        extra = jnp.where((lane16 >= 8 * g) & (lane16 < 8 * g + 8), moved, extra)
    out_ref[at, WIN : WIN + 16, :] = extra.astype(BF16)
    out_ref[at, WIN + 16 : ROWS, :] = tail.astype(BF16)


def unpack_block(block):
    first = block[0:WIN].astype(F32)
    extra = block[WIN : WIN + 16].astype(F32)
    tail = block[WIN + 16 : ROWS].astype(F32)[0:HALF]
    lane16 = lanes((16, 128))
    keep = (lane16 >= 64) & (lane16 < 72)
    spread = [jnp.where(keep, roll(extra, 64 - 8 * g), 0.0) for g in range(9)]
    spread = jnp.concatenate(spread, axis=0)
    lane = lanes((HALF, 128))
    second = [
        jnp.where(lane < 64, tail, spread[0:HALF]),
        jnp.where(lane < 64, roll(tail, 64), spread[HALF:WIN]),
    ]
    return first, second, extra


def vmem():
    return pl.BlockSpec(memory_space=pltpu.VMEM)


def smem():
    return pl.BlockSpec(memory_space=pltpu.SMEM)


def field_rows(targets, ground, count, padded):
    blank = jnp.zeros((count, 128 - LONS), F32)
    goal = [jnp.concatenate([t, blank], axis=1) for t in targets]
    ground = jnp.concatenate([ground, blank], axis=1)
    parts = split3(jnp.concatenate(goal, axis=1)) + split3(
        jnp.concatenate([ground, ground], axis=1)
    )
    if padded > count:
        more = jnp.zeros((padded - count, 256), F32)
        parts = [jnp.concatenate([v, more], axis=0) for v in parts]
    stacked = jnp.concatenate(parts, axis=0).astype(BF16)
    i = lax.broadcasted_iota(jnp.int32, (128, 6 * padded), 0)
    j = lanes((128, 6 * padded))
    hit = (j == padded * (i & 7) + (i >> 3)) & ((i & 7) < 6) & ((i >> 3) < count)
    return dot(jnp.where(hit, 1.0, 0.0).astype(BF16), stacked).astype(BF16)


def lon_pick(rows, first):
    x = lax.broadcasted_iota(jnp.int32, (rows, 256), 0)
    y = lanes((rows, 256))
    return jnp.where(y == 128 * (x & 1) + (x >> 1) + first, 1.0, 0.0).astype(BF16)


def rim_kernel(ids_ref, fa_ref, fb_ref, target_ref, surface_ref, next_ref, prev_ref):
    targets = [
        jnp.concatenate([target_ref[lev, r] for r in range(12)], axis=0) for lev in range(2)
    ]
    ground = jnp.concatenate([surface_ref[r] for r in range(12)], axis=0)
    fields = field_rows(targets, ground, 12, 16)
    spots = jnp.concatenate([lon_pick(8, 0), lon_pick(8, 86)], axis=0)
    values = dot_nt(spots, fields)
    lane = lanes((8, 128))
    idents = jnp.zeros((8, 128), F32)
    for p in range(4):
        idents = jnp.where(lane == 72 + p, ids_ref[p, 14].astype(F32), idents)
    for out_ref, f_ref, at, row, more in (
        (next_ref, fa_ref, 0, 0, 0.0), (prev_ref, fb_ref, 12, 8, idents)
    ):
        made = []
        for r in range(12):
            tokens = f_ref[r].reshape(20, C).astype(F32)[at : at + 8]
            second = jnp.concatenate([tokens[:, 128:C], jnp.zeros((8, 64), F32)], axis=1)
            extra = roll(values, 64 - 8 * r)[row : row + 8]
            second = jnp.where(lane < 64, second, jnp.where(lane < 72, extra, more))
            made.append(jnp.concatenate([tokens[:, 0:128], second], axis=1))
        out_ref[...] = jnp.concatenate(made, axis=0).astype(BF16)


def rim(ids, feats, target, surface):
    edge = jax.ShapeDtypeStruct((96, 256), BF16)
    return pl.pallas_call(
        rim_kernel,
        out_shape=(edge, edge),
        grid=(1,),
        in_specs=[
            smem(),
            pl.BlockSpec((12, 10, 2, C), lambda i: (0, 0, 0, 0)),
            pl.BlockSpec((12, 10, 2, C), lambda i: (0, 8, 0, 0)),
            pl.BlockSpec((2, 12, 1, LONS), lambda i: (0, 0, 0, 0)),
            pl.BlockSpec((12, 1, LONS), lambda i: (0, 0, 0)),
        ],
        out_specs=(
            pl.BlockSpec((96, 256), lambda i: (0, 0)),
            pl.BlockSpec((96, 256), lambda i: (0, 0)),
        ),
        compiler_params=pltpu.CompilerParams(vmem_limit_bytes=VMEM_ALL),
        name="rim",
    )(ids, feats, feats, target, surface)


def prep_kernel(
    half_ref, ids_ref, thick_ref, weight_ref, base_ref,
    f_ref, next_ref, prev_ref, target_ref, surface_ref, perm_ref,
    out_ref, rows_ref, packed, sems,
):
    upper = half_ref[0] == 1
    start = 6 * half_ref[0]
    targets = [
        jnp.concatenate([target_ref[lev, start + r] for r in range(6)], axis=0)
        for lev in range(2)
    ]
    ground = jnp.concatenate([surface_ref[start + r] for r in range(6)], axis=0)
    values = dot_nt(lon_pick(2 * LONS, 0), field_rows(targets, ground, 6, 8))
    after, before = (
        jnp.where(upper, ref[48:96].astype(F32), ref[0:48].astype(F32))
        for ref in (next_ref, prev_ref)
    )
    lane = lanes((2 * LONS, 128))
    for r in range(6):
        tokens = f_ref[start + r].reshape(2 * LONS, C).astype(F32)
        second = jnp.concatenate([tokens[:, 128:C], jnp.zeros((2 * LONS, 64), F32)], axis=1)
        extra = jnp.where(lane < 72, roll(values, 64 - 8 * r), 0.0)
        second = jnp.where(lane < 64, second, extra)
        for at, part in ((0, tokens[:, 0:128]), (128, second)):
            cut = slice(at, at + 128)
            rows_ref[208 * r : 208 * r + 176, cut] = part[0:176].astype(BF16)
            tail = [
                part[176:180],
                after[8 * r : 8 * r + 6, cut],
                before[8 * r + 2 : 8 * r + 8, cut],
                part[0:6],
                jnp.zeros((10, 128), F32),
            ]
            tail = jnp.concatenate(tail, axis=0).astype(BF16)
            rows_ref[208 * r + 176 : 208 * r + 208, cut] = tail
    lane16 = lanes((16, 128))
    row16 = lax.broadcasted_iota(jnp.int32, (16, 128), 0)
    scalars = jnp.zeros((16, 128), F32)
    for lev in range(2):
        for k, ref in enumerate((thick_ref, weight_ref, base_ref)):
            scalars = jnp.where((row16 == lev) & (lane16 == 72 + k), ref[lev], scalars)
    top, middle, low = split3(scalars)
    scalars = top + roll(middle, 3) + roll(low, 6)
    for m in range(4):
        source = [rows_ref[208 * r + 48 * m : 208 * r + 48 * m + 64, :] for r in range(6)]
        made = dot(perm_ref[...], jnp.concatenate(source, axis=0))
        for q in range(2):
            d = 2 * m + q
            spare = scalars
            for p in range(4):
                for col in range(2):
                    if 2 * d + col < 15:
                        ident = ids_ref[p, 2 * d + col].astype(F32)
                    else:
                        ident = before[0:1, 200 + p : 201 + p]
                    spare = jnp.where((row16 == 2 + p) & (lane16 == 81 + col), ident, spare)
            pack_block(packed, d, made[WIN * q : WIN * q + WIN], spare)
            pltpu.make_async_copy(packed.at[d], out_ref.at[d], sems.at[d]).start()
    for d in range(GROUP):
        pltpu.make_async_copy(packed.at[d], out_ref.at[d], sems.at[d]).wait()


def prep(half, ids, thick, weight, base, feats, after, before, target, surface, perm):
    return pl.pallas_call(
        prep_kernel,
        out_shape=jax.ShapeDtypeStruct((GROUP, ROWS, 128), BF16),
        in_specs=[smem()] * 5 + [vmem()] * 6,
        out_specs=pl.BlockSpec(memory_space=pl.ANY),
        scratch_shapes=[
            pltpu.VMEM((6 * 208, 256), BF16),
            pltpu.VMEM((GROUP, ROWS, 128), BF16),
            pltpu.SemaphoreType.DMA((GROUP,)),
        ],
        compiler_params=pltpu.CompilerParams(vmem_limit_bytes=SMALL_VMEM),
        cost_estimate=pl.CostEstimate(
            flops=1_000_000_000, bytes_accessed=2_500_000, transcendentals=0
        ),
        name="prep",
    )(half, ids, thick, weight, base, feats, after, before, target, surface, perm)


def post_kernel(half_ref, x_ref, perm_ref, *refs):
    height_out, grad_out, rows_ref, height_ref, grad_ref, sems = refs[-6:]
    start = 6 * half_ref[0]
    copies = [
        pltpu.make_async_copy(grad_ref, grad_out.at[pl.ds(start, 6)], sems.at[0]),
        pltpu.make_async_copy(height_ref, height_out.at[:, pl.ds(start, 6)], sems.at[1]),
    ]
    for d in range(GROUP):
        first, second, _ = unpack_block(x_ref[d])
        rows_ref[d, :, 0:128] = first.astype(BF16)
        rows_ref[d, :, 128:256] = jnp.concatenate(second, axis=0).astype(BF16)
    lane = lanes((48, 128))
    columns = []
    for m in range(4):
        source = [rows_ref[(2 * m + k) % GROUP] for k in (-1, 0, 1)]
        made = dot(perm_ref[...], jnp.concatenate(source, axis=0))
        count = 24 if m < 3 else 18
        column = jnp.zeros((48, 128), F32)
        for r in range(6):
            tokens = made[48 * r : 48 * r + 2 * count, 0:C].astype(BF16)
            grad_ref[r, 24 * m : 24 * m + count] = tokens.reshape(count, 2, C)
            moved = roll(made[48 * r : 48 * r + 48, 128:256], 8 * r - 64)
            column = jnp.where((lane >= 8 * r) & (lane < 8 * r + 3), moved, column)
        columns.append(column)
    copies[0].start()
    columns = jnp.concatenate(columns, axis=0).astype(BF16)
    rows = lax.dot_general(
        columns, lon_pick(192, 0), (((0,), (0,)), ((), ())), preferred_element_type=F32
    )
    for r in range(6):
        row = rows[8 * r : 8 * r + 1] + rows[8 * r + 1 : 8 * r + 2] + rows[8 * r + 2 : 8 * r + 3]
        for lev in range(2):
            height_ref[lev, r] = row[:, 128 * lev : 128 * lev + LONS]
    copies[1].start()
    for copy in copies:
        copy.wait()


def post(half, blocks, perm, earlier):
    kept = [] if earlier is None else list(earlier)
    return pl.pallas_call(
        post_kernel,
        out_shape=(
            jax.ShapeDtypeStruct((2, 12, 1, LONS), F32),
            jax.ShapeDtypeStruct((12, LONS, 2, C), BF16),
        ),
        in_specs=[smem(), vmem(), vmem()] + [pl.BlockSpec(memory_space=pl.ANY) for _ in kept],
        out_specs=(pl.BlockSpec(memory_space=pl.ANY), pl.BlockSpec(memory_space=pl.ANY)),
        scratch_shapes=[
            pltpu.VMEM((GROUP, WIN, 256), BF16),
            pltpu.VMEM((2, 6, 1, LONS), F32),
            pltpu.VMEM((6, LONS, 2, C), BF16),
            pltpu.SemaphoreType.DMA((2,)),
        ],
        input_output_aliases={3: 0, 4: 1} if kept else {},
        compiler_params=pltpu.CompilerParams(vmem_limit_bytes=SMALL_VMEM),
        cost_estimate=pl.CostEstimate(
            flops=1_000_000_000, bytes_accessed=2_500_000, transcendentals=0
        ),
        name="post",
    )(half, blocks, perm, *kept)


def norm_parts(x):
    center = jnp.sum(x, axis=-1, keepdims=True) * (1.0 / C)
    moved = x - center
    spread = jnp.sum(moved * moved, axis=-1, keepdims=True) * (1.0 / C)
    scale = lax.rsqrt(spread + EPS)
    return moved * scale, scale


def norm_back(cotangent, hat, scale):
    mean = jnp.sum(cotangent, axis=-1, keepdims=True) * (1.0 / C)
    along = jnp.sum(cotangent * hat, axis=-1, keepdims=True) * (1.0 / C)
    return scale * (cotangent - mean - hat * along)


def wide(value):
    return jnp.concatenate([value, value[:, 0:64]], axis=1)


def diagonal_tails(turned):
    lane = lanes((HEAD, 128))
    out = []
    for h in range(HEADS):
        rows = slice(HEAD * h, HEAD * h + HEAD)
        tail = jnp.concatenate([turned[rows, 128:WIN], jnp.zeros((HEAD, 112), F32)], axis=1)
        tail = roll(tail, 16 * h)
        out.append(jnp.where((lane >= 16 * h) & (lane < 16 * h + 16), tail, 0.0))
    return jnp.concatenate(out, axis=0)


def fill_diagonal(ref, turned, tails):
    for h in range(HEADS):
        rows = slice(HEAD * h, HEAD * h + HEAD)
        ref[rows, 128 * h : 128 * h + 128] = turned[rows, 0:128].astype(BF16)
    ref[0:C, 768:WIDE] = tails.astype(BF16)


def per_head(turned, weights):
    main = []
    for c in range(3):
        two = dot(turned[64 * c : 64 * c + 64], weights[:, 256 * c : 256 * c + 256])
        main += [two[0:HEAD, 0:128], two[HEAD:64, 128:256]]
    return jnp.concatenate(main, axis=0), dot(turned, weights[:, 768:WIDE])


def token_rows(main, tails):
    tails = tails.astype(BF16).T
    lane = lanes((16, C))
    last = jnp.zeros((16, C), BF16)
    for h in range(HEADS):
        mine = (lane >= HEAD * h) & (lane < HEAD * h + HEAD)
        last = jnp.where(mine, tails[16 * h : 16 * h + 16], last)
    return jnp.concatenate([main.astype(BF16).T, last], axis=0)


def head_rows(value):
    lane = lanes((WIN, C))
    parts, tails = [], []
    for h in range(HEADS):
        mine = jnp.where((lane >= HEAD * h) & (lane < HEAD * h + HEAD), value, 0.0).astype(BF16)
        parts.append(mine[0:128])
        tails.append(mine[128:WIN])
    return jnp.concatenate(parts + tails + [jnp.zeros((32, C), BF16)], axis=0)


def setup_kernel(
    w_ref, bias_ref, pat_ref, attn_gain_ref, mlp_gain_ref, temp_head_ref, reduce_ref,
    wt_ref, bias_out_ref, pat_q_ref, pat_k_ref, gains_ref, u_ref,
):
    wt_ref[...] = w_ref[...].astype(F32).T.astype(BF16)
    lane = lanes((WIN, 128))
    tails = jnp.zeros((WIN, 128), F32)
    for h in range(HEADS):
        turned = bias_ref[h].T
        bias_out_ref[:, 128 * h : 128 * h + 128] = turned[:, 0:128] * LOG2E
        tail = jnp.concatenate([turned[:, 128:WIN], jnp.zeros((WIN, 112), F32)], axis=1)
        tail = roll(tail, 16 * h)
        tails = jnp.where((lane >= 16 * h) & (lane < 16 * h + 16), tail, tails)
    bias_out_ref[:, 768:WIDE] = tails * LOG2E
    pat = pat_ref[...].astype(F32)
    for h in range(HEADS):
        pat_q_ref[:, 128 * h : 128 * h + 128] = pat[:, 0:128]
    tail = jnp.concatenate([pat[:, 128:WIN], jnp.zeros((8, 112), F32)], axis=1)
    tails = tail
    for h in range(1, 8):
        tails = tails + roll(tail, 16 * h)
    pat_q_ref[:, 768:WIDE] = tails
    pat_k_ref[...] = jnp.concatenate([pat, jnp.zeros((120, WIN), F32)], axis=0).T
    gains_ref[...] = jnp.zeros((8, 256), F32)
    gains_ref[0:1, 0:C] = attn_gain_ref[...]
    gains_ref[1:2, 0:C] = mlp_gain_ref[...]
    head_row = temp_head_ref[...].astype(F32)
    gains_ref[2:3, 0:C] = head_row
    u_ref[...] = dot(jnp.broadcast_to(head_row, (8, C)).astype(BF16), reduce_ref[...])


def setup(w_qkv, window_bias, patterns, attn_gain, mlp_gain, temp_head, reduce_t):
    return pl.pallas_call(
        setup_kernel,
        out_shape=(
            jax.ShapeDtypeStruct((3 * C, C), BF16),
            jax.ShapeDtypeStruct((WIN, WIDE), F32),
            jax.ShapeDtypeStruct((8, WIDE), F32),
            jax.ShapeDtypeStruct((WIN, 128), F32),
            jax.ShapeDtypeStruct((8, 256), F32),
            jax.ShapeDtypeStruct((8, FF), F32),
        ),
        in_specs=[vmem()] * 7,
        out_specs=(vmem(),) * 6,
        compiler_params=pltpu.CompilerParams(vmem_limit_bytes=SMALL_VMEM),
        cost_estimate=pl.CostEstimate(
            flops=1_000_000_000, bytes_accessed=3_000_000, transcendentals=0
        ),
        name="setup",
    )(w_qkv, window_bias, patterns, attn_gain[None], mlp_gain[None], temp_head[None], reduce_t)


LOG2E = 1.4426950408889634


def interleave(*runs):
    live = list(runs)
    while live:
        for run in list(live):
            try:
                next(run)
            except StopIteration:
                live.remove(run)


PER_COLUMN = (
    ((4, WIN, 256), F32),
    ((208, WIDE), BF16),
    ((208, WIDE), BF16),
    ((4, WIN, WIDE), BF16),
    ((4, WIN, WIDE), BF16),
    ((4, WIN, C), BF16),
    ((4, WIN, C), BF16),
    ((4, C, 256), F32),
    ((4, WIN, C), F32),
    ((4, WIN, C), F32),
    ((4, WIN, 128), F32),
    ((4, WIN, 128), F32),
    ((4, WIN, 128), F32),
    ((4, WIN, 256), F32),
    ((4, WIN, 128), F32),
    ((4, WIN, 256), BF16),
)


def main_kernel(
    x_ref, order_ref, back_ref, wt_ref, bias_ref, pat_q_ref, pat_k_ref, gains_ref, u_ref,
    proj_ref, expand_ref,
    out_ref, tok_in, levels_ref, packed, sems, *scratch,
):
    columns = (scratch[: len(PER_COLUMN)], scratch[len(PER_COLUMN) :])
    scale_q = 1.0 / HEAD**0.5
    lane72 = lanes((HALF, 128))
    lane16 = lanes((16, 128))
    row16 = lax.broadcasted_iota(jnp.int32, (16, 128), 0)
    for s in range(GROUP):
        first, second, extra = unpack_block(x_ref[s])
        tok_in[s, :, 0:128] = first
        tok_in[s, 0:HALF, 128:256] = second[0]
        tok_in[s, HALF:WIN, 128:256] = second[1]
        if s < 4:
            whole = (extra + roll(extra, -3)) + roll(extra, -6)
            levels_ref[s] = jnp.where(lane16 < 75, whole, extra)
    for col in range(2):
        for ref in columns[col][1:3]:
            ref[...] = jnp.zeros(ref.shape, BF16)

    def place(p, part):
        a, beta = part // 2, part % 2
        return beta * 4 + (p + a) % 4, (HALF if a == 0 else 0)

    pick_row = lax.broadcasted_iota(jnp.int32, (128, 256), 0)
    pick_lane = lanes((128, 256))
    pick = jnp.where(
        pick_lane < 128,
        jnp.where((pick_row >= 64) & (pick_row < 67), 1.0, 0.0),
        jnp.where((pick_row >= 67) & (pick_row < 70), 1.0, 0.0),
    ).astype(BF16)
    for p in range(4):
        for a in range(2):
            pieces = []
            for beta in range(2):
                s, at = place(p, 2 * a + beta)
                pieces.append(tok_in[s, at : at + HALF, :])
            moved = dot(order_ref[...], jnp.concatenate(pieces, axis=0).astype(BF16))
            fields = dot(moved[:, 128:256].astype(BF16), pick)
            for col in range(2):
                rows = slice(HALF * a, HALF * a + HALF)
                columns[col][0][p, rows, :] = moved[HALF * col : HALF * col + HALF]
                columns[col][13][p, rows, :] = fields[HALF * col : HALF * col + HALF]

    gain_one = gains_ref[0:1, 0:C]
    gain_two = gains_ref[1:2, 0:C]
    head_row = gains_ref[2:3, 0:C]
    u_row = u_ref[0:1, :]

    def forward(p, col):
        (tok, diag_q, diag_n, probs, dscores, q_rows, n_rows, dq_rows, resid, hats, scales,
         deltas, _, _, _, _) = columns[col]
        x = tok[p, :, 0:C]
        hat, scale = norm_parts(x)
        normed = (hat * gain_one).astype(BF16)
        hats[p] = hat
        scales[p] = jnp.broadcast_to(scale, (WIN, 128))
        spot = (row16 == 2 + p) & (lane16 == 81 + col)
        ident = jnp.sum(jnp.where(spot, levels_ref[0], 0.0), axis=0, keepdims=True)
        ident = jnp.sum(ident, axis=1, keepdims=True)
        row8 = lax.broadcasted_iota(jnp.int32, (8, 1), 0).astype(F32)
        label_q = jnp.sum(jnp.where(row8 == ident, pat_q_ref[...], 0.0), axis=0, keepdims=True)
        lane_row = lanes((1, 128)).astype(F32)
        label_k = jnp.sum(
            jnp.where(lane_row == ident, pat_k_ref[...], 0.0), axis=1, keepdims=True
        )
        yield
        turned = dot_nt(wt_ref[...], normed)
        q_turned = turned[0:C] * (scale_q * LOG2E)
        fill_diagonal(diag_q, q_turned, diagonal_tails(q_turned))
        apart = jnp.where(row8 == label_q, 0.0, -1e30)
        diag_q[C : C + 16, :] = jnp.concatenate(
            [apart, jnp.zeros((8, WIDE), F32)], axis=0
        ).astype(BF16)
        keys_t = turned[C : 2 * C].astype(BF16)
        values_t = turned[2 * C : 3 * C].astype(BF16)
        yield
        q_rows[p] = (dot_nt(normed, wt_ref[0:C, :]) * scale_q).astype(BF16)
        keys = dot_nt(normed, wt_ref[C : 2 * C, :])
        lane16w = lanes((WIN, 16))
        marks = jnp.where(lane16w.astype(F32) == label_k, 1.0, 0.0)
        keys = jnp.concatenate([keys, marks], axis=1).astype(BF16)
        values = dot_nt(normed, wt_ref[2 * C : 3 * C, :])
        ones = jnp.where(lane16w < 2, 1.0, 0.0)
        values = jnp.concatenate([values, ones], axis=1).astype(BF16)
        yield
        scores = dot(keys, diag_q[...]) + bias_ref[...]
        yield
        raised = jnp.exp2(scores - jnp.max(scores, axis=0, keepdims=True))
        weights = (raised * (1.0 / jnp.sum(raised, axis=0, keepdims=True))).astype(BF16)
        probs[p] = weights
        yield
        main, tails = per_head(values_t, weights)
        context = token_rows(main, tails)
        yield
        middle = (x + dot(context, proj_ref[...])).astype(BF16).astype(F32)
        hat_two, scale_two = norm_parts(middle)
        normed_two = (hat_two * gain_two).astype(BF16)
        yield
        acc = jnp.zeros((WIN, 256), F32)
        back = jnp.zeros((WIN, C), F32)
        c0 = 0.7978845608028654
        c1 = c0 * 0.044715
        for f in range(3):
            at = slice(256 * f, 256 * f + 256)
            pre = dot(normed_two, expand_ref[:, at])
            u = u_row[:, at]
            gate = 0.5 + 0.5 * jnp.tanh(pre * (c0 + c1 * (pre * pre)))
            unit = pre * gate
            acc = acc + unit * u
            pre, gate, unit = pre.astype(BF16), gate.astype(BF16), unit.astype(BF16)
            slope = gate * (1.0 + (pre - unit) * (2.0 * c0 + (6.0 * c1) * (pre * pre)))
            back = back + dot_nt(slope * u.astype(BF16), expand_ref[:, at])
            yield
        delta = jnp.sum(acc, axis=1, keepdims=True) + jnp.sum(
            middle * head_row, axis=1, keepdims=True
        )
        deltas[p] = jnp.broadcast_to(delta, (WIN, 128))
        kept = head_row + norm_back(back * gain_two, hat_two, scale_two)
        resid[p] = kept
        kept = kept.astype(BF16)
        yield
        n_turned = dot_nt(proj_ref[...], kept)
        n_tails = diagonal_tails(n_turned)
        fill_diagonal(diag_n, n_turned, n_tails)
        product = n_turned[:, 0:128] * main
        inner = [
            jnp.sum(product[HEAD * h : HEAD * h + HEAD], axis=0, keepdims=True)
            for h in range(HEADS)
        ]
        inner.append(jnp.sum(n_tails * tails, axis=0, keepdims=True))
        inner = jnp.concatenate(inner, axis=1)
        top = inner.astype(BF16).astype(F32)
        diag_n[C : C + 16, :] = jnp.concatenate(
            [-top, top - inner, jnp.zeros((14, WIDE), F32)], axis=0
        ).astype(BF16)
        n_rows[p] = dot_nt(kept, proj_ref[...]).astype(BF16)
        yield
        dweights = dot(values, diag_n[...])
        dscore = probs[p] * dweights.astype(BF16)
        dscores[p] = dscore
        yield
        main, tails = per_head(keys_t, dscore)
        dq_rows[p, :, 0:128] = main
        dq_rows[p, :, 128:256] = tails

    def forward_step(p, carry):
        interleave(forward(p, 0), forward(p, 1))
        return carry

    lax.fori_loop(0, 4, forward_step, 0)

    def scalar(l, k):
        return levels_ref[l // 2, l % 2 : l % 2 + 1, 72 + k : 73 + k]

    for col in range(2):
        deltas, source, fields, heights = (columns[col][k] for k in (11, 12, 13, 14))
        total = jnp.zeros((HALF, 128), F32)
        misfits, spots = [], []
        for l in range(8):
            a = 1 - l % 2
            p = (l // 2 - a) % 4
            rows = slice(HALF * a, HALF * a + HALF)
            spots.append((p, rows))
            temps = scalar(l, 2) + deltas[p, rows, :]
            total = total + scalar(l, 0) * temps
            height = fields[p, rows, 128:256] + total
            misfits.append(scalar(l, 1) * (height - fields[p, rows, 0:128]))
            top, middle, low = split3(height)
            heights[p, rows, :] = jnp.where(
                lane72 == 64, top, jnp.where(lane72 == 65, middle, low)
            )
        carried = jnp.zeros((HALF, 128), F32)
        for l in reversed(range(8)):
            p, rows = spots[l]
            carried = carried + misfits[l]
            source[p, rows, :] = scalar(l, 0) * carried

    def backward(p, col):
        (_, _, _, probs, dscores, q_rows, n_rows, dq_rows, resid, hats, scales,
         _, source, _, heights, made) = columns[col]
        s = wide(source[p])
        dk = dot(dscores[p], head_rows(s * q_rows[p].astype(F32))).astype(BF16)
        yield
        dv = dot(probs[p], head_rows(s * n_rows[p].astype(F32))).astype(BF16)
        yield
        dq = token_rows(dq_rows[p, :, 0:128], dq_rows[p, :, 128:256])
        dq = ((s * scale_q) * dq.astype(F32)).astype(BF16)
        dnormed = (
            dot(dq, wt_ref[0:C, :]) + dot(dk, wt_ref[C : 2 * C, :]) + dot(dv, wt_ref[2 * C :, :])
        )
        yield
        dx = norm_back(dnormed * gain_one, hats[p], wide(scales[p]))
        grad = s * resid[p] + dx
        lane = lanes((WIN, 128))
        last = jnp.concatenate([grad[:, 128:C], jnp.zeros((WIN, 64), F32)], axis=1)
        last = jnp.where(lane < 64, last, jnp.where(lane < 67, heights[p], 0.0))
        made[p, :, 0:128] = grad[:, 0:128].astype(BF16)
        made[p, :, 128:256] = last.astype(BF16)

    def backward_step(p, carry):
        interleave(backward(p, 0), backward(p, 1))
        return carry

    lax.fori_loop(0, 4, backward_step, 0)

    for p in range(4):
        for a in range(2):
            rows = slice(HALF * a, HALF * a + HALF)
            pair = [columns[col][15][p].astype(F32)[rows] for col in range(2)]
            moved = dot(back_ref[...], jnp.concatenate(pair, axis=0).astype(BF16))
            for beta in range(2):
                s, at = place(p, 2 * a + beta)
                tok_in[s, at : at + HALF, :] = moved[HALF * beta : HALF * beta + HALF]
    zero = jnp.zeros((16, 128), F32)
    for s in range(GROUP):
        pack_block(packed, s, tok_in[s], zero)
        pltpu.make_async_copy(packed.at[s], out_ref.at[s], sems.at[s]).start()
    for s in range(GROUP):
        pltpu.make_async_copy(packed.at[s], out_ref.at[s], sems.at[s]).wait()


def layer(x, consts):
    return pl.pallas_call(
        main_kernel,
        out_shape=jax.ShapeDtypeStruct((GROUP, ROWS, 128), BF16),
        in_specs=[vmem()] * (1 + len(consts)),
        out_specs=pl.BlockSpec(memory_space=pl.ANY),
        scratch_shapes=[
            pltpu.VMEM((GROUP, WIN, 256), F32),
            pltpu.VMEM((4, 16, 128), F32),
            pltpu.VMEM((GROUP, ROWS, 128), BF16),
            pltpu.SemaphoreType.DMA((GROUP,)),
        ]
        + [pltpu.VMEM(shape, kind) for shape, kind in PER_COLUMN] * 2,
        compiler_params=pltpu.CompilerParams(vmem_limit_bytes=VMEM_LIMIT),
        cost_estimate=pl.CostEstimate(
            flops=20_000_000_000, bytes_accessed=4_000_000, transcendentals=3_000_000
        ),
        name="layer",
    )(x, *consts)


def pair_groups(odd):
    out = []
    for block in range(BLOCKS):
        for band in range((odd + block) % 2, BANDS, 2):
            members = (band, (band + 1) % BANDS)
            out.append(
                [(b * BLOCKS + block) * LEVS + lev for b in members for lev in range(LEVS)]
            )
    return out


def exchange(blocks, odd):
    return lax.all_to_all(
        blocks, ("tile", "lev"), 0, 0, axis_index_groups=pair_groups(odd)
    )


def block_step(value, steps):
    pairs = [
        (t, t - t % BLOCKS + (t + steps) % BLOCKS) for t in range(BANDS * BLOCKS)
    ]
    return lax.ppermute(value, "tile", pairs)


def on_device(
    features, attn_gain, w_qkv, w_proj, window_bias, patterns, window_pattern, mlp_gain,
    w_expand, w_reduce, temp_head, temp_base, thickness, level_weight, surface, target,
):
    feats = features[:, 0].transpose(1, 2, 0, 3)
    goal = target.transpose(0, 2, 1, 3)
    ground = surface.transpose(1, 0, 2)
    after, before = rim(window_pattern, feats, goal, ground)
    after = block_step(after, -1)
    before = block_step(before, 1)

    band = lax.axis_index("tile") // BLOCKS
    block = lax.axis_index("tile") % BLOCKS
    even = ((band + block) % 2 == 0).astype(jnp.int32)
    halves = [even.reshape(1), (1 - even).reshape(1)]
    perm = jnp.asarray(source_rows(), BF16)
    perm_back = jnp.asarray(target_rows(), BF16)
    order = jnp.asarray(window_rows(), BF16)
    order_back = jnp.asarray(window_rows().T, BF16)

    made = [
        prep(
            half, window_pattern, thickness, level_weight, temp_base,
            feats, after, before, goal, ground, perm,
        )
        for half in halves
    ]
    weights = (w_qkv, window_bias, patterns, attn_gain, mlp_gain, temp_head, w_reduce.T)
    weights, made[0] = lax.optimization_barrier((weights, made[0]))
    consts = (order, order_back) + tuple(setup(*weights)) + (w_proj, w_expand)
    done = None
    for odd in range(2):
        got = exchange(made[odd], odd)
        done = post(halves[odd], exchange(layer(got, consts), odd), perm_back, done)
    height, grad = done
    return height.transpose(0, 2, 1, 3), grad.transpose(2, 0, 1, 3)[:, None]


def solution(mesh):
    placed = (
        P("lev", "tile", None, None, None),
        P(), P(), P(), P(), P(),
        P(None, "tile"),
        P(), P(), P(), P(),
        P("lev"), P("lev"), P("lev"),
        P("tile", None, None),
        P("lev", "tile", None, None),
    )
    return jax.shard_map(
        on_device,
        mesh=mesh,
        in_specs=placed,
        out_specs=(P("lev", "tile", None, None), P("lev", "tile", None, None, None)),
        check_vma=False,
    )
```

```python
import jax
import jax.numpy as jnp
import numpy as np
from jax import lax
from jax.experimental import pallas as pl
from jax.experimental.pallas import tpu as pltpu
from jax.sharding import PartitionSpec as P

F32 = jnp.float32
BF16 = jnp.bfloat16
C = 192
HEADS = 6
HEAD = 32
FF = 768
WIN = 144
HALF = 72
QUARTER = 36
LONS = 90
SHIFT = 3
BLOCKS = 4
BANDS = 16
LEVS = 4
GROUP = 8
ROWS = 240
WIDE = 896
EPS = 1e-05
VMEM_LIMIT = 28 * 1024 * 1024
SMALL_VMEM = 12 * 1024 * 1024
VMEM_ALL = 60 * 1024 * 1024


def source_rows():
    table = np.zeros((2 * WIN, 6 * 64), np.float32)
    for q in range(2):
        for lev in range(2):
            for col in range(2):
                for i in range(QUARTER):
                    r, o = i // 6, i % 6
                    place = 2 * (12 * q + 6 * col + o + SHIFT) + lev
                    table[((q * 2 + lev) * 2 + col) * QUARTER + i, 64 * r + place] = 1.0
    return table


def target_rows():
    table = np.zeros((6 * 48, 3 * WIN), np.float32)
    for r in range(6):
        for x in range(48):
            e, lev = x // 2 + 9, x % 2
            d, col, o = e // 12, e % 12 // 6, e % 6
            table[48 * r + x, d * WIN + lev * HALF + col * QUARTER + 6 * r + o] = 1.0
    return table


def window_rows():
    table = np.zeros((WIN, WIN), np.float32)
    for col in range(2):
        for beta in range(2):
            for i in range(QUARTER):
                table[(col * 2 + beta) * QUARTER + i, (beta * 2 + col) * QUARTER + i] = 1.0
    return table


def dot(a, b):
    return jnp.dot(a, b, preferred_element_type=F32)


def dot_nt(a, b):
    return lax.dot_general(a, b, (((1,), (1,)), ((), ())), preferred_element_type=F32)


def lanes(shape):
    return lax.broadcasted_iota(jnp.int32, shape, len(shape) - 1)


def split3(value):
    top = value.astype(BF16).astype(F32)
    rest = value - top
    middle = rest.astype(BF16).astype(F32)
    return top, middle, rest - middle


def roll(value, steps):
    return pltpu.roll(value, steps % 128, 1)


def pack_block(out_ref, at, made, spare):
    lane = lanes((HALF, 128))
    out_ref[at, 0:WIN, :] = made[:, 0:128].astype(BF16)
    both = made[:, 128:256]
    tail = jnp.where(lane < 64, both[0:HALF], roll(both[HALF:WIN], 64))
    tail = jnp.concatenate([tail, jnp.zeros((8, 128), F32)], axis=0)
    lane16 = lanes((16, 128))
    extra = spare
    for g in range(9):
        moved = roll(both[16 * g : 16 * g + 16], 8 * g - 64)
        extra = jnp.where((lane16 >= 8 * g) & (lane16 < 8 * g + 8), moved, extra)
    out_ref[at, WIN : WIN + 16, :] = extra.astype(BF16)
    out_ref[at, WIN + 16 : ROWS, :] = tail.astype(BF16)


def unpack_block(block):
    first = block[0:WIN].astype(F32)
    extra = block[WIN : WIN + 16].astype(F32)
    tail = block[WIN + 16 : ROWS].astype(F32)[0:HALF]
    lane16 = lanes((16, 128))
    keep = (lane16 >= 64) & (lane16 < 72)
    spread = [jnp.where(keep, roll(extra, 64 - 8 * g), 0.0) for g in range(9)]
    spread = jnp.concatenate(spread, axis=0)
    lane = lanes((HALF, 128))
    second = [
        jnp.where(lane < 64, tail, spread[0:HALF]),
        jnp.where(lane < 64, roll(tail, 64), spread[HALF:WIN]),
    ]
    return first, second, extra


def vmem():
    return pl.BlockSpec(memory_space=pltpu.VMEM)


def smem():
    return pl.BlockSpec(memory_space=pltpu.SMEM)


def field_rows(targets, ground, count, padded):
    blank = jnp.zeros((count, 128 - LONS), F32)
    goal = [jnp.concatenate([t, blank], axis=1) for t in targets]
    ground = jnp.concatenate([ground, blank], axis=1)
    parts = split3(jnp.concatenate(goal, axis=1)) + split3(
        jnp.concatenate([ground, ground], axis=1)
    )
    if padded > count:
        more = jnp.zeros((padded - count, 256), F32)
        parts = [jnp.concatenate([v, more], axis=0) for v in parts]
    stacked = jnp.concatenate(parts, axis=0).astype(BF16)
    i = lax.broadcasted_iota(jnp.int32, (128, 6 * padded), 0)
    j = lanes((128, 6 * padded))
    hit = (j == padded * (i & 7) + (i >> 3)) & ((i & 7) < 6) & ((i >> 3) < count)
    return dot(jnp.where(hit, 1.0, 0.0).astype(BF16), stacked).astype(BF16)


def lon_pick(rows, first):
    x = lax.broadcasted_iota(jnp.int32, (rows, 256), 0)
    y = lanes((rows, 256))
    return jnp.where(y == 128 * (x & 1) + (x >> 1) + first, 1.0, 0.0).astype(BF16)


def rim_kernel(ids_ref, fa_ref, fb_ref, target_ref, surface_ref, next_ref, prev_ref):
    targets = [
        jnp.concatenate([target_ref[lev, r] for r in range(12)], axis=0) for lev in range(2)
    ]
    ground = jnp.concatenate([surface_ref[r] for r in range(12)], axis=0)
    fields = field_rows(targets, ground, 12, 16)
    spots = jnp.concatenate([lon_pick(8, 0), lon_pick(8, 86)], axis=0)
    values = dot_nt(spots, fields)
    lane = lanes((8, 128))
    idents = jnp.zeros((8, 128), F32)
    for p in range(4):
        idents = jnp.where(lane == 72 + p, ids_ref[p, 14].astype(F32), idents)
    for out_ref, f_ref, at, row, more in (
        (next_ref, fa_ref, 0, 0, 0.0), (prev_ref, fb_ref, 12, 8, idents)
    ):
        made = []
        for r in range(12):
            tokens = f_ref[r].reshape(20, C).astype(F32)[at : at + 8]
            second = jnp.concatenate([tokens[:, 128:C], jnp.zeros((8, 64), F32)], axis=1)
            extra = roll(values, 64 - 8 * r)[row : row + 8]
            second = jnp.where(lane < 64, second, jnp.where(lane < 72, extra, more))
            made.append(jnp.concatenate([tokens[:, 0:128], second], axis=1))
        out_ref[...] = jnp.concatenate(made, axis=0).astype(BF16)


def rim(ids, feats, target, surface):
    edge = jax.ShapeDtypeStruct((96, 256), BF16)
    return pl.pallas_call(
        rim_kernel,
        out_shape=(edge, edge),
        grid=(1,),
        in_specs=[
            smem(),
            pl.BlockSpec((12, 10, 2, C), lambda i: (0, 0, 0, 0)),
            pl.BlockSpec((12, 10, 2, C), lambda i: (0, 8, 0, 0)),
            pl.BlockSpec((2, 12, 1, LONS), lambda i: (0, 0, 0, 0)),
            pl.BlockSpec((12, 1, LONS), lambda i: (0, 0, 0)),
        ],
        out_specs=(
            pl.BlockSpec((96, 256), lambda i: (0, 0)),
            pl.BlockSpec((96, 256), lambda i: (0, 0)),
        ),
        compiler_params=pltpu.CompilerParams(vmem_limit_bytes=VMEM_ALL),
        name="rim",
    )(ids, feats, feats, target, surface)


def fill_rows(half_ref, f_ref, target_ref, surface_ref, rows_ref, after, before):
    start = 6 * half_ref[0]
    targets = [
        jnp.concatenate([target_ref[lev, start + r] for r in range(6)], axis=0)
        for lev in range(2)
    ]
    ground = jnp.concatenate([surface_ref[start + r] for r in range(6)], axis=0)
    values = dot_nt(lon_pick(2 * LONS, 0), field_rows(targets, ground, 6, 8))
    lane = lanes((2 * LONS, 128))
    for r in range(6):
        tokens = f_ref[start + r].reshape(2 * LONS, C).astype(F32)
        second = jnp.concatenate([tokens[:, 128:C], jnp.zeros((2 * LONS, 64), F32)], axis=1)
        extra = jnp.where(lane < 72, roll(values, 64 - 8 * r), 0.0)
        second = jnp.where(lane < 64, second, extra)
        for at, part in ((0, tokens[:, 0:128]), (128, second)):
            cut = slice(at, at + 128)
            rows_ref[208 * r : 208 * r + 176, cut] = part[0:176].astype(BF16)
            if after is None:
                rim_part = [jnp.zeros((12, 128), F32)]
            else:
                rim_part = [after[8 * r : 8 * r + 6, cut], before[8 * r + 2 : 8 * r + 8, cut]]
            tail = [part[176:180]] + rim_part + [part[0:6], jnp.zeros((10, 128), F32)]
            tail = jnp.concatenate(tail, axis=0).astype(BF16)
            rows_ref[208 * r + 176 : 208 * r + 208, cut] = tail


def rims(half_ref, next_ref, prev_ref):
    upper = half_ref[0] == 1
    return [
        jnp.where(upper, ref[48:96].astype(F32), ref[0:48].astype(F32))
        for ref in (next_ref, prev_ref)
    ]


def send_blocks(pairs, ids_ref, level_refs, source, before, perm_ref, packed, out_ref, sems):
    lane16 = lanes((16, 128))
    row16 = lax.broadcasted_iota(jnp.int32, (16, 128), 0)
    scalars = jnp.zeros((16, 128), F32)
    for lev in range(2):
        for k, ref in enumerate(level_refs):
            scalars = jnp.where((row16 == lev) & (lane16 == 72 + k), ref[lev], scalars)
    top, middle, low = split3(scalars)
    scalars = top + roll(middle, 3) + roll(low, 6)
    copies = []
    for m in pairs:
        made = dot(perm_ref[...], jnp.concatenate([source(r, m) for r in range(6)], axis=0))
        for q in range(2):
            d = 2 * m + q
            spare = scalars
            for p in range(4):
                for col in range(2):
                    if 2 * d + col < 15:
                        ident = ids_ref[p, 2 * d + col].astype(F32)
                    else:
                        ident = before[0:1, 200 + p : 201 + p]
                    spare = jnp.where((row16 == 2 + p) & (lane16 == 81 + col), ident, spare)
            at = d - 2 * pairs[0]
            pack_block(packed, at, made[WIN * q : WIN * q + WIN], spare)
            copies.append(pltpu.make_async_copy(packed.at[at], out_ref.at[d], sems.at[at]))
            copies[-1].start()
    for copy in copies:
        copy.wait()


def prep_kernel(
    half_ref, ids_ref, thick_ref, weight_ref, base_ref,
    f_ref, next_ref, prev_ref, target_ref, surface_ref, perm_ref,
    out_ref, rows_ref, packed, sems,
):
    after, before = rims(half_ref, next_ref, prev_ref)
    fill_rows(half_ref, f_ref, target_ref, surface_ref, rows_ref, after, before)
    send_blocks(
        range(4), ids_ref, (thick_ref, weight_ref, base_ref),
        lambda r, m: rows_ref[208 * r + 48 * m : 208 * r + 48 * m + 64, :],
        before, perm_ref, packed, out_ref, sems,
    )


def inner_kernel(
    half_ref, ids_ref, thick_ref, weight_ref, base_ref,
    f_ref, target_ref, surface_ref, perm_ref,
    out_ref, rows_ref, packed, sems,
):
    fill_rows(half_ref, f_ref, target_ref, surface_ref, rows_ref, None, None)
    send_blocks(
        range(3), ids_ref, (thick_ref, weight_ref, base_ref),
        lambda r, m: rows_ref[208 * r + 48 * m : 208 * r + 48 * m + 64, :],
        None, perm_ref, packed, out_ref, sems,
    )


def outer_kernel(
    half_ref, ids_ref, thick_ref, weight_ref, base_ref,
    next_ref, prev_ref, rows_ref, perm_ref, _,
    out_ref, packed, sems,
):
    after, before = rims(half_ref, next_ref, prev_ref)

    def source(r, m):
        own = rows_ref[208 * r + 176 : 208 * r + 208, :].astype(F32)
        more = [
            jnp.zeros((4, 256), F32), after[8 * r : 8 * r + 6], before[8 * r + 2 : 8 * r + 8],
            jnp.zeros((16, 256), F32),
        ]
        tail = (own + jnp.concatenate(more, axis=0)).astype(BF16)
        return jnp.concatenate([rows_ref[208 * r + 144 : 208 * r + 176, :], tail], axis=0)

    send_blocks(
        range(3, 4), ids_ref, (thick_ref, weight_ref, base_ref),
        source, before, perm_ref, packed, out_ref, sems,
    )


def prep_call(kernel, name, count, outs, out_specs, scratch, aliases, args):
    return pl.pallas_call(
        kernel,
        out_shape=outs,
        in_specs=[smem()] * 5
        + [vmem()] * (len(args) - 5 - len(aliases))
        + [pl.BlockSpec(memory_space=pl.ANY)] * len(aliases),
        out_specs=out_specs,
        scratch_shapes=scratch
        + [pltpu.VMEM((count, ROWS, 128), BF16), pltpu.SemaphoreType.DMA((count,))],
        input_output_aliases=aliases,
        compiler_params=pltpu.CompilerParams(vmem_limit_bytes=SMALL_VMEM),
        cost_estimate=pl.CostEstimate(
            flops=1_000_000_000, bytes_accessed=2_500_000, transcendentals=0
        ),
        name=name,
    )(*args)


BLOCKS_OUT = jax.ShapeDtypeStruct((GROUP, ROWS, 128), BF16)


def prep(half, ids, thick, weight, base, feats, after, before, target, surface, perm):
    return prep_call(
        prep_kernel, "prep", GROUP, BLOCKS_OUT, pl.BlockSpec(memory_space=pl.ANY),
        [pltpu.VMEM((6 * 208, 256), BF16)], {},
        (half, ids, thick, weight, base, feats, after, before, target, surface, perm),
    )


def prep_early(half, ids, thick, weight, base, feats, after, before, target, surface, perm):
    blocks, rows = prep_call(
        inner_kernel, "inner", 6,
        (BLOCKS_OUT, jax.ShapeDtypeStruct((6 * 208, 256), BF16)),
        (pl.BlockSpec(memory_space=pl.ANY), vmem()), [], {},
        (half, ids, thick, weight, base, feats, target, surface, perm),
    )
    return prep_call(
        outer_kernel, "outer", 2, BLOCKS_OUT, pl.BlockSpec(memory_space=pl.ANY), [], {9: 0},
        (half, ids, thick, weight, base, after, before, rows, perm, blocks),
    )


def post_kernel(half_ref, x_ref, perm_ref, *refs):
    height_out, grad_out, rows_ref, height_ref, grad_ref, sems = refs[-6:]
    start = 6 * half_ref[0]
    copies = [
        pltpu.make_async_copy(grad_ref, grad_out.at[pl.ds(start, 6)], sems.at[0]),
        pltpu.make_async_copy(height_ref, height_out.at[:, pl.ds(start, 6)], sems.at[1]),
    ]
    for d in range(GROUP):
        first, second, _ = unpack_block(x_ref[d])
        rows_ref[d, :, 0:128] = first.astype(BF16)
        rows_ref[d, :, 128:256] = jnp.concatenate(second, axis=0).astype(BF16)
    lane = lanes((48, 128))
    columns = []
    for m in range(4):
        source = [rows_ref[(2 * m + k) % GROUP] for k in (-1, 0, 1)]
        made = dot(perm_ref[...], jnp.concatenate(source, axis=0))
        count = 24 if m < 3 else 18
        column = jnp.zeros((48, 128), F32)
        for r in range(6):
            tokens = made[48 * r : 48 * r + 2 * count, 0:C].astype(BF16)
            grad_ref[r, 24 * m : 24 * m + count] = tokens.reshape(count, 2, C)
            moved = roll(made[48 * r : 48 * r + 48, 128:256], 8 * r - 64)
            column = jnp.where((lane >= 8 * r) & (lane < 8 * r + 3), moved, column)
        columns.append(column)
    copies[0].start()
    columns = jnp.concatenate(columns, axis=0).astype(BF16)
    rows = lax.dot_general(
        columns, lon_pick(192, 0), (((0,), (0,)), ((), ())), preferred_element_type=F32
    )
    for r in range(6):
        row = rows[8 * r : 8 * r + 1] + rows[8 * r + 1 : 8 * r + 2] + rows[8 * r + 2 : 8 * r + 3]
        for lev in range(2):
            height_ref[lev, r] = row[:, 128 * lev : 128 * lev + LONS]
    copies[1].start()
    for copy in copies:
        copy.wait()


def post(half, blocks, perm, earlier):
    kept = [] if earlier is None else list(earlier)
    return pl.pallas_call(
        post_kernel,
        out_shape=(
            jax.ShapeDtypeStruct((2, 12, 1, LONS), F32),
            jax.ShapeDtypeStruct((12, LONS, 2, C), BF16),
        ),
        in_specs=[smem(), vmem(), vmem()] + [pl.BlockSpec(memory_space=pl.ANY) for _ in kept],
        out_specs=(pl.BlockSpec(memory_space=pl.ANY), pl.BlockSpec(memory_space=pl.ANY)),
        scratch_shapes=[
            pltpu.VMEM((GROUP, WIN, 256), BF16),
            pltpu.VMEM((2, 6, 1, LONS), F32),
            pltpu.VMEM((6, LONS, 2, C), BF16),
            pltpu.SemaphoreType.DMA((2,)),
        ],
        input_output_aliases={3: 0, 4: 1} if kept else {},
        compiler_params=pltpu.CompilerParams(vmem_limit_bytes=SMALL_VMEM),
        cost_estimate=pl.CostEstimate(
            flops=1_000_000_000, bytes_accessed=2_500_000, transcendentals=0
        ),
        name="post",
    )(half, blocks, perm, *kept)


def norm_parts(x):
    center = jnp.sum(x, axis=-1, keepdims=True) * (1.0 / C)
    moved = x - center
    spread = jnp.sum(moved * moved, axis=-1, keepdims=True) * (1.0 / C)
    scale = lax.rsqrt(spread + EPS)
    return moved * scale, scale


def norm_back(cotangent, hat, scale):
    mean = jnp.sum(cotangent, axis=-1, keepdims=True) * (1.0 / C)
    along = jnp.sum(cotangent * hat, axis=-1, keepdims=True) * (1.0 / C)
    return scale * (cotangent - mean - hat * along)


def wide(value):
    return jnp.concatenate([value, value[:, 0:64]], axis=1)


def diagonal_tails(turned):
    lane = lanes((HEAD, 128))
    out = []
    for h in range(HEADS):
        rows = slice(HEAD * h, HEAD * h + HEAD)
        tail = jnp.concatenate([turned[rows, 128:WIN], jnp.zeros((HEAD, 112), F32)], axis=1)
        tail = roll(tail, 16 * h)
        out.append(jnp.where((lane >= 16 * h) & (lane < 16 * h + 16), tail, 0.0))
    return jnp.concatenate(out, axis=0)


def fill_diagonal(ref, turned, tails):
    for h in range(HEADS):
        rows = slice(HEAD * h, HEAD * h + HEAD)
        ref[rows, 128 * h : 128 * h + 128] = turned[rows, 0:128].astype(BF16)
    ref[0:C, 768:WIDE] = tails.astype(BF16)


def per_head(turned, weights):
    main = []
    for c in range(3):
        two = dot(turned[64 * c : 64 * c + 64], weights[:, 256 * c : 256 * c + 256])
        main += [two[0:HEAD, 0:128], two[HEAD:64, 128:256]]
    return jnp.concatenate(main, axis=0), dot(turned, weights[:, 768:WIDE])


def token_rows(main, tails):
    tails = tails.astype(BF16).T
    lane = lanes((16, C))
    last = jnp.zeros((16, C), BF16)
    for h in range(HEADS):
        mine = (lane >= HEAD * h) & (lane < HEAD * h + HEAD)
        last = jnp.where(mine, tails[16 * h : 16 * h + 16], last)
    return jnp.concatenate([main.astype(BF16).T, last], axis=0)


def head_rows(value):
    lane = lanes((WIN, C))
    parts, tails = [], []
    for h in range(HEADS):
        mine = jnp.where((lane >= HEAD * h) & (lane < HEAD * h + HEAD), value, 0.0).astype(BF16)
        parts.append(mine[0:128])
        tails.append(mine[128:WIN])
    return jnp.concatenate(parts + tails + [jnp.zeros((32, C), BF16)], axis=0)


def setup_kernel(
    w_ref, bias_ref, pat_ref, attn_gain_ref, mlp_gain_ref, temp_head_ref, reduce_ref,
    wt_ref, bias_out_ref, pat_q_ref, pat_k_ref, gains_ref, u_ref,
):
    wt_ref[...] = w_ref[...].astype(F32).T.astype(BF16)
    lane = lanes((WIN, 128))
    tails = jnp.zeros((WIN, 128), F32)
    for h in range(HEADS):
        turned = bias_ref[h].T
        bias_out_ref[:, 128 * h : 128 * h + 128] = turned[:, 0:128] * LOG2E
        tail = jnp.concatenate([turned[:, 128:WIN], jnp.zeros((WIN, 112), F32)], axis=1)
        tail = roll(tail, 16 * h)
        tails = jnp.where((lane >= 16 * h) & (lane < 16 * h + 16), tail, tails)
    bias_out_ref[:, 768:WIDE] = tails * LOG2E
    pat = pat_ref[...].astype(F32)
    for h in range(HEADS):
        pat_q_ref[:, 128 * h : 128 * h + 128] = pat[:, 0:128]
    tail = jnp.concatenate([pat[:, 128:WIN], jnp.zeros((8, 112), F32)], axis=1)
    tails = tail
    for h in range(1, 8):
        tails = tails + roll(tail, 16 * h)
    pat_q_ref[:, 768:WIDE] = tails
    pat_k_ref[...] = jnp.concatenate([pat, jnp.zeros((120, WIN), F32)], axis=0).T
    gains_ref[...] = jnp.zeros((8, 256), F32)
    gains_ref[0:1, 0:C] = attn_gain_ref[...]
    gains_ref[1:2, 0:C] = mlp_gain_ref[...]
    head_row = temp_head_ref[...].astype(F32)
    gains_ref[2:3, 0:C] = head_row
    u_ref[...] = dot(jnp.broadcast_to(head_row, (8, C)).astype(BF16), reduce_ref[...])


def setup(w_qkv, window_bias, patterns, attn_gain, mlp_gain, temp_head, reduce_t):
    return pl.pallas_call(
        setup_kernel,
        out_shape=(
            jax.ShapeDtypeStruct((3 * C, C), BF16),
            jax.ShapeDtypeStruct((WIN, WIDE), F32),
            jax.ShapeDtypeStruct((8, WIDE), F32),
            jax.ShapeDtypeStruct((WIN, 128), F32),
            jax.ShapeDtypeStruct((8, 256), F32),
            jax.ShapeDtypeStruct((8, FF), F32),
        ),
        in_specs=[vmem()] * 7,
        out_specs=(vmem(),) * 6,
        compiler_params=pltpu.CompilerParams(vmem_limit_bytes=SMALL_VMEM),
        cost_estimate=pl.CostEstimate(
            flops=1_000_000_000, bytes_accessed=3_000_000, transcendentals=0
        ),
        name="setup",
    )(w_qkv, window_bias, patterns, attn_gain[None], mlp_gain[None], temp_head[None], reduce_t)


LOG2E = 1.4426950408889634


def interleave(*runs):
    live = list(runs)
    while live:
        for run in list(live):
            try:
                next(run)
            except StopIteration:
                live.remove(run)


PER_COLUMN = (
    ((4, WIN, 256), F32),
    ((208, WIDE), BF16),
    ((208, WIDE), BF16),
    ((4, WIN, WIDE), BF16),
    ((4, WIN, WIDE), BF16),
    ((4, WIN, C), BF16),
    ((4, WIN, C), BF16),
    ((4, C, 256), F32),
    ((4, WIN, C), F32),
    ((4, WIN, C), F32),
    ((4, WIN, 128), F32),
    ((4, WIN, 128), F32),
    ((4, WIN, 128), F32),
    ((4, WIN, 256), F32),
    ((4, WIN, 128), F32),
    ((4, WIN, 256), BF16),
)


def main_kernel(
    x_ref, order_ref, back_ref, wt_ref, bias_ref, pat_q_ref, pat_k_ref, gains_ref, u_ref,
    proj_ref, expand_ref,
    out_ref, tok_in, levels_ref, packed, sems, *scratch,
):
    columns = (scratch[: len(PER_COLUMN)], scratch[len(PER_COLUMN) :])
    scale_q = 1.0 / HEAD**0.5
    lane72 = lanes((HALF, 128))
    lane16 = lanes((16, 128))
    row16 = lax.broadcasted_iota(jnp.int32, (16, 128), 0)
    for s in range(GROUP):
        first, second, extra = unpack_block(x_ref[s])
        tok_in[s, :, 0:128] = first
        tok_in[s, 0:HALF, 128:256] = second[0]
        tok_in[s, HALF:WIN, 128:256] = second[1]
        if s < 4:
            whole = (extra + roll(extra, -3)) + roll(extra, -6)
            levels_ref[s] = jnp.where(lane16 < 75, whole, extra)
    for col in range(2):
        for ref in columns[col][1:3]:
            ref[...] = jnp.zeros(ref.shape, BF16)

    def place(p, part):
        a, beta = part // 2, part % 2
        return beta * 4 + (p + a) % 4, (HALF if a == 0 else 0)

    pick_row = lax.broadcasted_iota(jnp.int32, (128, 256), 0)
    pick_lane = lanes((128, 256))
    pick = jnp.where(
        pick_lane < 128,
        jnp.where((pick_row >= 64) & (pick_row < 67), 1.0, 0.0),
        jnp.where((pick_row >= 67) & (pick_row < 70), 1.0, 0.0),
    ).astype(BF16)
    for p in range(4):
        for a in range(2):
            pieces = []
            for beta in range(2):
                s, at = place(p, 2 * a + beta)
                pieces.append(tok_in[s, at : at + HALF, :])
            moved = dot(order_ref[...], jnp.concatenate(pieces, axis=0).astype(BF16))
            fields = dot(moved[:, 128:256].astype(BF16), pick)
            for col in range(2):
                rows = slice(HALF * a, HALF * a + HALF)
                columns[col][0][p, rows, :] = moved[HALF * col : HALF * col + HALF]
                columns[col][13][p, rows, :] = fields[HALF * col : HALF * col + HALF]

    gain_one = gains_ref[0:1, 0:C]
    gain_two = gains_ref[1:2, 0:C]
    head_row = gains_ref[2:3, 0:C]
    u_row = u_ref[0:1, :]

    def forward(p, col):
        (tok, diag_q, diag_n, probs, dscores, q_rows, n_rows, dq_rows, resid, hats, scales,
         deltas, _, _, _, _) = columns[col]
        x = tok[p, :, 0:C]
        hat, scale = norm_parts(x)
        normed = (hat * gain_one).astype(BF16)
        hats[p] = hat
        scales[p] = jnp.broadcast_to(scale, (WIN, 128))
        spot = (row16 == 2 + p) & (lane16 == 81 + col)
        ident = jnp.sum(jnp.where(spot, levels_ref[0], 0.0), axis=0, keepdims=True)
        ident = jnp.sum(ident, axis=1, keepdims=True)
        row8 = lax.broadcasted_iota(jnp.int32, (8, 1), 0).astype(F32)
        label_q = jnp.sum(jnp.where(row8 == ident, pat_q_ref[...], 0.0), axis=0, keepdims=True)
        lane_row = lanes((1, 128)).astype(F32)
        label_k = jnp.sum(
            jnp.where(lane_row == ident, pat_k_ref[...], 0.0), axis=1, keepdims=True
        )
        yield
        turned = dot_nt(wt_ref[...], normed)
        q_turned = turned[0:C] * (scale_q * LOG2E)
        fill_diagonal(diag_q, q_turned, diagonal_tails(q_turned))
        apart = jnp.where(row8 == label_q, 0.0, -1e30)
        diag_q[C : C + 16, :] = jnp.concatenate(
            [apart, jnp.zeros((8, WIDE), F32)], axis=0
        ).astype(BF16)
        keys_t = turned[C : 2 * C].astype(BF16)
        values_t = turned[2 * C : 3 * C].astype(BF16)
        yield
        q_rows[p] = (dot_nt(normed, wt_ref[0:C, :]) * scale_q).astype(BF16)
        keys = dot_nt(normed, wt_ref[C : 2 * C, :])
        lane16w = lanes((WIN, 16))
        marks = jnp.where(lane16w.astype(F32) == label_k, 1.0, 0.0)
        keys = jnp.concatenate([keys, marks], axis=1).astype(BF16)
        values = dot_nt(normed, wt_ref[2 * C : 3 * C, :])
        ones = jnp.where(lane16w < 2, 1.0, 0.0)
        values = jnp.concatenate([values, ones], axis=1).astype(BF16)
        yield
        scores = dot(keys, diag_q[...]) + bias_ref[...]
        yield
        raised = jnp.exp2(scores - jnp.max(scores, axis=0, keepdims=True))
        weights = (raised * (1.0 / jnp.sum(raised, axis=0, keepdims=True))).astype(BF16)
        probs[p] = weights
        yield
        main, tails = per_head(values_t, weights)
        context = token_rows(main, tails)
        yield
        middle = (x + dot(context, proj_ref[...])).astype(BF16).astype(F32)
        hat_two, scale_two = norm_parts(middle)
        normed_two = (hat_two * gain_two).astype(BF16)
        yield
        acc = jnp.zeros((WIN, 256), F32)
        back = jnp.zeros((WIN, C), F32)
        c0 = 0.7978845608028654
        c1 = c0 * 0.044715
        c2, c3 = -2.0 * LOG2E * c0, -2.0 * LOG2E * c1
        for f in range(3):
            at = slice(256 * f, 256 * f + 256)
            pre = dot(normed_two, expand_ref[:, at])
            u = u_row[:, at]
            gate = 1.0 / (1.0 + jnp.exp2(pre * (c2 + c3 * (pre * pre))))
            unit = pre * gate
            acc = acc + unit * u
            pre, gate, unit = pre.astype(BF16), gate.astype(BF16), unit.astype(BF16)
            slope = gate * (1.0 + (pre - unit) * (2.0 * c0 + (6.0 * c1) * (pre * pre)))
            back = back + dot_nt(slope * u.astype(BF16), expand_ref[:, at])
            yield
        delta = jnp.sum(acc, axis=1, keepdims=True) + jnp.sum(
            middle * head_row, axis=1, keepdims=True
        )
        deltas[p] = jnp.broadcast_to(delta, (WIN, 128))
        kept = head_row + norm_back(back * gain_two, hat_two, scale_two)
        resid[p] = kept
        kept = kept.astype(BF16)
        yield
        n_turned = dot_nt(proj_ref[...], kept)
        n_tails = diagonal_tails(n_turned)
        fill_diagonal(diag_n, n_turned, n_tails)
        product = n_turned[:, 0:128] * main
        inner = [
            jnp.sum(product[HEAD * h : HEAD * h + HEAD], axis=0, keepdims=True)
            for h in range(HEADS)
        ]
        inner.append(jnp.sum(n_tails * tails, axis=0, keepdims=True))
        inner = jnp.concatenate(inner, axis=1)
        top = inner.astype(BF16).astype(F32)
        diag_n[C : C + 16, :] = jnp.concatenate(
            [-top, top - inner, jnp.zeros((14, WIDE), F32)], axis=0
        ).astype(BF16)
        n_rows[p] = dot_nt(kept, proj_ref[...]).astype(BF16)
        yield
        dweights = dot(values, diag_n[...])
        dscore = probs[p] * dweights.astype(BF16)
        dscores[p] = dscore
        yield
        main, tails = per_head(keys_t, dscore)
        dq_rows[p, :, 0:128] = main
        dq_rows[p, :, 128:256] = tails

    def forward_step(p, carry):
        interleave(forward(p, 0), forward(p, 1))
        return carry

    lax.fori_loop(0, 4, forward_step, 0)

    def scalar(l, k):
        return levels_ref[l // 2, l % 2 : l % 2 + 1, 72 + k : 73 + k]

    for col in range(2):
        deltas, source, fields, heights = (columns[col][k] for k in (11, 12, 13, 14))
        total = jnp.zeros((HALF, 128), F32)
        misfits, spots = [], []
        for l in range(8):
            a = 1 - l % 2
            p = (l // 2 - a) % 4
            rows = slice(HALF * a, HALF * a + HALF)
            spots.append((p, rows))
            temps = scalar(l, 2) + deltas[p, rows, :]
            total = total + scalar(l, 0) * temps
            height = fields[p, rows, 128:256] + total
            misfits.append(scalar(l, 1) * (height - fields[p, rows, 0:128]))
            top, middle, low = split3(height)
            heights[p, rows, :] = jnp.where(
                lane72 == 64, top, jnp.where(lane72 == 65, middle, low)
            )
        carried = jnp.zeros((HALF, 128), F32)
        for l in reversed(range(8)):
            p, rows = spots[l]
            carried = carried + misfits[l]
            source[p, rows, :] = scalar(l, 0) * carried

    def backward(p, col):
        (_, _, _, probs, dscores, q_rows, n_rows, dq_rows, resid, hats, scales,
         _, source, _, heights, made) = columns[col]
        s = wide(source[p])
        dk = dot(dscores[p], head_rows(s * q_rows[p].astype(F32))).astype(BF16)
        yield
        dv = dot(probs[p], head_rows(s * n_rows[p].astype(F32))).astype(BF16)
        yield
        dq = token_rows(dq_rows[p, :, 0:128], dq_rows[p, :, 128:256])
        dq = ((s * scale_q) * dq.astype(F32)).astype(BF16)
        dnormed = (
            dot(dq, wt_ref[0:C, :]) + dot(dk, wt_ref[C : 2 * C, :]) + dot(dv, wt_ref[2 * C :, :])
        )
        yield
        dx = norm_back(dnormed * gain_one, hats[p], wide(scales[p]))
        grad = s * resid[p] + dx
        lane = lanes((WIN, 128))
        last = jnp.concatenate([grad[:, 128:C], jnp.zeros((WIN, 64), F32)], axis=1)
        last = jnp.where(lane < 64, last, jnp.where(lane < 67, heights[p], 0.0))
        made[p, :, 0:128] = grad[:, 0:128].astype(BF16)
        made[p, :, 128:256] = last.astype(BF16)

    def backward_step(p, carry):
        interleave(backward(p, 0), backward(p, 1))
        return carry

    lax.fori_loop(0, 4, backward_step, 0)

    for p in range(4):
        for a in range(2):
            rows = slice(HALF * a, HALF * a + HALF)
            pair = [columns[col][15][p].astype(F32)[rows] for col in range(2)]
            moved = dot(back_ref[...], jnp.concatenate(pair, axis=0).astype(BF16))
            for beta in range(2):
                s, at = place(p, 2 * a + beta)
                tok_in[s, at : at + HALF, :] = moved[HALF * beta : HALF * beta + HALF]
    zero = jnp.zeros((16, 128), F32)
    for s in range(GROUP):
        pack_block(packed, s, tok_in[s], zero)
        pltpu.make_async_copy(packed.at[s], out_ref.at[s], sems.at[s]).start()
    for s in range(GROUP):
        pltpu.make_async_copy(packed.at[s], out_ref.at[s], sems.at[s]).wait()


def layer(x, consts):
    return pl.pallas_call(
        main_kernel,
        out_shape=jax.ShapeDtypeStruct((GROUP, ROWS, 128), BF16),
        in_specs=[vmem()] * (1 + len(consts)),
        out_specs=pl.BlockSpec(memory_space=pl.ANY),
        scratch_shapes=[
            pltpu.VMEM((GROUP, WIN, 256), F32),
            pltpu.VMEM((4, 16, 128), F32),
            pltpu.VMEM((GROUP, ROWS, 128), BF16),
            pltpu.SemaphoreType.DMA((GROUP,)),
        ]
        + [pltpu.VMEM(shape, kind) for shape, kind in PER_COLUMN] * 2,
        compiler_params=pltpu.CompilerParams(vmem_limit_bytes=VMEM_LIMIT),
        cost_estimate=pl.CostEstimate(
            flops=20_000_000_000, bytes_accessed=4_000_000, transcendentals=3_000_000
        ),
        name="layer",
    )(x, *consts)


def pair_groups(odd):
    out = []
    for block in range(BLOCKS):
        for band in range((odd + block) % 2, BANDS, 2):
            members = (band, (band + 1) % BANDS)
            out.append(
                [(b * BLOCKS + block) * LEVS + lev for b in members for lev in range(LEVS)]
            )
    return out


def exchange(blocks, odd):
    return lax.all_to_all(
        blocks, ("tile", "lev"), 0, 0, axis_index_groups=pair_groups(odd)
    )


def block_step(value, steps):
    pairs = [
        (t, t - t % BLOCKS + (t + steps) % BLOCKS) for t in range(BANDS * BLOCKS)
    ]
    return lax.ppermute(value, "tile", pairs)


def on_device(
    features, attn_gain, w_qkv, w_proj, window_bias, patterns, window_pattern, mlp_gain,
    w_expand, w_reduce, temp_head, temp_base, thickness, level_weight, surface, target,
):
    feats = features[:, 0].transpose(1, 2, 0, 3)
    goal = target.transpose(0, 2, 1, 3)
    ground = surface.transpose(1, 0, 2)
    after, before = rim(window_pattern, feats, goal, ground)
    after = block_step(after, -1)
    before = block_step(before, 1)

    band = lax.axis_index("tile") // BLOCKS
    block = lax.axis_index("tile") % BLOCKS
    even = ((band + block) % 2 == 0).astype(jnp.int32)
    halves = [even.reshape(1), (1 - even).reshape(1)]
    perm = jnp.asarray(source_rows(), BF16)
    perm_back = jnp.asarray(target_rows(), BF16)
    order = jnp.asarray(window_rows(), BF16)
    order_back = jnp.asarray(window_rows().T, BF16)

    made = [
        step(
            half, window_pattern, thickness, level_weight, temp_base,
            feats, after, before, goal, ground, perm,
        )
        for step, half in zip((prep_early, prep), halves)
    ]
    weights = (w_qkv, window_bias, patterns, attn_gain, mlp_gain, temp_head, w_reduce.T)
    weights, made[0] = lax.optimization_barrier((weights, made[0]))
    consts = (order, order_back) + tuple(setup(*weights)) + (w_proj, w_expand)
    done = None
    for odd in range(2):
        got = exchange(made[odd], odd)
        done = post(halves[odd], exchange(layer(got, consts), odd), perm_back, done)
    height, grad = done
    return height.transpose(0, 2, 1, 3), grad.transpose(2, 0, 1, 3)[:, None]


def solution(mesh):
    placed = (
        P("lev", "tile", None, None, None),
        P(), P(), P(), P(), P(),
        P(None, "tile"),
        P(), P(), P(), P(),
        P("lev"), P("lev"), P("lev"),
        P("tile", None, None),
        P("lev", "tile", None, None),
    )
    return jax.shard_map(
        on_device,
        mesh=mesh,
        in_specs=placed,
        out_specs=(P("lev", "tile", None, None), P("lev", "tile", None, None, None)),
        check_vma=False,
    )
```

```python
import jax
import jax.numpy as jnp
import numpy as np
from jax import lax
from jax.experimental import pallas as pl
from jax.experimental.pallas import tpu as pltpu
from jax.sharding import PartitionSpec as P

F32 = jnp.float32
BF16 = jnp.bfloat16
C = 192
HEADS = 6
HEAD = 32
FF = 768
WIN = 144
HALF = 72
QUARTER = 36
LONS = 90
SHIFT = 3
BLOCKS = 4
BANDS = 16
LEVS = 4
GROUP = 8
ROWS = 240
WIDE = 896
EPS = 1e-05
VMEM_LIMIT = 28 * 1024 * 1024
SMALL_VMEM = 12 * 1024 * 1024
VMEM_ALL = 60 * 1024 * 1024


def source_rows():
    table = np.zeros((2 * WIN, 6 * 64), np.float32)
    for q in range(2):
        for lev in range(2):
            for col in range(2):
                for i in range(QUARTER):
                    r, o = i // 6, i % 6
                    place = 2 * (12 * q + 6 * col + o + SHIFT) + lev
                    table[((q * 2 + lev) * 2 + col) * QUARTER + i, 64 * r + place] = 1.0
    return table


def target_rows():
    table = np.zeros((6 * 48, 3 * WIN), np.float32)
    for r in range(6):
        for x in range(48):
            e, lev = x // 2 + 9, x % 2
            d, col, o = e // 12, e % 12 // 6, e % 6
            table[48 * r + x, d * WIN + lev * HALF + col * QUARTER + 6 * r + o] = 1.0
    return table


def window_rows():
    table = np.zeros((WIN, WIN), np.float32)
    for col in range(2):
        for beta in range(2):
            for i in range(QUARTER):
                table[(col * 2 + beta) * QUARTER + i, (beta * 2 + col) * QUARTER + i] = 1.0
    return table


def dot(a, b):
    return jnp.dot(a, b, preferred_element_type=F32)


def dot_nt(a, b):
    return lax.dot_general(a, b, (((1,), (1,)), ((), ())), preferred_element_type=F32)


def lanes(shape):
    return lax.broadcasted_iota(jnp.int32, shape, len(shape) - 1)


def split3(value):
    top = value.astype(BF16).astype(F32)
    rest = value - top
    middle = rest.astype(BF16).astype(F32)
    return top, middle, rest - middle


def roll(value, steps):
    return pltpu.roll(value, steps % 128, 1)


def pack_block(out_ref, at, made, spare):
    lane = lanes((HALF, 128))
    out_ref[at, 0:WIN, :] = made[:, 0:128].astype(BF16)
    both = made[:, 128:256]
    tail = jnp.where(lane < 64, both[0:HALF], roll(both[HALF:WIN], 64))
    tail = jnp.concatenate([tail, jnp.zeros((8, 128), F32)], axis=0)
    lane16 = lanes((16, 128))
    extra = spare
    for g in range(9):
        moved = roll(both[16 * g : 16 * g + 16], 8 * g - 64)
        extra = jnp.where((lane16 >= 8 * g) & (lane16 < 8 * g + 8), moved, extra)
    out_ref[at, WIN : WIN + 16, :] = extra.astype(BF16)
    out_ref[at, WIN + 16 : ROWS, :] = tail.astype(BF16)


def unpack_block(block):
    first = block[0:WIN].astype(F32)
    extra = block[WIN : WIN + 16].astype(F32)
    tail = block[WIN + 16 : ROWS].astype(F32)[0:HALF]
    lane16 = lanes((16, 128))
    keep = (lane16 >= 64) & (lane16 < 72)
    spread = [jnp.where(keep, roll(extra, 64 - 8 * g), 0.0) for g in range(9)]
    spread = jnp.concatenate(spread, axis=0)
    lane = lanes((HALF, 128))
    second = [
        jnp.where(lane < 64, tail, spread[0:HALF]),
        jnp.where(lane < 64, roll(tail, 64), spread[HALF:WIN]),
    ]
    return first, second, extra


def vmem():
    return pl.BlockSpec(memory_space=pltpu.VMEM)


def smem():
    return pl.BlockSpec(memory_space=pltpu.SMEM)


def field_rows(targets, ground, count, padded):
    blank = jnp.zeros((count, 128 - LONS), F32)
    goal = [jnp.concatenate([t, blank], axis=1) for t in targets]
    ground = jnp.concatenate([ground, blank], axis=1)
    parts = split3(jnp.concatenate(goal, axis=1)) + split3(
        jnp.concatenate([ground, ground], axis=1)
    )
    if padded > count:
        more = jnp.zeros((padded - count, 256), F32)
        parts = [jnp.concatenate([v, more], axis=0) for v in parts]
    stacked = jnp.concatenate(parts, axis=0).astype(BF16)
    i = lax.broadcasted_iota(jnp.int32, (128, 6 * padded), 0)
    j = lanes((128, 6 * padded))
    hit = (j == padded * (i & 7) + (i >> 3)) & ((i & 7) < 6) & ((i >> 3) < count)
    return dot(jnp.where(hit, 1.0, 0.0).astype(BF16), stacked).astype(BF16)


def lon_pick(rows, first):
    x = lax.broadcasted_iota(jnp.int32, (rows, 256), 0)
    y = lanes((rows, 256))
    return jnp.where(y == 128 * (x & 1) + (x >> 1) + first, 1.0, 0.0).astype(BF16)


def rim_kernel(ids_ref, fa_ref, fb_ref, target_ref, surface_ref, next_ref, prev_ref):
    targets = [
        jnp.concatenate([target_ref[lev, r] for r in range(12)], axis=0) for lev in range(2)
    ]
    ground = jnp.concatenate([surface_ref[r] for r in range(12)], axis=0)
    fields = field_rows(targets, ground, 12, 16)
    spots = jnp.concatenate([lon_pick(8, 0), lon_pick(8, 86)], axis=0)
    values = dot_nt(spots, fields)
    lane = lanes((8, 128))
    idents = jnp.zeros((8, 128), F32)
    for p in range(4):
        idents = jnp.where(lane == 72 + p, ids_ref[p, 14].astype(F32), idents)
    for out_ref, f_ref, at, row, more in (
        (next_ref, fa_ref, 0, 0, 0.0), (prev_ref, fb_ref, 12, 8, idents)
    ):
        made = []
        for r in range(12):
            tokens = f_ref[r].reshape(20, C).astype(F32)[at : at + 8]
            second = jnp.concatenate([tokens[:, 128:C], jnp.zeros((8, 64), F32)], axis=1)
            extra = roll(values, 64 - 8 * r)[row : row + 8]
            second = jnp.where(lane < 64, second, jnp.where(lane < 72, extra, more))
            made.append(jnp.concatenate([tokens[:, 0:128], second], axis=1))
        out_ref[...] = jnp.concatenate(made, axis=0).astype(BF16)


def rim(ids, feats, target, surface):
    edge = jax.ShapeDtypeStruct((96, 256), BF16)
    return pl.pallas_call(
        rim_kernel,
        out_shape=(edge, edge),
        grid=(1,),
        in_specs=[
            smem(),
            pl.BlockSpec((12, 10, 2, C), lambda i: (0, 0, 0, 0)),
            pl.BlockSpec((12, 10, 2, C), lambda i: (0, 8, 0, 0)),
            pl.BlockSpec((2, 12, 1, LONS), lambda i: (0, 0, 0, 0)),
            pl.BlockSpec((12, 1, LONS), lambda i: (0, 0, 0)),
        ],
        out_specs=(
            pl.BlockSpec((96, 256), lambda i: (0, 0)),
            pl.BlockSpec((96, 256), lambda i: (0, 0)),
        ),
        compiler_params=pltpu.CompilerParams(vmem_limit_bytes=VMEM_ALL),
        name="rim",
    )(ids, feats, feats, target, surface)


def fill_rows(half_ref, f_ref, target_ref, surface_ref, rows_ref, after, before):
    start = 6 * half_ref[0]
    targets = [
        jnp.concatenate([target_ref[lev, start + r] for r in range(6)], axis=0)
        for lev in range(2)
    ]
    ground = jnp.concatenate([surface_ref[start + r] for r in range(6)], axis=0)
    values = dot_nt(lon_pick(2 * LONS, 0), field_rows(targets, ground, 6, 8))
    lane = lanes((2 * LONS, 128))
    for r in range(6):
        tokens = f_ref[start + r].reshape(2 * LONS, C).astype(F32)
        second = jnp.concatenate([tokens[:, 128:C], jnp.zeros((2 * LONS, 64), F32)], axis=1)
        extra = jnp.where(lane < 72, roll(values, 64 - 8 * r), 0.0)
        second = jnp.where(lane < 64, second, extra)
        for at, part in ((0, tokens[:, 0:128]), (128, second)):
            cut = slice(at, at + 128)
            rows_ref[208 * r : 208 * r + 176, cut] = part[0:176].astype(BF16)
            if after is None:
                rim_part = [jnp.zeros((12, 128), F32)]
            else:
                rim_part = [after[8 * r : 8 * r + 6, cut], before[8 * r + 2 : 8 * r + 8, cut]]
            tail = [part[176:180]] + rim_part + [part[0:6], jnp.zeros((10, 128), F32)]
            tail = jnp.concatenate(tail, axis=0).astype(BF16)
            rows_ref[208 * r + 176 : 208 * r + 208, cut] = tail


def rims(half_ref, next_ref, prev_ref):
    upper = half_ref[0] == 1
    return [
        jnp.where(upper, ref[48:96].astype(F32), ref[0:48].astype(F32))
        for ref in (next_ref, prev_ref)
    ]


def send_blocks(pairs, ids_ref, level_refs, source, before, perm_ref, packed, out_ref, sems):
    lane16 = lanes((16, 128))
    row16 = lax.broadcasted_iota(jnp.int32, (16, 128), 0)
    scalars = jnp.zeros((16, 128), F32)
    for lev in range(2):
        for k, ref in enumerate(level_refs):
            scalars = jnp.where((row16 == lev) & (lane16 == 72 + k), ref[lev], scalars)
    top, middle, low = split3(scalars)
    scalars = top + roll(middle, 3) + roll(low, 6)
    copies = []
    for m in pairs:
        made = dot(perm_ref[...], jnp.concatenate([source(r, m) for r in range(6)], axis=0))
        for q in range(2):
            d = 2 * m + q
            spare = scalars
            for p in range(4):
                for col in range(2):
                    if 2 * d + col < 15:
                        ident = ids_ref[p, 2 * d + col].astype(F32)
                    else:
                        ident = before[0:1, 200 + p : 201 + p]
                    spare = jnp.where((row16 == 2 + p) & (lane16 == 81 + col), ident, spare)
            at = d - 2 * pairs[0]
            pack_block(packed, at, made[WIN * q : WIN * q + WIN], spare)
            copies.append(pltpu.make_async_copy(packed.at[at], out_ref.at[d], sems.at[at]))
            copies[-1].start()
    for copy in copies:
        copy.wait()


def prep_kernel(
    half_ref, ids_ref, thick_ref, weight_ref, base_ref,
    f_ref, next_ref, prev_ref, target_ref, surface_ref, perm_ref,
    out_ref, rows_ref, packed, sems,
):
    after, before = rims(half_ref, next_ref, prev_ref)
    fill_rows(half_ref, f_ref, target_ref, surface_ref, rows_ref, after, before)
    send_blocks(
        range(4), ids_ref, (thick_ref, weight_ref, base_ref),
        lambda r, m: rows_ref[208 * r + 48 * m : 208 * r + 48 * m + 64, :],
        before, perm_ref, packed, out_ref, sems,
    )


def inner_kernel(
    half_ref, ids_ref, thick_ref, weight_ref, base_ref,
    f_ref, target_ref, surface_ref, perm_ref,
    out_ref, rows_ref, packed, sems,
):
    fill_rows(half_ref, f_ref, target_ref, surface_ref, rows_ref, None, None)
    send_blocks(
        range(3), ids_ref, (thick_ref, weight_ref, base_ref),
        lambda r, m: rows_ref[208 * r + 48 * m : 208 * r + 48 * m + 64, :],
        None, perm_ref, packed, out_ref, sems,
    )


def outer_kernel(
    half_ref, ids_ref, thick_ref, weight_ref, base_ref,
    next_ref, prev_ref, rows_ref, perm_ref, _,
    out_ref, packed, sems,
):
    after, before = rims(half_ref, next_ref, prev_ref)

    def source(r, m):
        own = rows_ref[208 * r + 176 : 208 * r + 208, :].astype(F32)
        more = [
            jnp.zeros((4, 256), F32), after[8 * r : 8 * r + 6], before[8 * r + 2 : 8 * r + 8],
            jnp.zeros((16, 256), F32),
        ]
        tail = (own + jnp.concatenate(more, axis=0)).astype(BF16)
        return jnp.concatenate([rows_ref[208 * r + 144 : 208 * r + 176, :], tail], axis=0)

    send_blocks(
        range(3, 4), ids_ref, (thick_ref, weight_ref, base_ref),
        source, before, perm_ref, packed, out_ref, sems,
    )


def prep_call(kernel, name, count, outs, out_specs, scratch, aliases, args):
    return pl.pallas_call(
        kernel,
        out_shape=outs,
        in_specs=[smem()] * 5
        + [vmem()] * (len(args) - 5 - len(aliases))
        + [pl.BlockSpec(memory_space=pl.ANY)] * len(aliases),
        out_specs=out_specs,
        scratch_shapes=scratch
        + [pltpu.VMEM((count, ROWS, 128), BF16), pltpu.SemaphoreType.DMA((count,))],
        input_output_aliases=aliases,
        compiler_params=pltpu.CompilerParams(vmem_limit_bytes=SMALL_VMEM),
        cost_estimate=pl.CostEstimate(
            flops=1_000_000_000, bytes_accessed=2_500_000, transcendentals=0
        ),
        name=name,
    )(*args)


BLOCKS_OUT = jax.ShapeDtypeStruct((GROUP, ROWS, 128), BF16)


def prep(half, ids, thick, weight, base, feats, after, before, target, surface, perm):
    return prep_call(
        prep_kernel, "prep", GROUP, BLOCKS_OUT, pl.BlockSpec(memory_space=pl.ANY),
        [pltpu.VMEM((6 * 208, 256), BF16)], {},
        (half, ids, thick, weight, base, feats, after, before, target, surface, perm),
    )


def prep_early(half, ids, thick, weight, base, feats, after, before, target, surface, perm):
    blocks, rows = prep_call(
        inner_kernel, "inner", 6,
        (BLOCKS_OUT, jax.ShapeDtypeStruct((6 * 208, 256), BF16)),
        (pl.BlockSpec(memory_space=pl.ANY), vmem()), [], {},
        (half, ids, thick, weight, base, feats, target, surface, perm),
    )
    return prep_call(
        outer_kernel, "outer", 2, BLOCKS_OUT, pl.BlockSpec(memory_space=pl.ANY), [], {9: 0},
        (half, ids, thick, weight, base, after, before, rows, perm, blocks),
    )


def post_kernel(half_ref, x_ref, perm_ref, *refs):
    height_out, grad_out, rows_ref, height_ref, grad_ref, sems = refs[-6:]
    start = 6 * half_ref[0]
    copies = [
        pltpu.make_async_copy(grad_ref, grad_out.at[pl.ds(start, 6)], sems.at[0]),
        pltpu.make_async_copy(height_ref, height_out.at[:, pl.ds(start, 6)], sems.at[1]),
    ]
    for d in range(GROUP):
        first, second, _ = unpack_block(x_ref[d])
        rows_ref[d, :, 0:128] = first.astype(BF16)
        rows_ref[d, :, 128:256] = jnp.concatenate(second, axis=0).astype(BF16)
    lane = lanes((48, 128))
    columns = []
    for m in range(4):
        source = [rows_ref[(2 * m + k) % GROUP] for k in (-1, 0, 1)]
        made = dot(perm_ref[...], jnp.concatenate(source, axis=0))
        count = 24 if m < 3 else 18
        column = jnp.zeros((48, 128), F32)
        for r in range(6):
            tokens = made[48 * r : 48 * r + 2 * count, 0:C].astype(BF16)
            grad_ref[r, 24 * m : 24 * m + count] = tokens.reshape(count, 2, C)
            moved = roll(made[48 * r : 48 * r + 48, 128:256], 8 * r - 64)
            column = jnp.where((lane >= 8 * r) & (lane < 8 * r + 3), moved, column)
        columns.append(column)
    copies[0].start()
    columns = jnp.concatenate(columns, axis=0).astype(BF16)
    rows = lax.dot_general(
        columns, lon_pick(192, 0), (((0,), (0,)), ((), ())), preferred_element_type=F32
    )
    for r in range(6):
        row = rows[8 * r : 8 * r + 1] + rows[8 * r + 1 : 8 * r + 2] + rows[8 * r + 2 : 8 * r + 3]
        for lev in range(2):
            height_ref[lev, r] = row[:, 128 * lev : 128 * lev + LONS]
    copies[1].start()
    for copy in copies:
        copy.wait()


def post(half, blocks, perm, earlier):
    kept = [] if earlier is None else list(earlier)
    return pl.pallas_call(
        post_kernel,
        out_shape=(
            jax.ShapeDtypeStruct((2, 12, 1, LONS), F32),
            jax.ShapeDtypeStruct((12, LONS, 2, C), BF16),
        ),
        in_specs=[smem(), vmem(), vmem()] + [pl.BlockSpec(memory_space=pl.ANY) for _ in kept],
        out_specs=(pl.BlockSpec(memory_space=pl.ANY), pl.BlockSpec(memory_space=pl.ANY)),
        scratch_shapes=[
            pltpu.VMEM((GROUP, WIN, 256), BF16),
            pltpu.VMEM((2, 6, 1, LONS), F32),
            pltpu.VMEM((6, LONS, 2, C), BF16),
            pltpu.SemaphoreType.DMA((2,)),
        ],
        input_output_aliases={3: 0, 4: 1} if kept else {},
        compiler_params=pltpu.CompilerParams(vmem_limit_bytes=SMALL_VMEM),
        cost_estimate=pl.CostEstimate(
            flops=1_000_000_000, bytes_accessed=2_500_000, transcendentals=0
        ),
        name="post",
    )(half, blocks, perm, *kept)


def norm_parts(x):
    center = jnp.sum(x, axis=-1, keepdims=True) * (1.0 / C)
    moved = x - center
    spread = jnp.sum(moved * moved, axis=-1, keepdims=True) * (1.0 / C)
    scale = lax.rsqrt(spread + EPS)
    return moved * scale, scale


def norm_back(cotangent, hat, scale):
    mean = jnp.sum(cotangent, axis=-1, keepdims=True) * (1.0 / C)
    along = jnp.sum(cotangent * hat, axis=-1, keepdims=True) * (1.0 / C)
    return scale * (cotangent - mean - hat * along)


def wide(value):
    return jnp.concatenate([value, value[:, 0:64]], axis=1)


def diagonal_tails(turned):
    lane = lanes((HEAD, 128))
    out = []
    for h in range(HEADS):
        rows = slice(HEAD * h, HEAD * h + HEAD)
        tail = jnp.concatenate([turned[rows, 128:WIN], jnp.zeros((HEAD, 112), F32)], axis=1)
        tail = roll(tail, 16 * h)
        out.append(jnp.where((lane >= 16 * h) & (lane < 16 * h + 16), tail, 0.0))
    return jnp.concatenate(out, axis=0)


def fill_diagonal(ref, turned, tails):
    for h in range(HEADS):
        rows = slice(HEAD * h, HEAD * h + HEAD)
        ref[rows, 128 * h : 128 * h + 128] = turned[rows, 0:128].astype(BF16)
    ref[0:C, 768:WIDE] = tails.astype(BF16)


def per_head(turned, weights):
    main = []
    for c in range(3):
        two = dot(turned[64 * c : 64 * c + 64], weights[:, 256 * c : 256 * c + 256])
        main += [two[0:HEAD, 0:128], two[HEAD:64, 128:256]]
    return jnp.concatenate(main, axis=0), dot(turned, weights[:, 768:WIDE])


def token_rows(main, tails):
    tails = tails.astype(BF16).T
    lane = lanes((16, C))
    last = jnp.zeros((16, C), BF16)
    for h in range(HEADS):
        mine = (lane >= HEAD * h) & (lane < HEAD * h + HEAD)
        last = jnp.where(mine, tails[16 * h : 16 * h + 16], last)
    return jnp.concatenate([main.astype(BF16).T, last], axis=0)


def head_rows(value):
    lane = lanes((WIN, C))
    parts, tails = [], []
    for h in range(HEADS):
        mine = jnp.where((lane >= HEAD * h) & (lane < HEAD * h + HEAD), value, 0.0).astype(BF16)
        parts.append(mine[0:128])
        tails.append(mine[128:WIN])
    return jnp.concatenate(parts + tails + [jnp.zeros((32, C), BF16)], axis=0)


def setup_kernel(
    w_ref, bias_ref, pat_ref, attn_gain_ref, mlp_gain_ref, temp_head_ref, reduce_ref,
    wt_ref, bias_out_ref, pat_q_ref, pat_k_ref, gains_ref, u_ref,
):
    wt_ref[...] = w_ref[...].astype(F32).T.astype(BF16)
    lane = lanes((WIN, 128))
    tails = jnp.zeros((WIN, 128), F32)
    for h in range(HEADS):
        turned = bias_ref[h].T
        bias_out_ref[:, 128 * h : 128 * h + 128] = turned[:, 0:128] * LOG2E
        tail = jnp.concatenate([turned[:, 128:WIN], jnp.zeros((WIN, 112), F32)], axis=1)
        tail = roll(tail, 16 * h)
        tails = jnp.where((lane >= 16 * h) & (lane < 16 * h + 16), tail, tails)
    bias_out_ref[:, 768:WIDE] = tails * LOG2E
    pat = pat_ref[...].astype(F32)
    for h in range(HEADS):
        pat_q_ref[:, 128 * h : 128 * h + 128] = pat[:, 0:128]
    tail = jnp.concatenate([pat[:, 128:WIN], jnp.zeros((8, 112), F32)], axis=1)
    tails = tail
    for h in range(1, 8):
        tails = tails + roll(tail, 16 * h)
    pat_q_ref[:, 768:WIDE] = tails
    pat_k_ref[...] = jnp.concatenate([pat, jnp.zeros((120, WIN), F32)], axis=0).T
    gains_ref[...] = jnp.zeros((8, 256), F32)
    gains_ref[0:1, 0:C] = attn_gain_ref[...]
    gains_ref[1:2, 0:C] = mlp_gain_ref[...]
    head_row = temp_head_ref[...].astype(F32)
    gains_ref[2:3, 0:C] = head_row
    u_ref[...] = dot(jnp.broadcast_to(head_row, (8, C)).astype(BF16), reduce_ref[...])


def setup(w_qkv, window_bias, patterns, attn_gain, mlp_gain, temp_head, reduce_t):
    return pl.pallas_call(
        setup_kernel,
        out_shape=(
            jax.ShapeDtypeStruct((3 * C, C), BF16),
            jax.ShapeDtypeStruct((WIN, WIDE), F32),
            jax.ShapeDtypeStruct((8, WIDE), F32),
            jax.ShapeDtypeStruct((WIN, 128), F32),
            jax.ShapeDtypeStruct((8, 256), F32),
            jax.ShapeDtypeStruct((8, FF), F32),
        ),
        in_specs=[vmem()] * 7,
        out_specs=(vmem(),) * 6,
        compiler_params=pltpu.CompilerParams(vmem_limit_bytes=SMALL_VMEM),
        cost_estimate=pl.CostEstimate(
            flops=1_000_000_000, bytes_accessed=3_000_000, transcendentals=0
        ),
        name="setup",
    )(w_qkv, window_bias, patterns, attn_gain[None], mlp_gain[None], temp_head[None], reduce_t)


LOG2E = 1.4426950408889634


def interleave(*runs):
    live = list(runs)
    while live:
        for run in list(live):
            try:
                next(run)
            except StopIteration:
                live.remove(run)


PER_COLUMN = (
    ((4, WIN, 256), F32),
    ((208, WIDE), BF16),
    ((208, WIDE), BF16),
    ((4, WIN, WIDE), BF16),
    ((4, WIN, WIDE), BF16),
    ((4, WIN, C), BF16),
    ((4, WIN, C), BF16),
    ((4, C, 256), F32),
    ((4, WIN, C), F32),
    ((4, WIN, C), F32),
    ((4, WIN, 128), F32),
    ((4, WIN, 128), F32),
    ((4, WIN, 128), F32),
    ((4, WIN, 256), F32),
    ((4, WIN, 128), F32),
    ((4, WIN, 256), BF16),
)


def main_kernel(
    x_ref, order_ref, back_ref, wt_ref, bias_ref, pat_q_ref, pat_k_ref, gains_ref, u_ref,
    proj_ref, expand_ref,
    out_ref, tok_in, levels_ref, packed, sems, *scratch,
):
    columns = (scratch[: len(PER_COLUMN)], scratch[len(PER_COLUMN) :])
    scale_q = 1.0 / HEAD**0.5
    lane72 = lanes((HALF, 128))
    lane16 = lanes((16, 128))
    row16 = lax.broadcasted_iota(jnp.int32, (16, 128), 0)
    for s in range(GROUP):
        first, second, extra = unpack_block(x_ref[s])
        tok_in[s, :, 0:128] = first
        tok_in[s, 0:HALF, 128:256] = second[0]
        tok_in[s, HALF:WIN, 128:256] = second[1]
        if s < 4:
            whole = (extra + roll(extra, -3)) + roll(extra, -6)
            levels_ref[s] = jnp.where(lane16 < 75, whole, extra)
    for col in range(2):
        for ref in columns[col][1:3]:
            ref[...] = jnp.zeros(ref.shape, BF16)

    def place(p, part):
        a, beta = part // 2, part % 2
        return beta * 4 + (p + a) % 4, (HALF if a == 0 else 0)

    pick_row = lax.broadcasted_iota(jnp.int32, (128, 256), 0)
    pick_lane = lanes((128, 256))
    pick = jnp.where(
        pick_lane < 128,
        jnp.where((pick_row >= 64) & (pick_row < 67), 1.0, 0.0),
        jnp.where((pick_row >= 67) & (pick_row < 70), 1.0, 0.0),
    ).astype(BF16)
    for p in range(4):
        for a in range(2):
            pieces = []
            for beta in range(2):
                s, at = place(p, 2 * a + beta)
                pieces.append(tok_in[s, at : at + HALF, :])
            moved = dot(order_ref[...], jnp.concatenate(pieces, axis=0).astype(BF16))
            fields = dot(moved[:, 128:256].astype(BF16), pick)
            for col in range(2):
                rows = slice(HALF * a, HALF * a + HALF)
                columns[col][0][p, rows, :] = moved[HALF * col : HALF * col + HALF]
                columns[col][13][p, rows, :] = fields[HALF * col : HALF * col + HALF]

    gain_one = gains_ref[0:1, 0:C]
    gain_two = gains_ref[1:2, 0:C]
    head_row = gains_ref[2:3, 0:C]
    u_row = u_ref[0:1, :]

    def forward(p, col):
        (tok, diag_q, diag_n, probs, dscores, q_rows, n_rows, dq_rows, resid, hats, scales,
         deltas, _, _, _, _) = columns[col]
        x = tok[p, :, 0:C]
        hat, scale = norm_parts(x)
        normed = (hat * gain_one).astype(BF16)
        hats[p] = hat
        scales[p] = jnp.broadcast_to(scale, (WIN, 128))
        spot = (row16 == 2 + p) & (lane16 == 81 + col)
        ident = jnp.sum(jnp.where(spot, levels_ref[0], 0.0), axis=0, keepdims=True)
        ident = jnp.sum(ident, axis=1, keepdims=True)
        row8 = lax.broadcasted_iota(jnp.int32, (8, 1), 0).astype(F32)
        label_q = jnp.sum(jnp.where(row8 == ident, pat_q_ref[...], 0.0), axis=0, keepdims=True)
        lane_row = lanes((1, 128)).astype(F32)
        label_k = jnp.sum(
            jnp.where(lane_row == ident, pat_k_ref[...], 0.0), axis=1, keepdims=True
        )
        yield
        turned = dot_nt(wt_ref[...], normed)
        q_turned = turned[0:C] * (scale_q * LOG2E)
        fill_diagonal(diag_q, q_turned, diagonal_tails(q_turned))
        apart = jnp.where(row8 == label_q, 0.0, -1e30)
        diag_q[C : C + 16, :] = jnp.concatenate(
            [apart, jnp.zeros((8, WIDE), F32)], axis=0
        ).astype(BF16)
        keys_t = turned[C : 2 * C].astype(BF16)
        values_t = turned[2 * C : 3 * C].astype(BF16)
        yield
        q_rows[p] = (dot_nt(normed, wt_ref[0:C, :]) * scale_q).astype(BF16)
        keys = dot_nt(normed, wt_ref[C : 2 * C, :])
        lane16w = lanes((WIN, 16))
        marks = jnp.where(lane16w.astype(F32) == label_k, 1.0, 0.0)
        keys = jnp.concatenate([keys, marks], axis=1).astype(BF16)
        values = dot_nt(normed, wt_ref[2 * C : 3 * C, :])
        ones = jnp.where(lane16w < 2, 1.0, 0.0)
        values = jnp.concatenate([values, ones], axis=1).astype(BF16)
        yield
        scores = dot(keys, diag_q[...]) + bias_ref[...]
        yield
        raised = jnp.exp2(scores - jnp.max(scores, axis=0, keepdims=True))
        weights = (raised * (1.0 / jnp.sum(raised, axis=0, keepdims=True))).astype(BF16)
        probs[p] = weights
        yield
        main, tails = per_head(values_t, weights)
        context = token_rows(main, tails)
        yield
        middle = (x + dot(context, proj_ref[...])).astype(BF16).astype(F32)
        hat_two, scale_two = norm_parts(middle)
        normed_two = (hat_two * gain_two).astype(BF16)
        yield
        acc = jnp.zeros((WIN, 256), F32)
        back = jnp.zeros((WIN, C), F32)
        c0 = 0.7978845608028654
        c1 = c0 * 0.044715
        c2, c3 = -2.0 * LOG2E * c0, -2.0 * LOG2E * c1
        for f in range(3):
            at = slice(256 * f, 256 * f + 256)
            pre = dot(normed_two, expand_ref[:, at])
            u = u_row[:, at]
            gate = 1.0 / (1.0 + jnp.exp2(pre * (c2 + c3 * (pre * pre))))
            unit = pre * gate
            acc = acc + unit * u
            pre, gate, unit = pre.astype(BF16), gate.astype(BF16), unit.astype(BF16)
            slope = gate * (1.0 + (pre - unit) * (2.0 * c0 + (6.0 * c1) * (pre * pre)))
            back = back + dot_nt(slope * u.astype(BF16), expand_ref[:, at])
            yield
        delta = jnp.sum(acc, axis=1, keepdims=True) + jnp.sum(
            middle * head_row, axis=1, keepdims=True
        )
        deltas[p] = jnp.broadcast_to(delta, (WIN, 128))
        kept = head_row + norm_back(back * gain_two, hat_two, scale_two)
        resid[p] = kept
        kept = kept.astype(BF16)
        yield
        n_turned = dot_nt(proj_ref[...], kept)
        n_tails = diagonal_tails(n_turned)
        fill_diagonal(diag_n, n_turned, n_tails)
        product = n_turned[:, 0:128] * main
        inner = [
            jnp.sum(product[HEAD * h : HEAD * h + HEAD], axis=0, keepdims=True)
            for h in range(HEADS)
        ]
        inner.append(jnp.sum(n_tails * tails, axis=0, keepdims=True))
        inner = jnp.concatenate(inner, axis=1)
        top = inner.astype(BF16).astype(F32)
        diag_n[C : C + 16, :] = jnp.concatenate(
            [-top, top - inner, jnp.zeros((14, WIDE), F32)], axis=0
        ).astype(BF16)
        n_rows[p] = dot_nt(kept, proj_ref[...]).astype(BF16)
        yield
        dweights = dot(values, diag_n[...])
        dscore = probs[p] * dweights.astype(BF16)
        dscores[p] = dscore
        yield
        main, tails = per_head(keys_t, dscore)
        dq_rows[p, :, 0:128] = main
        dq_rows[p, :, 128:256] = tails

    def forward_step(p, carry):
        interleave(forward(p, 0), forward(p, 1))
        return carry

    for step in range(4):
        forward_step(step, 0)

    def scalar(l, k):
        return levels_ref[l // 2, l % 2 : l % 2 + 1, 72 + k : 73 + k]

    for col in range(2):
        deltas, source, fields, heights = (columns[col][k] for k in (11, 12, 13, 14))
        total = jnp.zeros((HALF, 128), F32)
        misfits, spots = [], []
        for l in range(8):
            a = 1 - l % 2
            p = (l // 2 - a) % 4
            rows = slice(HALF * a, HALF * a + HALF)
            spots.append((p, rows))
            temps = scalar(l, 2) + deltas[p, rows, :]
            total = total + scalar(l, 0) * temps
            height = fields[p, rows, 128:256] + total
            misfits.append(scalar(l, 1) * (height - fields[p, rows, 0:128]))
            top, middle, low = split3(height)
            heights[p, rows, :] = jnp.where(
                lane72 == 64, top, jnp.where(lane72 == 65, middle, low)
            )
        carried = jnp.zeros((HALF, 128), F32)
        for l in reversed(range(8)):
            p, rows = spots[l]
            carried = carried + misfits[l]
            source[p, rows, :] = scalar(l, 0) * carried

    def backward(p, col):
        (_, _, _, probs, dscores, q_rows, n_rows, dq_rows, resid, hats, scales,
         _, source, _, heights, made) = columns[col]
        s = wide(source[p])
        dk = dot(dscores[p], head_rows(s * q_rows[p].astype(F32))).astype(BF16)
        yield
        dv = dot(probs[p], head_rows(s * n_rows[p].astype(F32))).astype(BF16)
        yield
        dq = token_rows(dq_rows[p, :, 0:128], dq_rows[p, :, 128:256])
        dq = ((s * scale_q) * dq.astype(F32)).astype(BF16)
        dnormed = (
            dot(dq, wt_ref[0:C, :]) + dot(dk, wt_ref[C : 2 * C, :]) + dot(dv, wt_ref[2 * C :, :])
        )
        yield
        dx = norm_back(dnormed * gain_one, hats[p], wide(scales[p]))
        grad = s * resid[p] + dx
        lane = lanes((WIN, 128))
        last = jnp.concatenate([grad[:, 128:C], jnp.zeros((WIN, 64), F32)], axis=1)
        last = jnp.where(lane < 64, last, jnp.where(lane < 67, heights[p], 0.0))
        made[p, :, 0:128] = grad[:, 0:128].astype(BF16)
        made[p, :, 128:256] = last.astype(BF16)

    def backward_step(p, carry):
        interleave(backward(p, 0), backward(p, 1))
        return carry

    for step in range(4):
        backward_step(step, 0)

    for p in range(4):
        for a in range(2):
            rows = slice(HALF * a, HALF * a + HALF)
            pair = [columns[col][15][p].astype(F32)[rows] for col in range(2)]
            moved = dot(back_ref[...], jnp.concatenate(pair, axis=0).astype(BF16))
            for beta in range(2):
                s, at = place(p, 2 * a + beta)
                tok_in[s, at : at + HALF, :] = moved[HALF * beta : HALF * beta + HALF]
    zero = jnp.zeros((16, 128), F32)
    for s in range(GROUP):
        pack_block(packed, s, tok_in[s], zero)
        pltpu.make_async_copy(packed.at[s], out_ref.at[s], sems.at[s]).start()
    for s in range(GROUP):
        pltpu.make_async_copy(packed.at[s], out_ref.at[s], sems.at[s]).wait()


def layer(x, consts):
    return pl.pallas_call(
        main_kernel,
        out_shape=jax.ShapeDtypeStruct((GROUP, ROWS, 128), BF16),
        in_specs=[vmem()] * (1 + len(consts)),
        out_specs=pl.BlockSpec(memory_space=pl.ANY),
        scratch_shapes=[
            pltpu.VMEM((GROUP, WIN, 256), F32),
            pltpu.VMEM((4, 16, 128), F32),
            pltpu.VMEM((GROUP, ROWS, 128), BF16),
            pltpu.SemaphoreType.DMA((GROUP,)),
        ]
        + [pltpu.VMEM(shape, kind) for shape, kind in PER_COLUMN] * 2,
        compiler_params=pltpu.CompilerParams(vmem_limit_bytes=VMEM_LIMIT),
        cost_estimate=pl.CostEstimate(
            flops=20_000_000_000, bytes_accessed=4_000_000, transcendentals=3_000_000
        ),
        name="layer",
    )(x, *consts)


def pair_groups(odd):
    out = []
    for block in range(BLOCKS):
        for band in range((odd + block) % 2, BANDS, 2):
            members = (band, (band + 1) % BANDS)
            out.append(
                [(b * BLOCKS + block) * LEVS + lev for b in members for lev in range(LEVS)]
            )
    return out


def exchange(blocks, odd):
    return lax.all_to_all(
        blocks, ("tile", "lev"), 0, 0, axis_index_groups=pair_groups(odd)
    )


def block_step(value, steps):
    pairs = [
        (t, t - t % BLOCKS + (t + steps) % BLOCKS) for t in range(BANDS * BLOCKS)
    ]
    return lax.ppermute(value, "tile", pairs)


def on_device(
    features, attn_gain, w_qkv, w_proj, window_bias, patterns, window_pattern, mlp_gain,
    w_expand, w_reduce, temp_head, temp_base, thickness, level_weight, surface, target,
):
    feats = features[:, 0].transpose(1, 2, 0, 3)
    goal = target.transpose(0, 2, 1, 3)
    ground = surface.transpose(1, 0, 2)
    after, before = rim(window_pattern, feats, goal, ground)
    after = block_step(after, -1)
    before = block_step(before, 1)

    band = lax.axis_index("tile") // BLOCKS
    block = lax.axis_index("tile") % BLOCKS
    even = ((band + block) % 2 == 0).astype(jnp.int32)
    halves = [even.reshape(1), (1 - even).reshape(1)]
    perm = jnp.asarray(source_rows(), BF16)
    perm_back = jnp.asarray(target_rows(), BF16)
    order = jnp.asarray(window_rows(), BF16)
    order_back = jnp.asarray(window_rows().T, BF16)

    made = [
        step(
            half, window_pattern, thickness, level_weight, temp_base,
            feats, after, before, goal, ground, perm,
        )
        for step, half in zip((prep_early, prep), halves)
    ]
    weights = (w_qkv, window_bias, patterns, attn_gain, mlp_gain, temp_head, w_reduce.T)
    weights, made[0] = lax.optimization_barrier((weights, made[0]))
    consts = (order, order_back) + tuple(setup(*weights)) + (w_proj, w_expand)
    done = None
    for odd in range(2):
        got = exchange(made[odd], odd)
        done = post(halves[odd], exchange(layer(got, consts), odd), perm_back, done)
    height, grad = done
    return height.transpose(0, 2, 1, 3), grad.transpose(2, 0, 1, 3)[:, None]


def solution(mesh):
    placed = (
        P("lev", "tile", None, None, None),
        P(), P(), P(), P(), P(),
        P(None, "tile"),
        P(), P(), P(), P(),
        P("lev"), P("lev"), P("lev"),
        P("tile", None, None),
        P("lev", "tile", None, None),
    )
    return jax.shard_map(
        on_device,
        mesh=mesh,
        in_specs=placed,
        out_specs=(P("lev", "tile", None, None), P("lev", "tile", None, None, None)),
        check_vma=False,
    )
```
